128 devices in a mesh: curve: 16 (over x, z), sub: 8 (over y, core).
Axes of the slice: x: 4, y: 4, z: 4, core: 2. Of those that a mesh axis runs over, the one named last changes fastest.
Arguments:
- coefficients: float32 [5, 512, 16384], P(None, None, ('curve', 'sub')), may hold values from -6 to 6
- old_degree: int32 [16384], P(('curve', 'sub')), may hold values from 3 to 7
- new_degree: int32 [16384], P(('curve', 'sub')), may hold values from 3 to 7
- destination: int32 [16384], P(('curve', 'sub')), may hold values from 0 to 16383, as said below
- metric: float32 [3, 16384], P(None, ('curve', 'sub')), may hold values from 0.5 to 2
- neighbours: int32 [4, 16384], P(None, ('curve', 'sub')), may hold values from 0 to 128, as said below
- mortar_up: int32 [2, 18432], P(None, ('curve', 'sub')), may hold values from 0 to 127, as said below
- mortar_low: int32 [2, 18432], P(None, ('curve', 'sub')), may hold values from 0 to 127, as said below
Outputs:
- advanced: float32 [5, 512, 16384], P(None, None, ('curve', 'sub'))
The draws below stay inside these ranges and needn't reach their ends.
Inputs may be any that keep to these rules, and one draw needn't show every extreme that they name: A permutation of 0..16383; the new owner of element g is destination[g] // 128. Each device sends exactly 2 elements to each of 64 distinct devices and none to the others, and receives exactly 2 from each of 64 devices. `neighbours`: local index, on the element's own device, of the element across its +x, -x, +z, -z face, or 128 at the far field; mutual: b is across a's +x face exactly when a is across b's -x face, and likewise for z. `mortar_up`: row 0: local element whose +y face the mortar touches; row 1: 0 if the mortar covers that face whole, 1 or 2 if it covers its lower or upper half along x. Entries of device q are positions q * 144 onward. Every element of a device appears in its list; on each side of each interface 128 // 8 faces are split between two mortars with codes 1 and 2, whose two partners are whole faces. `mortar_low`: as mortar_up for the -y faces of the device's lower interface; mortar m here meets mortar m of the upper interface of the device below.
All inputs are finite; a program needn't handle non-finite values.
Results may differ from the reference program's by a relative error of at most 0.0001.
Values sent between devices are 32-bit elements; how exact they have to be, the bound alone decides.
No kernel may reach another device: no remote copies, remote signals or barrier semaphores. Data moves between devices by JAX's collectives and lax.ppermute only.
A program may use at most 128 MiB of HBM per device.

```python
import math
import jax
import jax.numpy as jnp
import numpy as np
from jax import lax

NV = 5
PMAX = 7
PMIN = 3
M = 512
E_DEV = 128
CAP = 2
MORT = 144
ELEMS = 16384
N_CURVE = 16
N_SUB = 8


row_length = 8


def draw_new_degree(key, part):
    key = jax.random.fold_in(key, 11)
    devices = N_CURVE * N_SUB
    heavy_rank = jax.random.randint(jax.random.fold_in(key, 1), (devices, 1), 0, 4) == 0
    spread = jax.random.randint(jax.random.fold_in(key, 2), (devices, E_DEV), PMIN, PMAX + 1)
    return jnp.where(heavy_rank, PMAX, spread).reshape(-1).astype(jnp.int32)


def shuffled(device_key):
    return jax.random.permutation(device_key, E_DEV).astype(jnp.int32)


def draw_destination(key, part):
    key = jax.random.fold_in(key, 5)
    devices = N_CURVE * N_SUB
    groups = E_DEV // CAP
    halfway = devices // 2
    others = jax.random.permutation(jax.random.fold_in(key, 1), devices - 1).astype(jnp.int32)
    others = jnp.where(others < halfway, others, others + 1)
    offsets = jnp.concatenate([jnp.full((1,), halfway, jnp.int32), others[:groups - 1]])
    send_order = jax.vmap(shuffled)(jax.random.split(jax.random.fold_in(key, 2), devices))
    recv_order = jax.vmap(shuffled)(jax.random.split(jax.random.fold_in(key, 3), devices))
    sender = jnp.arange(devices, dtype=jnp.int32)[:, None]
    target = (sender + offsets[send_order // CAP]) % devices
    arrival = recv_order[target, send_order]
    return (target * E_DEV + arrival).reshape(-1).astype(jnp.int32)


def lay_rows(device_key):
    order_list = jax.random.permutation(device_key, E_DEV).astype(jnp.int32)
    position = jnp.arange(E_DEV, dtype=jnp.int32)
    after = jnp.where((position + 1) % row_length == 0, E_DEV, order_list[jnp.minimum(position + 1, E_DEV - 1)])
    before = jnp.where(position % row_length == 0, E_DEV, order_list[jnp.maximum(position - 1, 0)])
    plus_side = jnp.zeros((E_DEV,), jnp.int32).at[order_list].set(after)
    minus_side = jnp.zeros((E_DEV,), jnp.int32).at[order_list].set(before)
    return jnp.stack([plus_side, minus_side])


def device_neighbours(device_key):
    first_key, second_key = jax.random.split(device_key)
    return jnp.concatenate([lay_rows(first_key), lay_rows(second_key)])


def draw_neighbours(key, part):
    key = jax.random.fold_in(key, 7)
    devices = N_CURVE * N_SUB
    tables = jax.vmap(device_neighbours)(jax.random.split(key, devices))
    return jnp.transpose(tables, (1, 0, 2)).reshape(4, devices * E_DEV).astype(jnp.int32)


def interface_lists(device_key):
    coarse = E_DEV // 8
    groups = E_DEV - coarse
    first_key, second_key, third_key = jax.random.split(device_key, 3)
    group_kind = jnp.concatenate([jnp.zeros((groups - 2 * coarse,), jnp.int32), jnp.ones((coarse,), jnp.int32), jnp.full((coarse,), 2, jnp.int32)])
    group_kind = jax.random.permutation(first_key, group_kind)
    widths = 1 + (group_kind > 0).astype(jnp.int32)
    starts = jnp.cumsum(widths) - widths
    left_count = jnp.where(group_kind == 2, 2, 1)
    left_start = jnp.cumsum(left_count) - left_count
    right_count = jnp.where(group_kind == 1, 2, 1)
    right_start = jnp.cumsum(right_count) - right_count
    mortar = jnp.arange(MORT, dtype=jnp.int32)
    owning = jnp.sum((starts[None, :] <= mortar[:, None]).astype(jnp.int32), axis=1) - 1
    within = mortar - starts[owning]
    kind_here = group_kind[owning]
    left_face = left_start[owning] + jnp.where(kind_here == 2, within, 0)
    left_half = jnp.where(kind_here == 1, within + 1, 0)
    right_face = right_start[owning] + jnp.where(kind_here == 1, within, 0)
    right_half = jnp.where(kind_here == 2, within + 1, 0)
    left_order = jax.random.permutation(second_key, E_DEV).astype(jnp.int32)
    right_order = jax.random.permutation(third_key, E_DEV).astype(jnp.int32)
    lower_side = jnp.stack([left_order[left_face], left_half]).astype(jnp.int32)
    upper_side = jnp.stack([right_order[right_face], right_half]).astype(jnp.int32)
    return (lower_side, upper_side)


def mortar_tables(key):
    devices = N_CURVE * N_SUB
    return jax.vmap(interface_lists)(jax.random.split(key, devices))


def draw_mortar_up(key, part):
    lower_side, upper_side = mortar_tables(key)
    return jnp.transpose(lower_side, (1, 0, 2)).reshape(2, -1)


def draw_mortar_low(key, part):
    lower_side, upper_side = mortar_tables(key)
    return jnp.transpose(jnp.roll(upper_side, 1, axis=0), (1, 0, 2)).reshape(2, -1)


def touch_ends(entries, stream_key, least, largest):
    index_at = [jax.random.randint(jax.random.fold_in(stream_key, axis), (), 0, length) for axis, length in enumerate(entries.shape)]
    main_axis = entries.shape.index(max(entries.shape))
    beside = index_at[:main_axis] + [(index_at[main_axis] + 1) % entries.shape[main_axis]] + index_at[main_axis + 1:]
    return entries.at[tuple(index_at)].set(least).at[tuple(beside)].set(largest)


def block_levels(own_key, extent, shards, least, top_value):
    factor_of = 1.0
    for dim, blocks in shards:
        steps = jax.random.uniform(jax.random.fold_in(jax.random.fold_in(own_key, 6), dim), (blocks,), jnp.float32, least / len(shards), top_value / len(shards))
        factor_of = factor_of * jnp.repeat(jnp.exp(steps), extent[dim] // blocks).reshape((-1,) + (1,) * (len(extent) - 1 - dim))
    return factor_of


def normal_values(key, shape, scale, most, pieces=(), held_as=jnp.bfloat16):
    factor_of = block_levels(key, shape, pieces, -0.22, 0.18) if pieces else 1.0
    values = jax.random.normal(key, shape, jnp.float32) * scale * factor_of
    return jnp.minimum(jnp.maximum(values, -most), most).astype(held_as)


def setup_inputs(seed: int = 0) -> dict:
    arg_keys = jax.random.split(jax.random.key(seed), 9)
    return {
        "coefficients": normal_values(arg_keys[0], (NV, M, ELEMS), 1.0, 6.0, ((2, 128),), jnp.float32),
        "old_degree": touch_ends(jax.random.randint(arg_keys[1], (ELEMS,), PMIN, PMAX + 1), jax.random.fold_in(arg_keys[1], 1), PMIN, PMAX).astype(jnp.int32),
        "new_degree": draw_new_degree(jax.random.fold_in(arg_keys[8], 71), 0),
        "destination": draw_destination(jax.random.fold_in(arg_keys[8], 71), 0),
        "metric": jnp.clip(jnp.exp(math.log(2.0) - 1.3862944 * jax.random.uniform(arg_keys[4], (3, ELEMS), jnp.float32) ** block_levels(arg_keys[4], (3, ELEMS), ((1, 128),), -0.2, 0.2)), 0.5, 2.0),
        "neighbours": draw_neighbours(jax.random.fold_in(arg_keys[8], 71), 0),
        "mortar_up": draw_mortar_up(jax.random.fold_in(arg_keys[8], 71), 0),
        "mortar_low": draw_mortar_low(jax.random.fold_in(arg_keys[8], 71), 0),
    }


precise = lax.Precision.HIGHEST
flow_x = 0.5
flow_y = 0.05
reach_x = 1.5
reach_y = 1.05
reach_z = 1.0
step_size = 0.006

def legendre_pair(degree_n, points):
    points = np.asarray(points) + 0.0
    value_before = points * 0.0
    value_now = points * 0.0 + 1.0
    for order in range(1, degree_n + 1):
        value_next = ((2 * order - 1) * points * value_now - (order - 1) * value_before) / order
        value_before = value_now
        value_now = value_next
    return (value_now, value_before)

def gauss_points(count):
    position = np.arange(1, count + 1) * 1.0
    abscissa = np.cos(np.pi * (position - 0.25) / (count + 0.5))
    for sweep in range(60):
        value_now, value_before = legendre_pair(count, abscissa)
        slope_now = count * (abscissa * value_now - value_before) / (abscissa * abscissa - 1.0)
        abscissa = abscissa - value_now / slope_now
    value_now, value_before = legendre_pair(count, abscissa)
    slope_now = count * (abscissa * value_now - value_before) / (abscissa * abscissa - 1.0)
    return (abscissa, 2.0 / ((1.0 - abscissa * abscissa) * slope_now * slope_now))

def orthonormal(degree_n, points):
    return math.sqrt((2 * degree_n + 1) / 2.0) * legendre_pair(degree_n, points)[0]

def basis_tables(mode_count):
    gauss_nodes, gauss_weights = gauss_points(2 * mode_count + 2)
    derivative = np.zeros((mode_count, mode_count))
    for b in range(mode_count):
        for a in range(b):
            if (b - a) % 2 == 1:
                derivative[a, b] = math.sqrt((2 * a + 1) * (2 * b + 1))
    upper_values = np.array([orthonormal(n, 1.0) for n in range(mode_count)])
    lower_values = np.array([orthonormal(n, -1.0) for n in range(mode_count)])
    halves = np.zeros((2, mode_count, mode_count))
    for half_index, offset in enumerate((-1.0, 1.0)):
        for a in range(mode_count):
            for b in range(mode_count):
                halves[half_index, a, b] = np.sum(gauss_weights * orthonormal(a, gauss_nodes) * orthonormal(b, (gauss_nodes + offset) / 2.0))
    mode_index = np.arange(mode_count)
    highest = np.maximum(np.maximum(mode_index[:, None, None], mode_index[None, :, None]), mode_index[None, None, :])
    return (jnp.asarray(derivative, jnp.float32), jnp.asarray(upper_values, jnp.float32), jnp.asarray(lower_values, jnp.float32), jnp.asarray(halves, jnp.float32), jnp.asarray(highest, jnp.int32))

def flux_x(states):
    return jnp.stack([flow_x * states[0] + states[1], flow_x * states[1] + states[4], flow_x * states[2], flow_x * states[3], states[1] + flow_x * states[4]])

def flux_y(states):
    return jnp.stack([flow_y * states[0] + states[2], flow_y * states[1], flow_y * states[2] + states[4], flow_y * states[3], states[2] + flow_y * states[4]])

def flux_z(states):
    nothing = jnp.zeros_like(states[0])
    return jnp.stack([states[3], nothing, nothing, states[4], states[3]])

def numerical(flux_fn, speed_bound, lower_state, upper_state):
    return 0.5 * (flux_fn(lower_state) + flux_fn(upper_state)) - 0.5 * speed_bound * (upper_state - lower_state)

def restrict(values, halves, half_code):
    lower_half = jnp.einsum('ab,vb...->va...', halves[0], values, precision=precise)
    upper_half = jnp.einsum('ab,vb...->va...', halves[1], values, precision=precise)
    return jnp.where(half_code == 1, lower_half, jnp.where(half_code == 2, upper_half, values))

def project(values, halves, half_code):
    lower_half = 0.5 * jnp.einsum('ab,va...->vb...', halves[0], values, precision=precise)
    upper_half = 0.5 * jnp.einsum('ab,va...->vb...', halves[1], values, precision=precise)
    return jnp.where(half_code == 1, lower_half, jnp.where(half_code == 2, upper_half, values))

def collect(values, elem_rows):
    devices = N_CURVE * N_SUB
    onehot = (elem_rows.reshape(devices, MORT)[:, :, None] == jnp.arange(E_DEV, dtype=jnp.int32)[None, None, :]).astype(jnp.float32)
    shaped = values.reshape(values.shape[0], values.shape[1], values.shape[2], devices, MORT)
    summed = jnp.einsum('vikdm,dme->vikde', shaped, onehot, precision=precise)
    return summed.reshape(values.shape[0], values.shape[1], values.shape[2], devices * E_DEV)

def tendency(solution, degree, metric, partners, present, mortar_up, mortar_low, tables):
    derivative, upper_values, lower_values, halves, highest = tables
    grad_x = jnp.einsum('ab,vbjke->vajke', derivative, solution, precision=precise)
    grad_y = jnp.einsum('ab,vibke->viake', derivative, solution, precision=precise)
    grad_z = jnp.einsum('ab,vijbe->vijae', derivative, solution, precision=precise)
    change = -(metric[0] * flux_x(grad_x) + metric[1] * flux_y(grad_y) + metric[2] * flux_z(grad_z))
    trace_xp = jnp.einsum('i,vijke->vjke', upper_values, solution, precision=precise)
    trace_xm = jnp.einsum('i,vijke->vjke', lower_values, solution, precision=precise)
    trace_yp = jnp.einsum('j,vijke->vike', upper_values, solution, precision=precise)
    trace_ym = jnp.einsum('j,vijke->vike', lower_values, solution, precision=precise)
    trace_zp = jnp.einsum('k,vijke->vije', upper_values, solution, precision=precise)
    trace_zm = jnp.einsum('k,vijke->vije', lower_values, solution, precision=precise)
    outer = jnp.take(trace_xm, partners[0], axis=-1) * present[0]
    face_xp = numerical(flux_x, reach_x, trace_xp, outer) - flux_x(trace_xp)
    outer = jnp.take(trace_xp, partners[1], axis=-1) * present[1]
    face_xm = numerical(flux_x, reach_x, outer, trace_xm) - flux_x(trace_xm)
    outer = jnp.take(trace_zm, partners[2], axis=-1) * present[2]
    face_zp = numerical(flux_z, reach_z, trace_zp, outer) - flux_z(trace_zp)
    outer = jnp.take(trace_zp, partners[3], axis=-1) * present[3]
    face_zm = numerical(flux_z, reach_z, outer, trace_zm) - flux_z(trace_zm)
    devices = N_CURVE * N_SUB
    block_base = (jnp.arange(devices, dtype=jnp.int32) * E_DEV)[:, None]
    up_index = (block_base + mortar_up[0].reshape(devices, MORT)).reshape(-1)
    low_index = (block_base + mortar_low[0].reshape(devices, MORT)).reshape(-1)
    left = restrict(jnp.take(trace_yp, up_index, axis=-1), halves, mortar_up[1])
    right = restrict(jnp.take(trace_ym, low_index, axis=-1), halves, mortar_low[1])
    axis_modes = PMAX + 1
    shaped = (NV, axis_modes, axis_modes, N_CURVE, N_SUB, MORT)
    empty = jnp.zeros((NV, axis_modes, axis_modes, N_CURVE, 1, MORT), jnp.float32)
    right_above = jnp.concatenate([right.reshape(shaped)[:, :, :, :, 1:], empty], axis=4).reshape(left.shape)
    left_below = jnp.concatenate([empty, left.reshape(shaped)[:, :, :, :, :-1]], axis=4).reshape(left.shape)
    face_up = numerical(flux_y, reach_y, left, right_above) - flux_y(left)
    face_low = numerical(flux_y, reach_y, left_below, right) - flux_y(right)
    sum_up = collect(project(face_up, halves, mortar_up[1]), mortar_up[0])
    sum_low = collect(project(face_low, halves, mortar_low[1]), mortar_low[0])
    change = change - metric[0] * upper_values[None, :, None, None, None] * face_xp[:, None]
    change = change + metric[0] * lower_values[None, :, None, None, None] * face_xm[:, None]
    change = change - metric[1] * upper_values[None, None, :, None, None] * sum_up[:, :, None]
    change = change + metric[1] * lower_values[None, None, :, None, None] * sum_low[:, :, None]
    change = change - metric[2] * upper_values[None, None, None, :, None] * face_zp[:, :, :, None]
    change = change + metric[2] * lower_values[None, None, None, :, None] * face_zm[:, :, :, None]
    live_modes = highest[..., None] <= degree[None, None, None, :]
    return jnp.where(live_modes[None], change, 0.0)

def reference(coefficients, old_degree, new_degree, destination, metric, neighbours, mortar_up, mortar_low):
    tables = basis_tables(PMAX + 1)
    highest = tables[4]
    axis_modes = PMAX + 1
    kept_degree = jnp.minimum(old_degree, new_degree)
    keep_mask = highest.reshape(-1)[:, None] <= kept_degree[None, :]
    trimmed = jnp.where(keep_mask[None], coefficients, 0.0)
    solution = jnp.zeros_like(trimmed).at[:, :, destination].set(trimmed)
    degree = jnp.zeros_like(new_degree).at[destination].set(new_degree)
    solution = solution.reshape(NV, axis_modes, axis_modes, axis_modes, ELEMS)
    owner_rank = jnp.arange(ELEMS, dtype=jnp.int32) // E_DEV
    partners = owner_rank[None, :] * E_DEV + jnp.minimum(neighbours, E_DEV - 1)
    present = (neighbours < E_DEV).astype(jnp.float32)

    def rate(values):
        return tendency(values, degree, metric, partners, present, mortar_up, mortar_low, tables)
    section_one = solution + step_size * rate(solution)
    section_two = 0.75 * solution + 0.25 * (section_one + step_size * rate(section_one))
    advanced = 1.0 / 3.0 * solution + 2.0 / 3.0 * (section_two + step_size * rate(section_two))
    return advanced.reshape(NV, M, ELEMS)
```

```python
import functools
import math

import jax
import jax.numpy as jnp
import numpy as np
from jax import lax
from jax.experimental import pallas as pl
from jax.experimental.pallas import tpu as pltpu
from jax.sharding import PartitionSpec as P

NV = 5
N = 8
MODES = N * N * N
ROWS = NV * MODES
FACE = NV * N * N
E = 128
BLOCK = 41
STEP = 0.006
ALPHA = (0.0, 0.75, 1.0 / 3.0)
BETA = (1.0, 0.25, 2.0 / 3.0)
PAY = FACE + 8
LIMIT = 24 * 1024 * 1024
F32 = jnp.float32
BF16 = jnp.bfloat16

VMEM = pl.BlockSpec(memory_space=pltpu.VMEM)
PARAMS = pltpu.CompilerParams(vmem_limit_bytes=LIMIT)


def legendre_pair(degree_n, points):
    points = np.asarray(points) + 0.0
    value_before = points * 0.0
    value_now = points * 0.0 + 1.0
    for order in range(1, degree_n + 1):
        value_next = ((2 * order - 1) * points * value_now - (order - 1) * value_before) / order
        value_before = value_now
        value_now = value_next
    return (value_now, value_before)


def half_table():
    nodes, weights = np.polynomial.legendre.leggauss(2 * N + 2)
    table = np.zeros((N, N))
    for a in range(N):
        for b in range(a, N):
            fa = math.sqrt((2 * a + 1) / 2.0) * legendre_pair(a, nodes)[0]
            fb = math.sqrt((2 * b + 1) / 2.0) * legendre_pair(b, (nodes - 1.0) / 2.0)[0]
            table[a, b] = np.sum(weights * fa * fb)
    return table


HALF = half_table()
RESTRICT = [[float(HALF[a, b] * math.sqrt((2 * a + 1) / (2 * b + 1))) for b in range(N)] for a in range(N)]
PROJECT = [[float(0.5 * HALF[a, b] * math.sqrt((2 * b + 1) / (2 * a + 1))) for a in range(N)] for b in range(N)]


def z_table():
    out = np.zeros((320, 256))
    for col in range(256):
        line, k = divmod(col, N)
        out[line, col] = 1.0
        out[32 + line, col] = (-1.0) ** k
        for a in range(k):
            if (k - a) % 2 == 1:
                out[64 + line * N + a, col] = 1.0
    return out


def iota(shape, axis):
    return lax.broadcasted_iota(jnp.int32, shape, axis)


def split(x):
    high = x.astype(BF16)
    return high, (x - high.astype(F32)).astype(BF16)


def dot(a, b):
    return lax.dot_general(a, b, (((1,), (0,)), ((), ())), preferred_element_type=F32)


def dot_nt(a, b):
    return lax.dot_general(a, b, (((1,), (1,)), ((), ())), preferred_element_type=F32)


def onehot(flag):
    return jnp.where(flag, 1.0, 0.0)


def pack_kernel(coef, old, new, dest, out):
    row = iota((E, E), 0)
    col = iota((E, E), 1)
    new_row = new[...]
    kept = jnp.minimum(old[...], new_row)
    target = lax.shift_right_logical(dest[...], 7)
    slot = dest[...] & (E - 1)
    target_f = jnp.broadcast_to(target.astype(F32), (E, E))
    same = target_f == target_f.T
    rank = jnp.sum(onehot(same & (row < col)), axis=0, keepdims=True)
    here = jnp.broadcast_to(target, (E, E)) == row
    pick0 = onehot(here & (rank < 0.5)).astype(BF16)
    pick1 = onehot(here & (rank > 0.5)).astype(BF16)
    slot_f = jnp.broadcast_to((slot - E).astype(F32), (E, E))
    new_f = jnp.broadcast_to(new_row.astype(F32), (E, E))
    tags0 = jnp.where(row == 0, slot_f, jnp.where(row == 1, new_f, 0.0)).astype(BF16)
    tags1 = jnp.where(row == 2, slot_f, jnp.where(row == 3, new_f, 0.0)).astype(BF16)
    tags = dot_nt(pick0, tags0) + dot_nt(pick1, tags1)
    tags = tags + jnp.where((col == 0) | (col == 2), float(E), 0.0)
    out[pl.ds(40, E, stride=BLOCK), :] = tags
    pick = jnp.concatenate([pick0, pick1], axis=0)
    pick = jnp.concatenate([pick, pick], axis=1)
    for q in range(4):
        mode = row + E * q
        i = lax.shift_right_logical(mode, 6)
        j = lax.shift_right_logical(mode, 3) & 7
        k = mode & 7
        live = jnp.maximum(jnp.maximum(i, j), k) <= kept
        weight = ((2 * i + 1) * (2 * j + 1) * (2 * k + 1)).astype(F32)
        weight = jnp.where(live, jnp.sqrt(weight), 0.0)
        for v in range(NV):
            g = 4 * v + q
            high, low = split(coef[v, E * q : E * (q + 1), :] * weight)
            moved = dot_nt(pick, jnp.concatenate([high, low], axis=1))
            out[pl.ds(g, E, stride=BLOCK), :] = moved[:E]
            out[pl.ds(20 + g, E, stride=BLOCK), :] = moved[E:]


def write_traces(even, odd, upper, lower, v, i):
    rows = slice((v * N + i) * N, (v * N + i) * N + N)
    upper[rows, :] = even + odd
    lower[rows, :] = even - odd


def unpack_kernel(got, mortar_up, mortar_low, solution, degree, upper, lower):
    row = iota((E, E), 0)
    tags = got[pl.ds(40, E, stride=BLOCK), :].T
    place0 = onehot(row.astype(F32) == tags[0:1, :]).astype(BF16)
    place1 = onehot(row.astype(F32) == tags[2:3, :]).astype(BF16)
    place = jnp.concatenate([place0, place1], axis=1)
    degrees = jnp.concatenate([tags[1:2, :], tags[3:4, :]], axis=1)
    degrees = jnp.broadcast_to(degrees, (16, 2 * E)).astype(BF16)
    degree[...] = dot_nt(degrees, place)[:8, :]
    for g in range(20):
        both = jnp.concatenate(
            [got[pl.ds(g, E, stride=BLOCK), :], got[pl.ds(20 + g, E, stride=BLOCK), :]], axis=0
        )
        high, low = split(both)
        moved = dot(place, jnp.concatenate([high, low], axis=1))
        solution[E * g : E * (g + 1), :] = (moved[:, :E] + moved[:, E:]).T
    for v in range(NV):
        for i in range(N):
            base = v * MODES + i * 64
            line = [solution[base + 8 * j : base + 8 * j + 8, :] for j in range(N)]
            even = (line[0] + line[2]) + (line[4] + line[6])
            odd = (line[1] + line[3]) + (line[5] + line[7])
            write_traces(even, odd, upper, lower, v, i)
    for table, face in ((mortar_up, upper), (mortar_low, lower)):
        face[FACE:PAY, :] = jnp.full((PAY - FACE, E), -1.0, F32)
        face[FACE : FACE + 2, :] = table[:, 0:E].astype(F32)
        face[FACE + 2 : FACE + 4, 0:16] = table[:, E : E + 16].astype(F32)


def couple(d, first, k):
    half = [(0.5 * k) * d[v] for v in range(NV)]
    vel, pres = 0.5 * d[first], 0.5 * d[4]
    half[0] = half[0] + vel
    half[first] = half[first] + pres
    half[4] = half[4] + vel
    return half


def halves_of(plus, minus):
    return [p - m for p, m in zip(plus, minus)], [p + m for p, m in zip(plus, minus)]


def volume_kernel(alpha, beta, *refs):
    if alpha:
        first, *refs = refs
    (state, upper, lower, metric, near, ztab, out, xsum, zsum, xp, xm, zp, zm, xl, zl, cat) = refs
    row = iota((E, E), 0)
    gather = []
    for d in range(4):
        pick = onehot(row == near[d : d + 1, :]).astype(BF16)
        gather.append(jnp.concatenate([pick, pick], axis=0))
    for v in range(NV):
        for h in range(2):
            base = v * MODES + 256 * h
            high, low = split(state[base : base + 256, :])
            both = jnp.concatenate([high, low], axis=1)
            count = 320 if v >= 3 else 64
            sums = dot(ztab[0:count, :], both)
            sums = sums[:, :E] + sums[:, E:]
            zp[v * 64 + 32 * h : v * 64 + 32 * h + 32, :] = sums[0:32]
            zm[v * 64 + 32 * h : v * 64 + 32 * h + 32, :] = sums[32:64]
            if v >= 3:
                zsum[(v - 3) * MODES + 256 * h : (v - 3) * MODES + 256 * h + 256, :] = sums[64:]
    for v in range(NV):
        for j in range(N):
            line = [state[v * MODES + 64 * i + 8 * j : v * MODES + 64 * i + 8 * j + 8, :] for i in range(N)]
            even = (line[0] + line[2]) + (line[4] + line[6])
            odd = (line[1] + line[3]) + (line[5] + line[7])
            write_traces(even, odd, xp, xm, v, j)

    def outer(face, pick):
        for v in range(NV):
            high, low = split(face[64 * v : 64 * v + 64, :])
            cat[64 * v : 64 * v + 64, 0:E] = high
            cat[64 * v : 64 * v + 64, E : 2 * E] = low
        return dot(cat[...], pick)

    def by_variable(x):
        return [x[64 * v : 64 * v + 64] for v in range(NV)]

    for plus, minus, where, first_v, k_minus, scale, result in (
        (xp, xm, (0, 1), 1, 2.0, 1.0, xl),
        (zp, zm, (2, 3), 3, 1.0, 0.5, zl),
    ):
        d_plus = by_variable(outer(minus, gather[where[0]]) - plus[...])
        d_minus = by_variable(outer(plus, gather[where[1]]) - minus[...])
        even, odd = halves_of(couple(d_plus, first_v, -1.0), couple(d_minus, first_v, k_minus))
        for v in range(NV):
            result[64 * v : 64 * v + 64, :] = scale * even[v] if scale != 1.0 else even[v]
            result[FACE + 64 * v : FACE + 64 * v + 64, :] = scale * odd[v] if scale != 1.0 else odd[v]

    full = [jnp.broadcast_to(metric[d : d + 1, :], (8, E)) for d in range(3)]
    kx = [full[0] * (-0.5 * beta * STEP * (2 * a + 1)) for a in range(N)]
    ky = [full[1] * (-0.05 * beta * STEP * (2 * a + 1)) for a in range(N)]
    kz = full[2] * (-beta * STEP) * (2 * iota((8, E), 0) + 1).astype(F32)
    odd_k = (iota((8, E), 0) & 1) == 1

    def at(ref, start):
        return ref[pl.ds(pl.multiple_of(start, 8), 8), :]

    def x_pass(j, carry):
        s = [
            [at(xl, 64 * v + 8 * j) for v in range(NV)],
            [at(xl, FACE + 64 * v + 8 * j) for v in range(NV)],
        ]
        for i in range(N - 1, -1, -1):
            rows = [v * MODES + 64 * i + 8 * j for v in range(NV)]
            now = s[i % 2]
            for v in range(NV):
                xsum[pl.ds(pl.multiple_of(rows[v], 8), 8), :] = kx[i] * now[v]
            if i:
                r, u, y, w, p = [at(state, rows[v]) for v in range(NV)]
                twice = u + u
                f = [r + twice, u + (p + p), y, w, p + twice]
                s[(i + 1) % 2] = [a + b for a, b in zip(s[(i + 1) % 2], f)]
        return carry

    lax.fori_loop(0, N, x_pass, 0)

    def y_pass(i, carry):
        d_plus = [-at(upper, 64 * v + 8 * i) for v in range(NV)]
        d_minus = [-at(lower, 64 * v + 8 * i) for v in range(NV)]
        even, odd = halves_of(couple(d_plus, 2, -1.0), couple(d_minus, 2, 1.1))
        s = [[10.0 * x for x in even], [10.0 * x for x in odd]]
        z_even = [at(zl, 64 * v + 8 * i) for v in range(NV)]
        z_odd = [at(zl, FACE + 64 * v + 8 * i) for v in range(NV)]
        for j in range(N - 1, -1, -1):
            inner = 64 * i + 8 * j
            rows = [v * MODES + inner for v in range(NV)]
            c = [at(state, rows[v]) for v in range(NV)]
            sw, sp = at(zsum, inner), at(zsum, MODES + inner)
            zs = (sw, None, None, sp, sw)
            now = s[j % 2]
            for v in range(NV):
                lift = jnp.where(
                    odd_k,
                    jnp.broadcast_to(z_odd[v][j : j + 1, :], (8, E)),
                    jnp.broadcast_to(z_even[v][j : j + 1, :], (8, E)),
                )
                if zs[v] is not None:
                    lift = lift + zs[v]
                total = at(xsum, rows[v]) + ky[j] * now[v] + kz * lift
                if alpha:
                    total = total + (alpha * at(first, rows[v]) + beta * c[v])
                else:
                    total = total + c[v]
                out[pl.ds(pl.multiple_of(rows[v], 8), 8), :] = total
            if j:
                r, u, y, w, p = c
                y20 = 20.0 * y
                f = [r + y20, u, y + 20.0 * p, w, p + y20]
                s[(j + 1) % 2] = [a + b for a, b in zip(s[(j + 1) % 2], f)]
        return carry

    lax.fori_loop(0, N, y_pass, 0)


def build_routes(pay, table):
    wide = iota((E, 2 * E), 0).astype(F32)
    pad = jnp.full((1, E - 16), -1.0, F32)

    def own(r):
        return jnp.concatenate([table[r : r + 1, 0:E].astype(F32), table[r : r + 1, E : E + 16].astype(F32), pad], axis=1)

    far_elem = jnp.concatenate([pay[FACE : FACE + 1, :], pay[FACE + 2 : FACE + 3, :]], axis=1)
    far_half = jnp.concatenate([pay[FACE + 1 : FACE + 2, :], pay[FACE + 3 : FACE + 4, :]], axis=1)
    own_elem, own_half = own(0), own(1)
    far_pick = onehot(wide == far_elem)
    own_pick = onehot(wide == own_elem).astype(BF16)
    far_whole, own_whole = onehot(far_half == 0.0), onehot(own_half == 0.0)
    far_1, far_2 = onehot(far_half == 1.0), onehot(far_half == 2.0)
    own_1, own_2 = onehot(own_half == 1.0), onehot(own_half == 2.0)
    weights = (
        far_whole * own_whole,
        own_whole * (far_1 + far_2),
        own_whole * (far_1 - far_2),
        far_whole * (own_1 + own_2),
        far_whole * (own_1 - own_2),
    )
    return [dot_nt((far_pick * w).astype(BF16), own_pick).astype(BF16) for w in weights]


def post_kernel(stage, *refs):
    beta = BETA[stage]
    if stage == 0:
        (partial, above, below, metric, degree, table_up, table_low, out, upper, lower, routes, cat_up, cat_low) = refs
        for side, (pay, table) in enumerate(((above, table_up), (below, table_low))):
            for n, route in enumerate(build_routes(pay, table)):
                for part in range(2):
                    start = side * 10 * E + part * 5 * E + n * E
                    routes[start : start + E, :] = route
    elif stage == 1:
        (partial, above, below, metric, degree, routes, out, upper, lower, cat_up, cat_low) = refs
    else:
        (partial, above, below, metric, degree, routes, out, cat_up, cat_low) = refs

    def mix(line, table, parity, transposed):
        result = []
        for a in range(N):
            total = None
            for b in range(N):
                if (a + b) % 2 != parity or (b > a if transposed else b < a):
                    continue
                term = table[a][b] * line[b]
                total = term if total is None else total + term
            result.append(jnp.zeros_like(line[0]) if total is None else total)
        return jnp.concatenate(result, axis=0)

    far = []
    for side, (face, cat) in enumerate(((above, cat_up), (below, cat_low))):
        for v in range(NV):
            whole = face[64 * v : 64 * v + 64, :]
            line = [whole[8 * i : 8 * i + 8] for i in range(N)]
            kinds = (
                whole,
                mix(line, RESTRICT, 0, False),
                mix(line, RESTRICT, 1, False),
                mix(line, PROJECT, 0, True),
                mix(line, PROJECT, 1, True),
            )
            for n, kind in enumerate(kinds):
                high, low = split(kind)
                cat[64 * v : 64 * v + 64, n * E : n * E + E] = high
                cat[64 * v : 64 * v + 64, (n + 5) * E : (n + 5) * E + E] = low
        far.append(dot(cat[...], routes[side * 10 * E : (side + 1) * 10 * E, :]))
    far_up, far_low = far
    k_row = iota((8, E), 0)
    deg = degree[...]
    masks = [onehot(jnp.maximum(k_row, n).astype(F32) <= deg) for n in range(N)]
    if stage == 2:
        back = 1.0 / jnp.sqrt((2 * k_row + 1).astype(F32))
        masks = [m * back for m in masks]
    full = jnp.broadcast_to(metric[1:2, :], (8, E))
    ky = [full * (-0.5 * beta * STEP * (2 * a + 1)) for a in range(N)]
    for i in range(N):
        up = [far_up[64 * v + 8 * i : 64 * v + 8 * i + 8] for v in range(NV)]
        low = [far_low[64 * v + 8 * i : 64 * v + 8 * i + 8] for v in range(NV)]
        lift = halves_of(couple(up, 2, -1.0), couple(low, 2, 1.1))
        for v in range(NV):
            sums = [None, None]
            for j in range(N):
                start = v * MODES + 64 * i + 8 * j
                value = masks[max(i, j)] * (partial[start : start + 8, :] + ky[j] * lift[j % 2][v])
                if stage == 2:
                    value = value * (1.0 / math.sqrt((2 * i + 1) * (2 * j + 1)))
                else:
                    sums[j % 2] = value if sums[j % 2] is None else sums[j % 2] + value
                out[start : start + 8, :] = value
            if stage < 2:
                write_traces(sums[0], sums[1], upper, lower, v, i)


def call(kernel, outs, scratch, args):
    return pl.pallas_call(
        kernel,
        out_shape=outs,
        in_specs=[VMEM] * len(args),
        out_specs=jax.tree.map(lambda _: VMEM, outs),
        scratch_shapes=scratch,
        compiler_params=PARAMS,
    )(*args)


def f32(*shape):
    return jax.ShapeDtypeStruct(shape, F32)


def swap(upper, lower):
    count = lax.axis_size("sub")
    below = lax.ppermute(upper, "sub", [(i, i + 1) for i in range(count - 1)])
    above = lax.ppermute(lower, "sub", [(i + 1, i) for i in range(count - 1)])
    return above, below


def shards(coefficients, old_degree, new_degree, destination, metric, near, mortar_up, mortar_low):
    ztab = jnp.asarray(z_table(), BF16)
    packed = call(
        pack_kernel,
        f32(E * BLOCK, E),
        [],
        (coefficients, old_degree.reshape(1, E), new_degree.reshape(1, E), destination.reshape(1, E)),
    )
    packed = packed.reshape(E, 1, BLOCK * E)
    got = lax.all_to_all(packed, ("curve", "sub"), split_axis=0, concat_axis=0, tiled=True)
    got = got.reshape(E * BLOCK, E)
    first, degree, upper, lower = call(
        unpack_kernel, (f32(ROWS, E), f32(8, E), f32(PAY, E), f32(PAY, E)), [], (got, mortar_up, mortar_low)
    )
    state = first
    routes = None
    for stage in range(3):
        above, below = swap(upper, lower)
        given = (state, upper, lower, metric, near, ztab)
        partial = call(
            functools.partial(volume_kernel, ALPHA[stage], BETA[stage]),
            f32(ROWS, E),
            [pltpu.VMEM((ROWS, E), F32), pltpu.VMEM((2 * MODES, E), F32)]
            + [pltpu.VMEM((FACE, E), F32)] * 4
            + [pltpu.VMEM((2 * FACE, E), F32)] * 2
            + [pltpu.VMEM((FACE, 2 * E), BF16)],
            (first,) + given if stage else given,
        )
        cats = [pltpu.VMEM((FACE, 10 * E), BF16)] * 2
        body = functools.partial(post_kernel, stage)
        faces = (f32(FACE, E), f32(FACE, E))
        if stage == 0:
            state, upper, lower, routes = call(
                body,
                (f32(ROWS, E),) + faces + (jax.ShapeDtypeStruct((20 * E, E), BF16),),
                cats,
                (partial, above, below, metric, degree, mortar_up, mortar_low),
            )
        elif stage == 1:
            state, upper, lower = call(
                body, (f32(ROWS, E),) + faces, cats, (partial, above, below, metric, degree, routes)
            )
        else:
            state = call(body, f32(ROWS, E), cats, (partial, above, below, metric, degree, routes))
    return state.reshape(NV, MODES, E)


def solution(mesh):
    lanes = P(None, ("curve", "sub"))
    rank = P(("curve", "sub"))
    cube = P(None, None, ("curve", "sub"))
    return jax.shard_map(
        shards,
        mesh=mesh,
        in_specs=(cube, rank, rank, rank, lanes, lanes, lanes, lanes),
        out_specs=cube,
        check_vma=False,
    )
```

```python
import functools
import math

import jax
import jax.numpy as jnp
import numpy as np
from jax import lax
from jax.experimental import pallas as pl
from jax.experimental.pallas import tpu as pltpu
from jax.sharding import PartitionSpec as P

NV = 5
N = 8
MODES = N * N * N
ROWS = NV * MODES
FACE = NV * N * N
E = 128
BLOCK = 41
STEP = 0.006
ALPHA = (0.0, 0.75, 1.0 / 3.0)
BETA = (1.0, 0.25, 2.0 / 3.0)
PAY = FACE + 8
LIMIT = 24 * 1024 * 1024
F32 = jnp.float32
BF16 = jnp.bfloat16

VMEM = pl.BlockSpec(memory_space=pltpu.VMEM)
HBM = pl.BlockSpec(memory_space=pltpu.HBM)
PARAMS = pltpu.CompilerParams(vmem_limit_bytes=LIMIT)


def legendre_pair(degree_n, points):
    points = np.asarray(points) + 0.0
    value_before = points * 0.0
    value_now = points * 0.0 + 1.0
    for order in range(1, degree_n + 1):
        value_next = ((2 * order - 1) * points * value_now - (order - 1) * value_before) / order
        value_before = value_now
        value_now = value_next
    return (value_now, value_before)


def half_table():
    nodes, weights = np.polynomial.legendre.leggauss(2 * N + 2)
    table = np.zeros((N, N))
    for a in range(N):
        for b in range(a, N):
            fa = math.sqrt((2 * a + 1) / 2.0) * legendre_pair(a, nodes)[0]
            fb = math.sqrt((2 * b + 1) / 2.0) * legendre_pair(b, (nodes - 1.0) / 2.0)[0]
            table[a, b] = np.sum(weights * fa * fb)
    return table


HALF = half_table()
RESTRICT = [[float(HALF[a, b] * math.sqrt((2 * a + 1) / (2 * b + 1))) for b in range(N)] for a in range(N)]
PROJECT = [[float(0.5 * HALF[a, b] * math.sqrt((2 * b + 1) / (2 * a + 1))) for a in range(N)] for b in range(N)]


def z_table():
    out = np.zeros((320, 256))
    for col in range(256):
        line, k = divmod(col, N)
        out[line, col] = 1.0
        out[32 + line, col] = (-1.0) ** k
        for a in range(k):
            if (k - a) % 2 == 1:
                out[64 + line * N + a, col] = 1.0
    return out


def iota(shape, axis):
    return lax.broadcasted_iota(jnp.int32, shape, axis)


def split(x):
    high = x.astype(BF16)
    return high, (x - high.astype(F32)).astype(BF16)


def dot(a, b):
    return lax.dot_general(a, b, (((1,), (0,)), ((), ())), preferred_element_type=F32)


def dot_nt(a, b):
    return lax.dot_general(a, b, (((1,), (1,)), ((), ())), preferred_element_type=F32)


def onehot(flag):
    return jnp.where(flag, 1.0, 0.0)


def pack_kernel(coef, index, out):
    row = iota((E, E), 0)
    col = iota((E, E), 1)
    old, new_row, dest = index[0:1, :], index[1:2, :], index[2:3, :]
    kept = jnp.minimum(old, new_row)
    target = lax.shift_right_logical(dest, 7)
    slot = dest & (E - 1)
    target_f = jnp.broadcast_to(target.astype(F32), (E, E))
    same = target_f == target_f.T
    rank = jnp.sum(onehot(same & (row < col)), axis=0, keepdims=True)
    here = jnp.broadcast_to(target, (E, E)) == row
    pick0 = onehot(here & (rank < 0.5)).astype(BF16)
    pick1 = onehot(here & (rank > 0.5)).astype(BF16)
    slot_f = jnp.broadcast_to((slot - E).astype(F32), (E, E))
    new_f = jnp.broadcast_to(new_row.astype(F32), (E, E))
    tags0 = jnp.where(row == 0, slot_f, jnp.where(row == 1, new_f, 0.0)).astype(BF16)
    tags1 = jnp.where(row == 2, slot_f, jnp.where(row == 3, new_f, 0.0)).astype(BF16)
    tags = dot_nt(pick0, tags0) + dot_nt(pick1, tags1)
    tags = tags + jnp.where((col == 0) | (col == 2), float(E), 0.0)
    out[pl.ds(40, E, stride=BLOCK), :] = tags
    pick = jnp.concatenate([pick0, pick1], axis=0)
    pick = jnp.concatenate([pick, pick], axis=1)
    for q in range(4):
        mode = row + E * q
        i = lax.shift_right_logical(mode, 6)
        j = lax.shift_right_logical(mode, 3) & 7
        k = mode & 7
        live = jnp.maximum(jnp.maximum(i, j), k) <= kept
        weight = ((2 * i + 1) * (2 * j + 1) * (2 * k + 1)).astype(F32)
        weight = jnp.where(live, jnp.sqrt(weight), 0.0)
        for v in range(NV):
            g = 4 * v + q
            high, low = split(coef[v, E * q : E * (q + 1), :] * weight)
            moved = dot_nt(pick, jnp.concatenate([high, low], axis=1))
            out[pl.ds(g, E, stride=BLOCK), :] = moved[:E]
            out[pl.ds(20 + g, E, stride=BLOCK), :] = moved[E:]


def write_traces(even, odd, upper, lower, v, i):
    rows = slice((v * N + i) * N, (v * N + i) * N + N)
    upper[rows, :] = even + odd
    lower[rows, :] = even - odd


def unpack_kernel(got, mortar_up, mortar_low, solution, degree, upper, lower):
    row = iota((E, E), 0)
    tags = got[pl.ds(40, E, stride=BLOCK), :].T
    place0 = onehot(row.astype(F32) == tags[0:1, :]).astype(BF16)
    place1 = onehot(row.astype(F32) == tags[2:3, :]).astype(BF16)
    place = jnp.concatenate([place0, place1], axis=1)
    degrees = jnp.concatenate([tags[1:2, :], tags[3:4, :]], axis=1)
    degrees = jnp.broadcast_to(degrees, (16, 2 * E)).astype(BF16)
    degree[...] = dot_nt(degrees, place)[:8, :]
    for g in range(20):
        both = jnp.concatenate(
            [got[pl.ds(g, E, stride=BLOCK), :], got[pl.ds(20 + g, E, stride=BLOCK), :]], axis=0
        )
        high, low = split(both)
        moved = dot(place, jnp.concatenate([high, low], axis=1))
        solution[E * g : E * (g + 1), :] = (moved[:, :E] + moved[:, E:]).T
    for v in range(NV):
        for i in range(N):
            base = v * MODES + i * 64
            line = [solution[base + 8 * j : base + 8 * j + 8, :] for j in range(N)]
            even = (line[0] + line[2]) + (line[4] + line[6])
            odd = (line[1] + line[3]) + (line[5] + line[7])
            write_traces(even, odd, upper, lower, v, i)
    for table, face in ((mortar_up, upper), (mortar_low, lower)):
        face[FACE:PAY, :] = jnp.full((PAY - FACE, E), -1.0, F32)
        face[FACE : FACE + 2, :] = table[:, 0:E].astype(F32)
        face[FACE + 2 : FACE + 4, 0:16] = table[:, E : E + 16].astype(F32)


def couple(d, first, k):
    half = [(0.5 * k) * d[v] for v in range(NV)]
    vel, pres = 0.5 * d[first], 0.5 * d[4]
    half[0] = half[0] + vel
    half[first] = half[first] + pres
    half[4] = half[4] + vel
    return half


def halves_of(plus, minus):
    return [p - m for p, m in zip(plus, minus)], [p + m for p, m in zip(plus, minus)]


def volume_kernel(alpha, beta, *refs):
    if alpha:
        first, *refs = refs
    (state, upper, lower, metric, near, ztab, out, xsum, zsum, xp, xm, zp, zm, xl, zl, cat) = refs
    row = iota((E, E), 0)
    gather = []
    for d in range(4):
        pick = onehot(row == near[d : d + 1, :]).astype(BF16)
        gather.append(jnp.concatenate([pick, pick], axis=0))
    for v in range(NV):
        for h in range(2):
            base = v * MODES + 256 * h
            high, low = split(state[base : base + 256, :])
            both = jnp.concatenate([high, low], axis=1)
            count = 320 if v >= 3 else 64
            sums = dot(ztab[0:count, :], both)
            sums = sums[:, :E] + sums[:, E:]
            zp[v * 64 + 32 * h : v * 64 + 32 * h + 32, :] = sums[0:32]
            zm[v * 64 + 32 * h : v * 64 + 32 * h + 32, :] = sums[32:64]
            if v >= 3:
                zsum[(v - 3) * MODES + 256 * h : (v - 3) * MODES + 256 * h + 256, :] = sums[64:]
    for v in range(NV):
        for j in range(N):
            line = [state[v * MODES + 64 * i + 8 * j : v * MODES + 64 * i + 8 * j + 8, :] for i in range(N)]
            even = (line[0] + line[2]) + (line[4] + line[6])
            odd = (line[1] + line[3]) + (line[5] + line[7])
            write_traces(even, odd, xp, xm, v, j)

    def outer(face, pick):
        for v in range(NV):
            high, low = split(face[64 * v : 64 * v + 64, :])
            cat[64 * v : 64 * v + 64, 0:E] = high
            cat[64 * v : 64 * v + 64, E : 2 * E] = low
        return dot(cat[...], pick)

    def by_variable(x):
        return [x[64 * v : 64 * v + 64] for v in range(NV)]

    for plus, minus, where, first_v, k_minus, scale, result in (
        (xp, xm, (0, 1), 1, 2.0, 1.0, xl),
        (zp, zm, (2, 3), 3, 1.0, 0.5, zl),
    ):
        d_plus = by_variable(outer(minus, gather[where[0]]) - plus[...])
        d_minus = by_variable(outer(plus, gather[where[1]]) - minus[...])
        even, odd = halves_of(couple(d_plus, first_v, -1.0), couple(d_minus, first_v, k_minus))
        for v in range(NV):
            result[64 * v : 64 * v + 64, :] = scale * even[v] if scale != 1.0 else even[v]
            result[FACE + 64 * v : FACE + 64 * v + 64, :] = scale * odd[v] if scale != 1.0 else odd[v]

    full = [jnp.broadcast_to(metric[d : d + 1, :], (8, E)) for d in range(3)]
    kx = [full[0] * (-0.5 * beta * STEP * (2 * a + 1)) for a in range(N)]
    ky = [full[1] * (-0.05 * beta * STEP * (2 * a + 1)) for a in range(N)]
    kz = full[2] * (-beta * STEP) * (2 * iota((8, E), 0) + 1).astype(F32)
    odd_k = (iota((8, E), 0) & 1) == 1

    def at(ref, start):
        return ref[pl.ds(pl.multiple_of(start, 8), 8), :]

    def x_pass(j, carry):
        s = [
            [at(xl, 64 * v + 8 * j) for v in range(NV)],
            [at(xl, FACE + 64 * v + 8 * j) for v in range(NV)],
        ]
        for i in range(N - 1, -1, -1):
            rows = [v * MODES + 64 * i + 8 * j for v in range(NV)]
            now = s[i % 2]
            for v in range(NV):
                xsum[pl.ds(pl.multiple_of(rows[v], 8), 8), :] = kx[i] * now[v]
            if i:
                r, u, y, w, p = [at(state, rows[v]) for v in range(NV)]
                twice = u + u
                f = [r + twice, u + (p + p), y, w, p + twice]
                s[(i + 1) % 2] = [a + b for a, b in zip(s[(i + 1) % 2], f)]
        return carry

    lax.fori_loop(0, N, x_pass, 0)

    def y_pass(i, carry):
        d_plus = [-at(upper, 64 * v + 8 * i) for v in range(NV)]
        d_minus = [-at(lower, 64 * v + 8 * i) for v in range(NV)]
        even, odd = halves_of(couple(d_plus, 2, -1.0), couple(d_minus, 2, 1.1))
        s = [[10.0 * x for x in even], [10.0 * x for x in odd]]
        z_even = [at(zl, 64 * v + 8 * i) for v in range(NV)]
        z_odd = [at(zl, FACE + 64 * v + 8 * i) for v in range(NV)]
        for j in range(N - 1, -1, -1):
            inner = 64 * i + 8 * j
            rows = [v * MODES + inner for v in range(NV)]
            c = [at(state, rows[v]) for v in range(NV)]
            sw, sp = at(zsum, inner), at(zsum, MODES + inner)
            zs = (sw, None, None, sp, sw)
            now = s[j % 2]
            for v in range(NV):
                lift = jnp.where(
                    odd_k,
                    jnp.broadcast_to(z_odd[v][j : j + 1, :], (8, E)),
                    jnp.broadcast_to(z_even[v][j : j + 1, :], (8, E)),
                )
                if zs[v] is not None:
                    lift = lift + zs[v]
                total = at(xsum, rows[v]) + ky[j] * now[v] + kz * lift
                if alpha:
                    total = total + (alpha * at(first, rows[v]) + beta * c[v])
                else:
                    total = total + c[v]
                out[pl.ds(pl.multiple_of(rows[v], 8), 8), :] = total
            if j:
                r, u, y, w, p = c
                y20 = 20.0 * y
                f = [r + y20, u, y + 20.0 * p, w, p + y20]
                s[(j + 1) % 2] = [a + b for a, b in zip(s[(j + 1) % 2], f)]
        return carry

    lax.fori_loop(0, N, y_pass, 0)


def build_routes(pay, table, inside):
    wide = iota((E, 2 * E), 0).astype(F32)
    pad = jnp.full((1, E - 16), -1.0, F32)

    def own(r):
        return jnp.concatenate([table[r : r + 1, 0:E].astype(F32), table[r : r + 1, E : E + 16].astype(F32), pad], axis=1)

    far_elem = jnp.concatenate([pay[FACE : FACE + 1, :], pay[FACE + 2 : FACE + 3, :]], axis=1)
    far_half = jnp.concatenate([pay[FACE + 1 : FACE + 2, :], pay[FACE + 3 : FACE + 4, :]], axis=1)
    own_elem, own_half = own(0), own(1)
    far_pick = jnp.where(wide == far_elem, inside, 0.0)
    own_pick = onehot(wide == own_elem).astype(BF16)
    far_whole, own_whole = onehot(far_half == 0.0), onehot(own_half == 0.0)
    far_1, far_2 = onehot(far_half == 1.0), onehot(far_half == 2.0)
    own_1, own_2 = onehot(own_half == 1.0), onehot(own_half == 2.0)
    weights = (
        far_whole * own_whole,
        own_whole * (far_1 + far_2),
        own_whole * (far_1 - far_2),
        far_whole * (own_1 + own_2),
        far_whole * (own_1 - own_2),
    )
    return [dot_nt((far_pick * w).astype(BF16), own_pick).astype(BF16) for w in weights]


def post_kernel(stage, *refs):
    beta = BETA[stage]
    if stage == 0:
        (partial, above, below, metric, degree, table_up, table_low, out, upper, lower, routes, cat_up, cat_low) = refs
        place = lax.axis_index("sub")
        last = lax.axis_size("sub") - 1
        inside = (jnp.where(place < last, 1.0, 0.0), jnp.where(place > 0, 1.0, 0.0))
        for side, (pay, table) in enumerate(((above, table_up), (below, table_low))):
            for n, route in enumerate(build_routes(pay, table, inside[side])):
                for part in range(2):
                    start = side * 10 * E + part * 5 * E + n * E
                    routes[start : start + E, :] = route
    elif stage == 1:
        (partial, above, below, metric, degree, routes, out, upper, lower, cat_up, cat_low) = refs
    else:
        (partial, above, below, metric, degree, routes, final, cat_up, cat_low, out, sems) = refs

    def mix(line, table, parity, transposed):
        result = []
        for a in range(N):
            total = None
            for b in range(N):
                if (a + b) % 2 != parity or (b > a if transposed else b < a):
                    continue
                term = table[a][b] * line[b]
                total = term if total is None else total + term
            result.append(jnp.zeros_like(line[0]) if total is None else total)
        return jnp.concatenate(result, axis=0)

    far = []
    for side, (face, cat) in enumerate(((above, cat_up), (below, cat_low))):
        for v in range(NV):
            whole = face[64 * v : 64 * v + 64, :]
            line = [whole[8 * i : 8 * i + 8] for i in range(N)]
            kinds = (
                whole,
                mix(line, RESTRICT, 0, False),
                mix(line, RESTRICT, 1, False),
                mix(line, PROJECT, 0, True),
                mix(line, PROJECT, 1, True),
            )
            for n, kind in enumerate(kinds):
                high, low = split(kind)
                cat[64 * v : 64 * v + 64, n * E : n * E + E] = high
                cat[64 * v : 64 * v + 64, (n + 5) * E : (n + 5) * E + E] = low
        far.append(dot(cat[...], routes[side * 10 * E : (side + 1) * 10 * E, :]))
    far_up, far_low = far
    k_row = iota((8, E), 0)
    deg = degree[...]
    masks = [onehot(jnp.maximum(k_row, n).astype(F32) <= deg) for n in range(N)]
    if stage == 2:
        back = 1.0 / jnp.sqrt((2 * k_row + 1).astype(F32))
        masks = [m * back for m in masks]
    full = jnp.broadcast_to(metric[1:2, :], (8, E))
    ky = [full * (-0.5 * beta * STEP * (2 * a + 1)) for a in range(N)]
    sent = []
    for i in range(N):
        up = [far_up[64 * v + 8 * i : 64 * v + 8 * i + 8] for v in range(NV)]
        low = [far_low[64 * v + 8 * i : 64 * v + 8 * i + 8] for v in range(NV)]
        lift = halves_of(couple(up, 2, -1.0), couple(low, 2, 1.1))
        for v in range(NV):
            sums = [None, None]
            for j in range(N):
                start = v * MODES + 64 * i + 8 * j
                value = masks[max(i, j)] * (partial[start : start + 8, :] + ky[j] * lift[j % 2][v])
                if stage == 2:
                    value = value * (1.0 / math.sqrt((2 * i + 1) * (2 * j + 1)))
                else:
                    sums[j % 2] = value if sums[j % 2] is None else sums[j % 2] + value
                if stage == 2:
                    out[v, 64 * i + 8 * j : 64 * i + 8 * j + 8, :] = value
                else:
                    out[start : start + 8, :] = value
            if stage < 2:
                write_traces(sums[0], sums[1], upper, lower, v, i)
        if stage == 2:
            part = pl.ds(64 * i, 64)
            sent.append(pltpu.make_async_copy(out.at[:, part, :], final.at[:, part, :], sems.at[i]))
            sent[i].start()
    for copy in sent:
        copy.wait()


def call(kernel, outs, scratch, args, result=VMEM):
    return pl.pallas_call(
        kernel,
        out_shape=outs,
        in_specs=[VMEM] * len(args),
        out_specs=jax.tree.map(lambda _: result, outs),
        scratch_shapes=scratch,
        compiler_params=PARAMS,
    )(*args)


def f32(*shape):
    return jax.ShapeDtypeStruct(shape, F32)


def swap(upper, lower):
    count = lax.axis_size("sub")
    below = lax.ppermute(upper, "sub", [(i, (i + 1) % count) for i in range(count)])
    above = lax.ppermute(lower, "sub", [((i + 1) % count, i) for i in range(count)])
    return above, below


def shards(coefficients, old_degree, new_degree, destination, metric, near, mortar_up, mortar_low):
    ztab = jnp.asarray(z_table(), BF16)
    packed = call(
        pack_kernel,
        f32(E * BLOCK, E),
        [],
        (coefficients, jnp.stack([old_degree, new_degree, destination])),
    )
    packed = packed.reshape(E, 1, BLOCK * E)
    got = lax.all_to_all(packed, ("curve", "sub"), split_axis=0, concat_axis=0, tiled=True)
    got = got.reshape(E * BLOCK, E)
    first, degree, upper, lower = call(
        unpack_kernel, (f32(ROWS, E), f32(8, E), f32(PAY, E), f32(PAY, E)), [], (got, mortar_up, mortar_low)
    )
    state = first
    routes = None
    for stage in range(3):
        above, below = swap(upper, lower)
        given = (state, upper, lower, metric, near, ztab)
        partial = call(
            functools.partial(volume_kernel, ALPHA[stage], BETA[stage]),
            f32(ROWS, E),
            [pltpu.VMEM((ROWS, E), F32), pltpu.VMEM((2 * MODES, E), F32)]
            + [pltpu.VMEM((FACE, E), F32)] * 4
            + [pltpu.VMEM((2 * FACE, E), F32)] * 2
            + [pltpu.VMEM((FACE, 2 * E), BF16)],
            (first,) + given if stage else given,
        )
        cats = [pltpu.VMEM((FACE, 10 * E), BF16)] * 2
        body = functools.partial(post_kernel, stage)
        faces = (f32(FACE, E), f32(FACE, E))
        if stage == 0:
            state, upper, lower, routes = call(
                body,
                (f32(ROWS, E),) + faces + (jax.ShapeDtypeStruct((20 * E, E), BF16),),
                cats,
                (partial, above, below, metric, degree, mortar_up, mortar_low),
            )
        elif stage == 1:
            state, upper, lower = call(
                body, (f32(ROWS, E),) + faces, cats, (partial, above, below, metric, degree, routes)
            )
        else:
            cats = cats + [pltpu.VMEM((NV, MODES, E), F32), pltpu.SemaphoreType.DMA((N,))]
            args = (partial, above, below, metric, degree, routes)
            state = call(body, f32(NV, MODES, E), cats, args, result=HBM)
    return state


def solution(mesh):
    lanes = P(None, ("curve", "sub"))
    rank = P(("curve", "sub"))
    cube = P(None, None, ("curve", "sub"))
    return jax.shard_map(
        shards,
        mesh=mesh,
        in_specs=(cube, rank, rank, rank, lanes, lanes, lanes, lanes),
        out_specs=cube,
        check_vma=False,
    )
```

```python
import functools
import math

import jax
import jax.numpy as jnp
import numpy as np
from jax import lax
from jax.experimental import pallas as pl
from jax.experimental.pallas import tpu as pltpu
from jax.sharding import PartitionSpec as P

NV = 5
N = 8
MODES = N * N * N
ROWS = NV * MODES
FACE = NV * N * N
E = 128
BLOCK = 41
STEP = 0.006
ALPHA = (0.0, 0.75, 1.0 / 3.0)
BETA = (1.0, 0.25, 2.0 / 3.0)
PAY = FACE + 8
LIMIT = 24 * 1024 * 1024
F32 = jnp.float32
BF16 = jnp.bfloat16

VMEM = pl.BlockSpec(memory_space=pltpu.VMEM)
HBM = pl.BlockSpec(memory_space=pltpu.HBM)
PARAMS = pltpu.CompilerParams(vmem_limit_bytes=LIMIT)


def legendre_pair(degree_n, points):
    points = np.asarray(points) + 0.0
    value_before = points * 0.0
    value_now = points * 0.0 + 1.0
    for order in range(1, degree_n + 1):
        value_next = ((2 * order - 1) * points * value_now - (order - 1) * value_before) / order
        value_before = value_now
        value_now = value_next
    return (value_now, value_before)


def half_table():
    nodes, weights = np.polynomial.legendre.leggauss(2 * N + 2)
    table = np.zeros((N, N))
    for a in range(N):
        for b in range(a, N):
            fa = math.sqrt((2 * a + 1) / 2.0) * legendre_pair(a, nodes)[0]
            fb = math.sqrt((2 * b + 1) / 2.0) * legendre_pair(b, (nodes - 1.0) / 2.0)[0]
            table[a, b] = np.sum(weights * fa * fb)
    return table


HALF = half_table()
RESTRICT = [[float(HALF[a, b] * math.sqrt((2 * a + 1) / (2 * b + 1))) for b in range(N)] for a in range(N)]
PROJECT = [[float(0.5 * HALF[a, b] * math.sqrt((2 * b + 1) / (2 * a + 1))) for a in range(N)] for b in range(N)]


def z_table():
    out = np.zeros((320, 256))
    for col in range(256):
        line, k = divmod(col, N)
        out[line, col] = 1.0
        out[32 + line, col] = (-1.0) ** k
        for a in range(k):
            if (k - a) % 2 == 1:
                out[64 + line * N + a, col] = 1.0
    return out


def iota(shape, axis):
    return lax.broadcasted_iota(jnp.int32, shape, axis)


def split(x):
    high = x.astype(BF16)
    return high, (x - high.astype(F32)).astype(BF16)


def dot(a, b):
    return lax.dot_general(a, b, (((1,), (0,)), ((), ())), preferred_element_type=F32)


def dot_nt(a, b):
    return lax.dot_general(a, b, (((1,), (1,)), ((), ())), preferred_element_type=F32)


def onehot(flag):
    return jnp.where(flag, 1.0, 0.0)


def pack_kernel(coef, index, out):
    row = iota((E, E), 0)
    col = iota((E, E), 1)
    old, new_row, dest = index[0:1, :], index[1:2, :], index[2:3, :]
    kept = jnp.minimum(old, new_row)
    target = lax.shift_right_logical(dest, 7)
    slot = dest & (E - 1)
    target_f = jnp.broadcast_to(target.astype(F32), (E, E))
    same = target_f == target_f.T
    rank = jnp.sum(onehot(same & (row < col)), axis=0, keepdims=True)
    here = jnp.broadcast_to(target, (E, E)) == row
    pick0 = onehot(here & (rank < 0.5)).astype(BF16)
    pick1 = onehot(here & (rank > 0.5)).astype(BF16)
    slot_f = jnp.broadcast_to((slot - E).astype(F32), (E, E))
    new_f = jnp.broadcast_to(new_row.astype(F32), (E, E))
    tags0 = jnp.where(row == 0, slot_f, jnp.where(row == 1, new_f, 0.0)).astype(BF16)
    tags1 = jnp.where(row == 2, slot_f, jnp.where(row == 3, new_f, 0.0)).astype(BF16)
    tags = dot_nt(pick0, tags0) + dot_nt(pick1, tags1)
    tags = tags + jnp.where((col == 0) | (col == 2), float(E), 0.0)
    out[pl.ds(40, E, stride=BLOCK), :] = tags
    pick = jnp.concatenate([pick0, pick1], axis=0)
    pick = jnp.concatenate([pick, pick], axis=1)
    for q in range(4):
        mode = row + E * q
        i = lax.shift_right_logical(mode, 6)
        j = lax.shift_right_logical(mode, 3) & 7
        k = mode & 7
        live = jnp.maximum(jnp.maximum(i, j), k) <= kept
        weight = ((2 * i + 1) * (2 * j + 1) * (2 * k + 1)).astype(F32)
        weight = jnp.where(live, jnp.sqrt(weight), 0.0)
        for v in range(NV):
            g = 4 * v + q
            high, low = split(coef[v, E * q : E * (q + 1), :] * weight)
            moved = dot_nt(pick, jnp.concatenate([high, low], axis=1))
            out[pl.ds(g, E, stride=BLOCK), :] = moved[:E]
            out[pl.ds(20 + g, E, stride=BLOCK), :] = moved[E:]


def write_traces(even, odd, upper, lower, v, i):
    rows = slice((v * N + i) * N, (v * N + i) * N + N)
    upper[rows, :] = even + odd
    lower[rows, :] = even - odd


def unpack_kernel(got, mortar_up, mortar_low, solution, degree, upper, lower):
    row = iota((E, E), 0)
    tags = got[pl.ds(40, E, stride=BLOCK), :].T
    place0 = onehot(row.astype(F32) == tags[0:1, :]).astype(BF16)
    place1 = onehot(row.astype(F32) == tags[2:3, :]).astype(BF16)
    place = jnp.concatenate([place0, place1], axis=1)
    degrees = jnp.concatenate([tags[1:2, :], tags[3:4, :]], axis=1)
    degrees = jnp.broadcast_to(degrees, (16, 2 * E)).astype(BF16)
    degree[...] = dot_nt(degrees, place)[:8, :]
    for g in range(20):
        both = jnp.concatenate(
            [got[pl.ds(g, E, stride=BLOCK), :], got[pl.ds(20 + g, E, stride=BLOCK), :]], axis=0
        )
        high, low = split(both)
        moved = dot(place, jnp.concatenate([high, low], axis=1))
        solution[E * g : E * (g + 1), :] = (moved[:, :E] + moved[:, E:]).T
    for v in range(NV):
        for i in range(N):
            base = v * MODES + i * 64
            line = [solution[base + 8 * j : base + 8 * j + 8, :] for j in range(N)]
            even = (line[0] + line[2]) + (line[4] + line[6])
            odd = (line[1] + line[3]) + (line[5] + line[7])
            write_traces(even, odd, upper, lower, v, i)
    for table, face in ((mortar_up, upper), (mortar_low, lower)):
        face[FACE:PAY, :] = jnp.full((PAY - FACE, E), -1.0, F32)
        face[FACE : FACE + 2, :] = table[:, 0:E].astype(F32)
        face[FACE + 2 : FACE + 4, 0:16] = table[:, E : E + 16].astype(F32)


def couple(d, first, k):
    half = [(0.5 * k) * d[v] for v in range(NV)]
    vel, pres = 0.5 * d[first], 0.5 * d[4]
    half[0] = half[0] + vel
    half[first] = half[first] + pres
    half[4] = half[4] + vel
    return half


def halves_of(plus, minus):
    return [p - m for p, m in zip(plus, minus)], [p + m for p, m in zip(plus, minus)]


def degree_masks(degree):
    k_row = iota((8, E), 0)
    return [onehot(jnp.maximum(k_row, n).astype(F32) <= degree[...]) for n in range(N)]


def lift_weights(metric, stage):
    full = jnp.broadcast_to(metric[1:2, :], (8, E))
    return [full * (-0.5 * BETA[stage] * STEP * (2 * a + 1)) for a in range(N)]


def volume_kernel(stage, *refs):
    alpha, beta = ALPHA[stage], BETA[stage]
    if stage:
        first, before, lifts, *refs, state = refs
    else:
        first, *refs = refs
        state = first
    if stage < 2:
        sums_out = refs.pop(7)
    (degree, upper, lower, metric, near, ztab, out, xsum, zsum, xp, xm, zp, zm, xl, zl, cat, live) = refs
    row = iota((E, E), 0)
    masks = degree_masks(degree)
    for n in range(N):
        live[8 * n : 8 * n + 8, :] = masks[n]
    if stage:
        kq = lift_weights(metric, stage - 1)
        for v in range(NV):
            for i in range(N):
                face = 64 * v + 8 * i
                lift = (lifts[face : face + 8, :], lifts[FACE + face : FACE + face + 8, :])
                for j in range(N):
                    start = v * MODES + 64 * i + 8 * j
                    state[start : start + 8, :] = masks[max(i, j)] * (before[start : start + 8, :] + kq[j] * lift[j % 2])
    gather = []
    for d in range(4):
        pick = onehot(row == near[d : d + 1, :]).astype(BF16)
        gather.append(jnp.concatenate([pick, pick], axis=0))
    for v in range(NV):
        for h in range(2):
            base = v * MODES + 256 * h
            high, low = split(state[base : base + 256, :])
            both = jnp.concatenate([high, low], axis=1)
            count = 320 if v >= 3 else 64
            sums = dot(ztab[0:count, :], both)
            sums = sums[:, :E] + sums[:, E:]
            zp[v * 64 + 32 * h : v * 64 + 32 * h + 32, :] = sums[0:32]
            zm[v * 64 + 32 * h : v * 64 + 32 * h + 32, :] = sums[32:64]
            if v >= 3:
                zsum[(v - 3) * MODES + 256 * h : (v - 3) * MODES + 256 * h + 256, :] = sums[64:]
    for v in range(NV):
        for j in range(N):
            line = [state[v * MODES + 64 * i + 8 * j : v * MODES + 64 * i + 8 * j + 8, :] for i in range(N)]
            even = (line[0] + line[2]) + (line[4] + line[6])
            odd = (line[1] + line[3]) + (line[5] + line[7])
            write_traces(even, odd, xp, xm, v, j)

    def outer(face, pick):
        for v in range(NV):
            high, low = split(face[64 * v : 64 * v + 64, :])
            cat[64 * v : 64 * v + 64, 0:E] = high
            cat[64 * v : 64 * v + 64, E : 2 * E] = low
        return dot(cat[...], pick)

    def by_variable(x):
        return [x[64 * v : 64 * v + 64] for v in range(NV)]

    for plus, minus, where, first_v, k_minus, scale, result in (
        (xp, xm, (0, 1), 1, 2.0, 1.0, xl),
        (zp, zm, (2, 3), 3, 1.0, 0.5, zl),
    ):
        d_plus = by_variable(outer(minus, gather[where[0]]) - plus[...])
        d_minus = by_variable(outer(plus, gather[where[1]]) - minus[...])
        even, odd = halves_of(couple(d_plus, first_v, -1.0), couple(d_minus, first_v, k_minus))
        for v in range(NV):
            result[64 * v : 64 * v + 64, :] = scale * even[v] if scale != 1.0 else even[v]
            result[FACE + 64 * v : FACE + 64 * v + 64, :] = scale * odd[v] if scale != 1.0 else odd[v]

    full = [jnp.broadcast_to(metric[d : d + 1, :], (8, E)) for d in range(3)]
    kx = [full[0] * (-0.5 * beta * STEP * (2 * a + 1)) for a in range(N)]
    ky = [full[1] * (-0.05 * beta * STEP * (2 * a + 1)) for a in range(N)]
    kz = full[2] * (-beta * STEP) * (2 * iota((8, E), 0) + 1).astype(F32)
    odd_k = (iota((8, E), 0) & 1) == 1

    def at(ref, start):
        return ref[pl.ds(pl.multiple_of(start, 8), 8), :]

    def x_pass(j, carry):
        s = [
            [at(xl, 64 * v + 8 * j) for v in range(NV)],
            [at(xl, FACE + 64 * v + 8 * j) for v in range(NV)],
        ]
        for i in range(N - 1, -1, -1):
            rows = [v * MODES + 64 * i + 8 * j for v in range(NV)]
            now = s[i % 2]
            for v in range(NV):
                xsum[pl.ds(pl.multiple_of(rows[v], 8), 8), :] = kx[i] * now[v]
            if i:
                r, u, y, w, p = [at(state, rows[v]) for v in range(NV)]
                twice = u + u
                f = [r + twice, u + (p + p), y, w, p + twice]
                s[(i + 1) % 2] = [a + b for a, b in zip(s[(i + 1) % 2], f)]
        return carry

    lax.fori_loop(0, N, x_pass, 0)

    def y_pass(i, carry):
        d_plus = [-at(upper, 64 * v + 8 * i) for v in range(NV)]
        d_minus = [-at(lower, 64 * v + 8 * i) for v in range(NV)]
        even, odd = halves_of(couple(d_plus, 2, -1.0), couple(d_minus, 2, 1.1))
        s = [[10.0 * x for x in even], [10.0 * x for x in odd]]
        z_even = [at(zl, 64 * v + 8 * i) for v in range(NV)]
        z_odd = [at(zl, FACE + 64 * v + 8 * i) for v in range(NV)]
        sums = [[None] * NV, [None] * NV]
        for j in range(N - 1, -1, -1):
            inner = 64 * i + 8 * j
            rows = [v * MODES + inner for v in range(NV)]
            c = [at(state, rows[v]) for v in range(NV)]
            sw, sp = at(zsum, inner), at(zsum, MODES + inner)
            zs = (sw, None, None, sp, sw)
            now = s[j % 2]
            mask = at(live, 8 * jnp.maximum(i, j))
            for v in range(NV):
                lift = jnp.where(
                    odd_k,
                    jnp.broadcast_to(z_odd[v][j : j + 1, :], (8, E)),
                    jnp.broadcast_to(z_even[v][j : j + 1, :], (8, E)),
                )
                if zs[v] is not None:
                    lift = lift + zs[v]
                total = at(xsum, rows[v]) + ky[j] * now[v] + kz * lift
                if alpha:
                    total = total + (alpha * at(first, rows[v]) + beta * c[v])
                else:
                    total = total + c[v]
                total = mask * total
                out[pl.ds(pl.multiple_of(rows[v], 8), 8), :] = total
                held = sums[j % 2]
                held[v] = total if held[v] is None else held[v] + total
            if j:
                r, u, y, w, p = c
                y20 = 20.0 * y
                f = [r + y20, u, y + 20.0 * p, w, p + y20]
                s[(j + 1) % 2] = [a + b for a, b in zip(s[(j + 1) % 2], f)]
        for parity in range(2):
            for v in range(NV if stage < 2 else 0):
                start = FACE * parity + 64 * v + 8 * i
                sums_out[pl.ds(pl.multiple_of(start, 8), 8), :] = sums[parity][v]
        return carry

    lax.fori_loop(0, N, y_pass, 0)


def build_routes(pay, table, inside):
    wide = iota((E, 2 * E), 0).astype(F32)
    pad = jnp.full((1, E - 16), -1.0, F32)

    def own(r):
        return jnp.concatenate([table[r : r + 1, 0:E].astype(F32), table[r : r + 1, E : E + 16].astype(F32), pad], axis=1)

    far_elem = jnp.concatenate([pay[FACE : FACE + 1, :], pay[FACE + 2 : FACE + 3, :]], axis=1)
    far_half = jnp.concatenate([pay[FACE + 1 : FACE + 2, :], pay[FACE + 3 : FACE + 4, :]], axis=1)
    own_elem, own_half = own(0), own(1)
    far_pick = jnp.where(wide == far_elem, inside, 0.0)
    own_pick = onehot(wide == own_elem).astype(BF16)
    far_whole, own_whole = onehot(far_half == 0.0), onehot(own_half == 0.0)
    far_1, far_2 = onehot(far_half == 1.0), onehot(far_half == 2.0)
    own_1, own_2 = onehot(own_half == 1.0), onehot(own_half == 2.0)
    weights = (
        far_whole * own_whole,
        own_whole * (far_1 + far_2),
        own_whole * (far_1 - far_2),
        far_whole * (own_1 + own_2),
        far_whole * (own_1 - own_2),
    )
    return [dot_nt((far_pick * w).astype(BF16), own_pick).astype(BF16) for w in weights]


def far_side(face, cat, routes):
    for v in range(NV):
        high, low = split(face[64 * v : 64 * v + 64, :])
        cat[64 * v : 64 * v + 64, 0:E] = high
        cat[64 * v : 64 * v + 64, E : 2 * E] = low
    picked = dot(cat[...], routes)
    result = []
    for v in range(NV):
        lines = [
            [picked[64 * v + 8 * a : 64 * v + 8 * a + 8, E * n : E * n + E] for a in range(N)] for n in range(5)
        ]
        totals = []
        for a in range(N):
            total = lines[0][a]
            for b in range(a, N):
                total = total + RESTRICT[a][b] * lines[1 + (a + b) % 2][b]
            for b in range(a + 1):
                total = total + PROJECT[a][b] * lines[3 + (a + b) % 2][b]
            totals.append(total)
        result.append(totals)
    return result


def far_lifts(above, below, cat_up, cat_low, routes):
    up = far_side(above, cat_up, routes[0 : 2 * E, :])
    low = far_side(below, cat_low, routes[2 * E : 4 * E, :])
    result = []
    for i in range(N):
        plus = couple([up[v][i] for v in range(NV)], 2, -1.0)
        minus = couple([low[v][i] for v in range(NV)], 2, 1.1)
        result.append(halves_of(plus, minus))
    return result


def trace_kernel(stage, *refs):
    if stage == 0:
        (sums, above, below, metric, degree, table_up, table_low, upper, lower, lifts, routes, cat_up, cat_low) = refs
        place = lax.axis_index("sub")
        last = lax.axis_size("sub") - 1
        inside = (jnp.where(place < last, 1.0, 0.0), jnp.where(place > 0, 1.0, 0.0))
        for side, (pay, table) in enumerate(((above, table_up), (below, table_low))):
            for n, route in enumerate(build_routes(pay, table, inside[side])):
                for part in range(2):
                    start = (side * 2 + part) * E
                    routes[start : start + E, E * n : E * n + E] = route
    else:
        (sums, above, below, metric, degree, routes, upper, lower, lifts, cat_up, cat_low) = refs
    masks = degree_masks(degree)
    kq = lift_weights(metric, stage)
    far = far_lifts(above, below, cat_up, cat_low, routes)
    for i in range(N):
        weight = [sum(masks[max(i, j)] * kq[j] for j in range(p, N, 2)) for p in range(2)]
        for v in range(NV):
            rows = slice(64 * v + 8 * i, 64 * v + 8 * i + 8)
            odd_rows = slice(FACE + 64 * v + 8 * i, FACE + 64 * v + 8 * i + 8)
            lifts[rows, :] = far[i][0][v]
            lifts[odd_rows, :] = far[i][1][v]
            even = sums[rows, :] + weight[0] * far[i][0][v]
            odd = sums[odd_rows, :] + weight[1] * far[i][1][v]
            write_traces(even, odd, upper, lower, v, i)


def final_kernel(partial, above, below, metric, degree, routes, final, cat_up, cat_low, out, sems):
    back = 1.0 / jnp.sqrt((2 * iota((8, E), 0) + 1).astype(F32))
    masks = [m * back for m in degree_masks(degree)]
    kq = lift_weights(metric, 2)
    far = far_lifts(above, below, cat_up, cat_low, routes)
    sent = []
    for i in range(N):
        for v in range(NV):
            for j in range(N):
                start = 64 * i + 8 * j
                value = partial[v * MODES + start : v * MODES + start + 8, :] + kq[j] * far[i][j % 2][v]
                value = (masks[max(i, j)] * (1.0 / math.sqrt((2 * i + 1) * (2 * j + 1)))) * value
                out[v, start : start + 8, :] = value
            part = pl.ds(64 * i, 64)
            copy = pltpu.make_async_copy(out.at[v, part, :], final.at[v, part, :], sems.at[v * N + i])
            copy.start()
            sent.append(copy)
    for copy in sent:
        copy.wait()


def call(kernel, outs, scratch, args, result=VMEM):
    return pl.pallas_call(
        kernel,
        out_shape=outs,
        in_specs=[VMEM] * len(args),
        out_specs=jax.tree.map(lambda _: result, outs),
        scratch_shapes=scratch,
        compiler_params=PARAMS,
    )(*args)


def f32(*shape):
    return jax.ShapeDtypeStruct(shape, F32)


def swap(upper, lower):
    count = lax.axis_size("sub")
    below = lax.ppermute(upper, "sub", [(i, (i + 1) % count) for i in range(count)])
    above = lax.ppermute(lower, "sub", [((i + 1) % count, i) for i in range(count)])
    return above, below


def shards(coefficients, old_degree, new_degree, destination, metric, near, mortar_up, mortar_low):
    ztab = jnp.asarray(z_table(), BF16)
    packed = call(
        pack_kernel,
        f32(E * BLOCK, E),
        [],
        (coefficients, jnp.stack([old_degree, new_degree, destination])),
    )
    packed = packed.reshape(E, 1, BLOCK * E)
    got = lax.all_to_all(packed, ("curve", "sub"), split_axis=0, concat_axis=0, tiled=True)
    got = got.reshape(E * BLOCK, E)
    first, degree, upper, lower = call(
        unpack_kernel, (f32(ROWS, E), f32(8, E), f32(PAY, E), f32(PAY, E)), [], (got, mortar_up, mortar_low)
    )
    faces = (f32(FACE, E), f32(FACE, E))
    cats = [pltpu.VMEM((FACE, 2 * E), BF16)] * 2
    for stage in range(3):
        above, below = swap(upper, lower)
        given = (first,) if stage == 0 else (first, partial, lifts)
        partial, *sums = call(
            functools.partial(volume_kernel, stage),
            (f32(ROWS, E), f32(2 * FACE, E))[: 2 if stage < 2 else 1],
            [pltpu.VMEM((ROWS, E), F32), pltpu.VMEM((2 * MODES, E), F32)]
            + [pltpu.VMEM((FACE, E), F32)] * 4
            + [pltpu.VMEM((2 * FACE, E), F32)] * 2
            + [pltpu.VMEM((FACE, 2 * E), BF16), pltpu.VMEM((8 * N, E), F32)]
            + ([pltpu.VMEM((ROWS, E), F32)] if stage else []),
            given + (degree, upper, lower, metric, near, ztab),
        )
        body = functools.partial(trace_kernel, stage)
        outs = faces + (f32(2 * FACE, E),)
        if stage == 0:
            upper, lower, lifts, routes = call(
                body,
                outs + (jax.ShapeDtypeStruct((4 * E, 5 * E), BF16),),
                cats,
                (*sums, above, below, metric, degree, mortar_up, mortar_low),
            )
        elif stage == 1:
            upper, lower, lifts = call(body, outs, cats, (*sums, above, below, metric, degree, routes))
        else:
            scratch = cats + [pltpu.VMEM((NV, MODES, E), F32), pltpu.SemaphoreType.DMA((NV * N,))]
            args = (partial, above, below, metric, degree, routes)
            return call(final_kernel, f32(NV, MODES, E), scratch, args, result=HBM)


def solution(mesh):
    lanes = P(None, ("curve", "sub"))
    rank = P(("curve", "sub"))
    cube = P(None, None, ("curve", "sub"))
    return jax.shard_map(
        shards,
        mesh=mesh,
        in_specs=(cube, rank, rank, rank, lanes, lanes, lanes, lanes),
        out_specs=cube,
        check_vma=False,
    )
```

```python
import functools
import math

import jax
import jax.numpy as jnp
import numpy as np
from jax import lax
from jax.experimental import pallas as pl
from jax.experimental.pallas import tpu as pltpu
from jax.sharding import PartitionSpec as P

NV = 5
N = 8
MODES = N * N * N
ROWS = NV * MODES
FACE = NV * N * N
E = 128
BLOCK = 41
STEP = 0.006
ALPHA = (0.0, 0.75, 1.0 / 3.0)
BETA = (1.0, 0.25, 2.0 / 3.0)
PAY = FACE + 8
LIMIT = 24 * 1024 * 1024
F32 = jnp.float32
BF16 = jnp.bfloat16

VMEM = pl.BlockSpec(memory_space=pltpu.VMEM)
HBM = pl.BlockSpec(memory_space=pltpu.HBM)
PARAMS = pltpu.CompilerParams(vmem_limit_bytes=LIMIT)


def legendre_pair(degree_n, points):
    points = np.asarray(points) + 0.0
    value_before = points * 0.0
    value_now = points * 0.0 + 1.0
    for order in range(1, degree_n + 1):
        value_next = ((2 * order - 1) * points * value_now - (order - 1) * value_before) / order
        value_before = value_now
        value_now = value_next
    return (value_now, value_before)


def half_table():
    nodes, weights = np.polynomial.legendre.leggauss(2 * N + 2)
    table = np.zeros((N, N))
    for a in range(N):
        for b in range(a, N):
            fa = math.sqrt((2 * a + 1) / 2.0) * legendre_pair(a, nodes)[0]
            fb = math.sqrt((2 * b + 1) / 2.0) * legendre_pair(b, (nodes - 1.0) / 2.0)[0]
            table[a, b] = np.sum(weights * fa * fb)
    return table


HALF = half_table()
RESTRICT = [[float(HALF[a, b] * math.sqrt((2 * a + 1) / (2 * b + 1))) for b in range(N)] for a in range(N)]
PROJECT = [[float(0.5 * HALF[a, b] * math.sqrt((2 * b + 1) / (2 * a + 1))) for a in range(N)] for b in range(N)]


def z_table():
    out = np.zeros((320, 256))
    for col in range(256):
        line, k = divmod(col, N)
        out[line, col] = 1.0
        out[32 + line, col] = (-1.0) ** k
        for a in range(k):
            if (k - a) % 2 == 1:
                out[64 + line * N + a, col] = 1.0
    return out


def iota(shape, axis):
    return lax.broadcasted_iota(jnp.int32, shape, axis)


def split(x):
    high = x.astype(BF16)
    return high, (x - high.astype(F32)).astype(BF16)


def dot(a, b):
    return lax.dot_general(a, b, (((1,), (0,)), ((), ())), preferred_element_type=F32)


def dot_nt(a, b):
    return lax.dot_general(a, b, (((1,), (1,)), ((), ())), preferred_element_type=F32)


def onehot(flag):
    return jnp.where(flag, 1.0, 0.0)


def setup_kernel(index, pick, weights, tags_out):
    row = iota((E, E), 0)
    col = iota((E, E), 1)
    old, new_row, dest = index[0:1, :], index[1:2, :], index[2:3, :]
    kept = jnp.minimum(old, new_row)
    target = lax.shift_right_logical(dest, 7)
    slot = dest & (E - 1)
    target_f = jnp.broadcast_to(target.astype(F32), (E, E))
    same = target_f == target_f.T
    rank = jnp.sum(onehot(same & (row < col)), axis=0, keepdims=True)
    here = jnp.broadcast_to(target, (E, E)) == row
    pick0 = onehot(here & (rank < 0.5)).astype(BF16)
    pick1 = onehot(here & (rank > 0.5)).astype(BF16)
    slot_f = jnp.broadcast_to((slot - E).astype(F32), (E, E))
    new_f = jnp.broadcast_to(new_row.astype(F32), (E, E))
    tags0 = jnp.where(row == 0, slot_f, jnp.where(row == 1, new_f, 0.0)).astype(BF16)
    tags1 = jnp.where(row == 2, slot_f, jnp.where(row == 3, new_f, 0.0)).astype(BF16)
    tags = dot_nt(pick0, tags0) + dot_nt(pick1, tags1)
    tags_out[...] = tags + jnp.where((col == 0) | (col == 2), float(E), 0.0)
    half = jnp.concatenate([pick0, pick1], axis=0)
    pick[...] = jnp.concatenate([half, half], axis=1)
    for q in range(4):
        mode = row + E * q
        i = lax.shift_right_logical(mode, 6)
        j = lax.shift_right_logical(mode, 3) & 7
        k = mode & 7
        live = jnp.maximum(jnp.maximum(i, j), k) <= kept
        weight = ((2 * i + 1) * (2 * j + 1) * (2 * k + 1)).astype(F32)
        weights[E * q : E * (q + 1), :] = jnp.where(live, jnp.sqrt(weight), 0.0)


def pack_kernel(coef, pick, weights, tags, out):
    out[pl.ds(40, E, stride=BLOCK), :] = tags[...]

    def send(group, rows):
        high, low = split(rows)
        moved = dot_nt(pick[...], jnp.concatenate([high, low], axis=1))
        out[pl.ds(group, E, stride=BLOCK), :] = moved[:E]
        out[pl.ds(20 + group, E, stride=BLOCK), :] = moved[E:]

    for v in range(NV):
        x = (coef[v] * weights[...]).reshape(N, N, N, E)
        sums = [(x[:, p] + x[:, p + 2]) + (x[:, p + 4] + x[:, p + 6]) for p in range(2)]
        send(v, jnp.concatenate([part.reshape(64, E) for part in sums], axis=0))
        rest = x[:, 2:].reshape(3 * E, E)
        for n in range(3):
            send(NV + 3 * v + n, rest[E * n : E * (n + 1)])


def write_traces(even, odd, upper, lower, v, i):
    rows = slice((v * N + i) * N, (v * N + i) * N + N)
    upper[rows, :] = even + odd
    lower[rows, :] = even - odd


def placed(got, place, group):
    both = jnp.concatenate(
        [got[pl.ds(group, E, stride=BLOCK), :], got[pl.ds(20 + group, E, stride=BLOCK), :]], axis=0
    )
    high, low = split(both)
    moved = dot(place, jnp.concatenate([high, low], axis=1))
    return (moved[:, :E] + moved[:, E:]).T


def unpack_kernel(got, mortar_up, mortar_low, place_out, degree, upper, lower):
    row = iota((E, E), 0)
    tags = got[pl.ds(40, E, stride=BLOCK), :].T
    place0 = onehot(row.astype(F32) == tags[0:1, :]).astype(BF16)
    place1 = onehot(row.astype(F32) == tags[2:3, :]).astype(BF16)
    place = jnp.concatenate([place0, place1], axis=1)
    place_out[...] = place
    degrees = jnp.concatenate([tags[1:2, :], tags[3:4, :]], axis=1)
    degrees = jnp.broadcast_to(degrees, (16, 2 * E)).astype(BF16)
    degree[...] = dot_nt(degrees, place)[:8, :]
    for v in range(NV):
        sums = placed(got, place, v)
        upper[64 * v : 64 * v + 64, :] = sums[:64] + sums[64:]
        lower[64 * v : 64 * v + 64, :] = sums[:64] - sums[64:]
    for table, face in ((mortar_up, upper), (mortar_low, lower)):
        face[FACE:PAY, :] = jnp.full((PAY - FACE, E), -1.0, F32)
        face[FACE : FACE + 2, :] = table[:, 0:E].astype(F32)
        face[FACE + 2 : FACE + 4, 0:16] = table[:, E : E + 16].astype(F32)


def unpack_rest(got, place, upper, lower, state):
    pick = place[...]
    for v in range(NV):
        for n in range(3):
            rows = placed(got, pick, NV + 3 * v + n)
            for m in range(16):
                i, j = divmod(16 * n + m, 6)
                start = v * MODES + 64 * i + 8 * j + 16
                state[start : start + 8, :] = rows[8 * m : 8 * m + 8]
        for i in range(N):
            base = v * MODES + 64 * i
            face = slice(64 * v + 8 * i, 64 * v + 8 * i + 8)
            line = [state[base + 8 * j : base + 8 * j + 8, :] for j in range(2, N)]
            up, low = 0.5 * upper[face, :], 0.5 * lower[face, :]
            state[base : base + 8, :] = (up + low) - (line[0] + line[2] + line[4])
            state[base + 8 : base + 16, :] = (up - low) - (line[1] + line[3] + line[5])


def couple_one(d, v, first, k):
    half = (0.5 * k) * d[v]
    if v in (0, 4):
        half = half + 0.5 * d[first]
    if v == first:
        half = half + 0.5 * d[4]
    return half


def couple(d, first, k):
    return [couple_one(d, v, first, k) for v in range(NV)]


def halves_of(plus, minus):
    return [p - m for p, m in zip(plus, minus)], [p + m for p, m in zip(plus, minus)]


def degree_masks(degree):
    k_row = iota((8, E), 0)
    return [onehot(jnp.maximum(k_row, n).astype(F32) <= degree[...]) for n in range(N)]


def lift_weights(metric, stage):
    full = jnp.broadcast_to(metric[1:2, :], (8, E))
    return [full * (-0.5 * BETA[stage] * STEP * (2 * a + 1)) for a in range(N)]


def volume_kernel(stage, *refs):
    alpha, beta = ALPHA[stage], BETA[stage]
    if stage:
        first, before, lifts, *refs, state = refs
    else:
        got, place, *refs = refs
        state = refs.pop(8)
    if stage < 2:
        sums_out = refs.pop(7)
    (degree, upper, lower, metric, near, ztab, out, xsum, zsum, xp, xm, zp, zm, xl, zl, cat, live) = refs
    row = iota((E, E), 0)
    masks = degree_masks(degree)
    if stage == 0:
        unpack_rest(got, place, upper, lower, state)
    for n in range(N):
        live[8 * n : 8 * n + 8, :] = masks[n]
    if stage:
        kq = lift_weights(metric, stage - 1)
        for v in range(NV):
            for i in range(N):
                face = 64 * v + 8 * i
                lift = (lifts[face : face + 8, :], lifts[FACE + face : FACE + face + 8, :])
                for j in range(N):
                    start = v * MODES + 64 * i + 8 * j
                    state[start : start + 8, :] = masks[max(i, j)] * (before[start : start + 8, :] + kq[j] * lift[j % 2])
    gather = []
    for d in range(4):
        pick = onehot(row == near[d : d + 1, :]).astype(BF16)
        gather.append(jnp.concatenate([pick, pick], axis=0))
    for v in range(NV):
        for h in range(2):
            base = v * MODES + 256 * h
            high, low = split(state[base : base + 256, :])
            both = jnp.concatenate([high, low], axis=1)
            count = 320 if v >= 3 else 64
            sums = dot(ztab[0:count, :], both)
            sums = sums[:, :E] + sums[:, E:]
            zp[v * 64 + 32 * h : v * 64 + 32 * h + 32, :] = sums[0:32]
            zm[v * 64 + 32 * h : v * 64 + 32 * h + 32, :] = sums[32:64]
            if v >= 3:
                zsum[(v - 3) * MODES + 256 * h : (v - 3) * MODES + 256 * h + 256, :] = sums[64:]
    for v in range(NV):
        for j in range(N):
            line = [state[v * MODES + 64 * i + 8 * j : v * MODES + 64 * i + 8 * j + 8, :] for i in range(N)]
            even = (line[0] + line[2]) + (line[4] + line[6])
            odd = (line[1] + line[3]) + (line[5] + line[7])
            write_traces(even, odd, xp, xm, v, j)

    def outer(face, pick):
        for v in range(NV):
            high, low = split(face[64 * v : 64 * v + 64, :])
            cat[64 * v : 64 * v + 64, 0:E] = high
            cat[64 * v : 64 * v + 64, E : 2 * E] = low
        return dot(cat[...], pick)

    def by_variable(x):
        return [x[64 * v : 64 * v + 64] for v in range(NV)]

    for plus, minus, where, first_v, k_minus, scale, result in (
        (xp, xm, (0, 1), 1, 2.0, 1.0, xl),
        (zp, zm, (2, 3), 3, 1.0, 0.5, zl),
    ):
        d_plus = by_variable(outer(minus, gather[where[0]]) - plus[...])
        d_minus = by_variable(outer(plus, gather[where[1]]) - minus[...])
        even, odd = halves_of(couple(d_plus, first_v, -1.0), couple(d_minus, first_v, k_minus))
        for v in range(NV):
            result[64 * v : 64 * v + 64, :] = scale * even[v] if scale != 1.0 else even[v]
            result[FACE + 64 * v : FACE + 64 * v + 64, :] = scale * odd[v] if scale != 1.0 else odd[v]

    full = [jnp.broadcast_to(metric[d : d + 1, :], (8, E)) for d in range(3)]
    kx = [full[0] * (-0.5 * beta * STEP * (2 * a + 1)) for a in range(N)]
    ky = [full[1] * (-0.05 * beta * STEP * (2 * a + 1)) for a in range(N)]
    kz = full[2] * (-beta * STEP) * (2 * iota((8, E), 0) + 1).astype(F32)
    odd_k = (iota((8, E), 0) & 1) == 1

    def at(ref, start):
        return ref[pl.ds(pl.multiple_of(start, 8), 8), :]

    def x_pass(j, carry):
        s = [
            [at(xl, 64 * v + 8 * j) for v in range(NV)],
            [at(xl, FACE + 64 * v + 8 * j) for v in range(NV)],
        ]
        for i in range(N - 1, -1, -1):
            rows = [v * MODES + 64 * i + 8 * j for v in range(NV)]
            now = s[i % 2]
            for v in range(NV):
                xsum[pl.ds(pl.multiple_of(rows[v], 8), 8), :] = kx[i] * now[v]
            if i:
                r, u, y, w, p = [at(state, rows[v]) for v in range(NV)]
                twice = u + u
                f = [r + twice, u + (p + p), y, w, p + twice]
                s[(i + 1) % 2] = [a + b for a, b in zip(s[(i + 1) % 2], f)]
        return carry

    lax.fori_loop(0, N, x_pass, 0)

    def y_pass(i, carry):
        d_plus = [-at(upper, 64 * v + 8 * i) for v in range(NV)]
        d_minus = [-at(lower, 64 * v + 8 * i) for v in range(NV)]
        even, odd = halves_of(couple(d_plus, 2, -1.0), couple(d_minus, 2, 1.1))
        s = [[10.0 * x for x in even], [10.0 * x for x in odd]]
        z_even = [at(zl, 64 * v + 8 * i) for v in range(NV)]
        z_odd = [at(zl, FACE + 64 * v + 8 * i) for v in range(NV)]
        sums = [[None] * NV, [None] * NV]
        for j in range(N - 1, -1, -1):
            inner = 64 * i + 8 * j
            rows = [v * MODES + inner for v in range(NV)]
            c = [at(state, rows[v]) for v in range(NV)]
            sw, sp = at(zsum, inner), at(zsum, MODES + inner)
            zs = (sw, None, None, sp, sw)
            now = s[j % 2]
            mask = at(live, 8 * jnp.maximum(i, j))
            for v in range(NV):
                lift = jnp.where(
                    odd_k,
                    jnp.broadcast_to(z_odd[v][j : j + 1, :], (8, E)),
                    jnp.broadcast_to(z_even[v][j : j + 1, :], (8, E)),
                )
                if zs[v] is not None:
                    lift = lift + zs[v]
                total = at(xsum, rows[v]) + ky[j] * now[v] + kz * lift
                if alpha:
                    total = total + (alpha * at(first, rows[v]) + beta * c[v])
                else:
                    total = total + c[v]
                total = mask * total
                out[pl.ds(pl.multiple_of(rows[v], 8), 8), :] = total
                held = sums[j % 2]
                held[v] = total if held[v] is None else held[v] + total
            if j:
                r, u, y, w, p = c
                y20 = 20.0 * y
                f = [r + y20, u, y + 20.0 * p, w, p + y20]
                s[(j + 1) % 2] = [a + b for a, b in zip(s[(j + 1) % 2], f)]
        for parity in range(2):
            for v in range(NV if stage < 2 else 0):
                start = FACE * parity + 64 * v + 8 * i
                sums_out[pl.ds(pl.multiple_of(start, 8), 8), :] = sums[parity][v]
        return carry

    lax.fori_loop(0, N, y_pass, 0)


def build_routes(pay, table, inside):
    wide = iota((E, 2 * E), 0).astype(F32)
    pad = jnp.full((1, E - 16), -1.0, F32)

    def own(r):
        return jnp.concatenate([table[r : r + 1, 0:E].astype(F32), table[r : r + 1, E : E + 16].astype(F32), pad], axis=1)

    far_elem = jnp.concatenate([pay[FACE : FACE + 1, :], pay[FACE + 2 : FACE + 3, :]], axis=1)
    far_half = jnp.concatenate([pay[FACE + 1 : FACE + 2, :], pay[FACE + 3 : FACE + 4, :]], axis=1)
    own_elem, own_half = own(0), own(1)
    far_pick = jnp.where(wide == far_elem, inside, 0.0)
    own_pick = onehot(wide == own_elem).astype(BF16)
    far_whole, own_whole = onehot(far_half == 0.0), onehot(own_half == 0.0)
    far_1, far_2 = onehot(far_half == 1.0), onehot(far_half == 2.0)
    own_1, own_2 = onehot(own_half == 1.0), onehot(own_half == 2.0)
    weights = (
        far_whole * own_whole,
        own_whole * (far_1 + far_2),
        own_whole * (far_1 - far_2),
        far_whole * (own_1 + own_2),
        far_whole * (own_1 - own_2),
    )
    return [dot_nt((far_pick * w).astype(BF16), own_pick).astype(BF16) for w in weights]


def far_side(face, cat, routes):
    for v in range(NV):
        high, low = split(face[64 * v : 64 * v + 64, :])
        cat[64 * v : 64 * v + 64, 0:E] = high
        cat[64 * v : 64 * v + 64, E : 2 * E] = low
    return dot(cat[...], routes)


def mixed(picked, v):
    lines = [[picked[64 * v + 8 * a : 64 * v + 8 * a + 8, E * n : E * n + E] for a in range(N)] for n in range(5)]
    totals = []
    for a in range(N):
        total = lines[0][a]
        for b in range(a, N):
            total = total + RESTRICT[a][b] * lines[1 + (a + b) % 2][b]
        for b in range(a + 1):
            total = total + PROJECT[a][b] * lines[3 + (a + b) % 2][b]
        totals.append(total)
    return totals


def far_lifts(above, below, cat_up, cat_low, routes):
    picked_up = far_side(above, cat_up, routes[0 : 2 * E, :])
    picked_low = far_side(below, cat_low, routes[2 * E : 4 * E, :])
    up, low = {}, {}
    for v in (1, 3, 2, 4, 0):
        for n in (2, 4) if v == 2 else (v,):
            if n not in up:
                up[n], low[n] = mixed(picked_up, n), mixed(picked_low, n)
        even, odd = [], []
        for i in range(N):
            plus = couple_one({n: x[i] for n, x in up.items()}, v, 2, -1.0)
            minus = couple_one({n: x[i] for n, x in low.items()}, v, 2, 1.1)
            even.append(plus - minus)
            odd.append(plus + minus)
        yield v, even, odd


def trace_kernel(stage, *refs):
    if stage == 0:
        (sums, above, below, metric, degree, table_up, table_low, upper, lower, lifts, routes, cat_up, cat_low) = refs
        place = lax.axis_index("sub")
        last = lax.axis_size("sub") - 1
        inside = (jnp.where(place < last, 1.0, 0.0), jnp.where(place > 0, 1.0, 0.0))
        for side, (pay, table) in enumerate(((above, table_up), (below, table_low))):
            for n, route in enumerate(build_routes(pay, table, inside[side])):
                for part in range(2):
                    start = (side * 2 + part) * E
                    routes[start : start + E, E * n : E * n + E] = route
    else:
        (sums, above, below, metric, degree, routes, upper, lower, lifts, cat_up, cat_low) = refs
    masks = degree_masks(degree)
    kq = lift_weights(metric, stage)
    weights = [[sum(masks[max(i, j)] * kq[j] for j in range(p, N, 2)) for p in range(2)] for i in range(N)]
    for v, lift_even, lift_odd in far_lifts(above, below, cat_up, cat_low, routes):
        for i in range(N):
            rows = slice(64 * v + 8 * i, 64 * v + 8 * i + 8)
            odd_rows = slice(FACE + 64 * v + 8 * i, FACE + 64 * v + 8 * i + 8)
            lifts[rows, :] = lift_even[i]
            lifts[odd_rows, :] = lift_odd[i]
            even = sums[rows, :] + weights[i][0] * lift_even[i]
            odd = sums[odd_rows, :] + weights[i][1] * lift_odd[i]
            write_traces(even, odd, upper, lower, v, i)


def final_kernel(partial, above, below, metric, degree, routes, final, cat_up, cat_low, out, sems):
    back = 1.0 / jnp.sqrt((2 * iota((8, E), 0) + 1).astype(F32))
    masks = [m * back for m in degree_masks(degree)]
    kq = lift_weights(metric, 2)
    sent = []
    for v, lift_even, lift_odd in far_lifts(above, below, cat_up, cat_low, routes):
        for i in range(N):
            for j in range(N):
                start = 64 * i + 8 * j
                lift = (lift_even, lift_odd)[j % 2][i]
                value = partial[v * MODES + start : v * MODES + start + 8, :] + kq[j] * lift
                value = (masks[max(i, j)] * (1.0 / math.sqrt((2 * i + 1) * (2 * j + 1)))) * value
                out[v, start : start + 8, :] = value
            part = pl.ds(64 * i, 64)
            copy = pltpu.make_async_copy(out.at[v, part, :], final.at[v, part, :], sems.at[v * N + i])
            copy.start()
            sent.append(copy)
    for copy in sent:
        copy.wait()


def call(kernel, outs, scratch, args, result=VMEM, cost=None):
    return pl.pallas_call(
        kernel,
        out_shape=outs,
        in_specs=[VMEM] * len(args),
        out_specs=jax.tree.map(lambda _: result, outs),
        scratch_shapes=scratch,
        compiler_params=PARAMS,
        cost_estimate=cost,
    )(*args)


def f32(*shape):
    return jax.ShapeDtypeStruct(shape, F32)


def swap(upper, lower):
    count = lax.axis_size("sub")
    below = lax.ppermute(upper, "sub", [(i, (i + 1) % count) for i in range(count)])
    above = lax.ppermute(lower, "sub", [((i + 1) % count, i) for i in range(count)])
    return above, below


def shards(coefficients, old_degree, new_degree, destination, metric, near, mortar_up, mortar_low):
    ztab = jnp.asarray(z_table(), BF16)
    chosen = call(
        setup_kernel,
        (jax.ShapeDtypeStruct((2 * E, 2 * E), BF16), f32(MODES, E), f32(E, E)),
        [],
        (jnp.stack([old_degree, new_degree, destination]),),
        cost=pl.CostEstimate(flops=400_000_000, bytes_accessed=1_000_000, transcendentals=0),
    )
    packed = call(pack_kernel, f32(E * BLOCK, E), [], (coefficients, *chosen))
    packed = packed.reshape(E, 1, BLOCK * E)
    got = lax.all_to_all(packed, ("curve", "sub"), split_axis=0, concat_axis=0, tiled=True)
    got = got.reshape(E * BLOCK, E)
    place, degree, upper, lower = call(
        unpack_kernel,
        (jax.ShapeDtypeStruct((E, 2 * E), BF16), f32(8, E), f32(PAY, E), f32(PAY, E)),
        [],
        (got, mortar_up, mortar_low),
    )
    faces = (f32(FACE, E), f32(FACE, E))
    cats = [pltpu.VMEM((FACE, 2 * E), BF16)] * 2
    for stage in range(3):
        above, below = swap(upper, lower)
        given = (got, place) if stage == 0 else (first, partial, lifts)
        partial, *sums = call(
            functools.partial(volume_kernel, stage),
            (f32(ROWS, E), f32(2 * FACE, E), f32(ROWS, E))[: 3 - stage],
            [pltpu.VMEM((ROWS, E), F32), pltpu.VMEM((2 * MODES, E), F32)]
            + [pltpu.VMEM((FACE, E), F32)] * 4
            + [pltpu.VMEM((2 * FACE, E), F32)] * 2
            + [pltpu.VMEM((FACE, 2 * E), BF16), pltpu.VMEM((8 * N, E), F32)]
            + ([pltpu.VMEM((ROWS, E), F32)] if stage else []),
            given + (degree, upper, lower, metric, near, ztab),
        )
        if stage == 0:
            first = sums.pop()
        body = functools.partial(trace_kernel, stage)
        outs = faces + (f32(2 * FACE, E),)
        if stage == 0:
            upper, lower, lifts, routes = call(
                body,
                outs + (jax.ShapeDtypeStruct((4 * E, 5 * E), BF16),),
                cats,
                (*sums, above, below, metric, degree, mortar_up, mortar_low),
            )
        elif stage == 1:
            upper, lower, lifts = call(body, outs, cats, (*sums, above, below, metric, degree, routes))
        else:
            scratch = cats + [pltpu.VMEM((NV, MODES, E), F32), pltpu.SemaphoreType.DMA((NV * N,))]
            args = (partial, above, below, metric, degree, routes)
            return call(final_kernel, f32(NV, MODES, E), scratch, args, result=HBM)


def solution(mesh):
    lanes = P(None, ("curve", "sub"))
    rank = P(("curve", "sub"))
    cube = P(None, None, ("curve", "sub"))
    return jax.shard_map(
        shards,
        mesh=mesh,
        in_specs=(cube, rank, rank, rank, lanes, lanes, lanes, lanes),
        out_specs=cube,
        check_vma=False,
    )
```

```python
import functools
import math

import jax
import jax.numpy as jnp
import numpy as np
from jax import lax
from jax.experimental import pallas as pl
from jax.experimental.pallas import tpu as pltpu
from jax.sharding import PartitionSpec as P

NV = 5
N = 8
MODES = N * N * N
ROWS = NV * MODES
FACE = NV * N * N
E = 128
BLOCK = 41
STEP = 0.006
ALPHA = (0.0, 0.75, 1.0 / 3.0)
BETA = (1.0, 0.25, 2.0 / 3.0)
PAY = FACE + 8
LIMIT = 24 * 1024 * 1024
F32 = jnp.float32
BF16 = jnp.bfloat16

VMEM = pl.BlockSpec(memory_space=pltpu.VMEM)
HBM = pl.BlockSpec(memory_space=pltpu.HBM)
PARAMS = pltpu.CompilerParams(vmem_limit_bytes=LIMIT)


def legendre_pair(degree_n, points):
    points = np.asarray(points) + 0.0
    value_before = points * 0.0
    value_now = points * 0.0 + 1.0
    for order in range(1, degree_n + 1):
        value_next = ((2 * order - 1) * points * value_now - (order - 1) * value_before) / order
        value_before = value_now
        value_now = value_next
    return (value_now, value_before)


def half_table():
    nodes, weights = np.polynomial.legendre.leggauss(2 * N + 2)
    table = np.zeros((N, N))
    for a in range(N):
        for b in range(a, N):
            fa = math.sqrt((2 * a + 1) / 2.0) * legendre_pair(a, nodes)[0]
            fb = math.sqrt((2 * b + 1) / 2.0) * legendre_pair(b, (nodes - 1.0) / 2.0)[0]
            table[a, b] = np.sum(weights * fa * fb)
    return table


HALF = half_table()
RESTRICT = [[float(HALF[a, b] * math.sqrt((2 * a + 1) / (2 * b + 1))) for b in range(N)] for a in range(N)]
PROJECT = [[float(0.5 * HALF[a, b] * math.sqrt((2 * b + 1) / (2 * a + 1))) for a in range(N)] for b in range(N)]


def z_table():
    out = np.zeros((320, 256))
    for col in range(256):
        line, k = divmod(col, N)
        out[line, col] = 1.0
        out[32 + line, col] = (-1.0) ** k
        for a in range(k):
            if (k - a) % 2 == 1:
                out[64 + line * N + a, col] = 1.0
    return out


def iota(shape, axis):
    return lax.broadcasted_iota(jnp.int32, shape, axis)


def split(x):
    high = x.astype(BF16)
    return high, (x - high.astype(F32)).astype(BF16)


def dot(a, b):
    return lax.dot_general(a, b, (((1,), (0,)), ((), ())), preferred_element_type=F32)


def dot_nt(a, b):
    return lax.dot_general(a, b, (((1,), (1,)), ((), ())), preferred_element_type=F32)


def onehot(flag):
    return jnp.where(flag, 1.0, 0.0)


def setup_kernel(index, pick, weights, tags_out):
    row = iota((E, E), 0)
    col = iota((E, E), 1)
    old, new_row, dest = index[0:1, :], index[1:2, :], index[2:3, :]
    kept = jnp.minimum(old, new_row)
    target = lax.shift_right_logical(dest, 7)
    slot = dest & (E - 1)
    target_f = jnp.broadcast_to(target.astype(F32), (E, E))
    same = target_f == target_f.T
    rank = jnp.sum(onehot(same & (row < col)), axis=0, keepdims=True)
    here = jnp.broadcast_to(target, (E, E)) == row
    pick0 = onehot(here & (rank < 0.5)).astype(BF16)
    pick1 = onehot(here & (rank > 0.5)).astype(BF16)
    slot_f = jnp.broadcast_to((slot - E).astype(F32), (E, E))
    new_f = jnp.broadcast_to(new_row.astype(F32), (E, E))
    tags0 = jnp.where(row == 0, slot_f, jnp.where(row == 1, new_f, 0.0)).astype(BF16)
    tags1 = jnp.where(row == 2, slot_f, jnp.where(row == 3, new_f, 0.0)).astype(BF16)
    tags = dot_nt(pick0, tags0) + dot_nt(pick1, tags1)
    tags_out[...] = tags + jnp.where((col == 0) | (col == 2), float(E), 0.0)
    half = jnp.concatenate([pick0, pick1], axis=0)
    pick[...] = jnp.concatenate([half, half], axis=1)
    for q in range(4):
        mode = row + E * q
        i = lax.shift_right_logical(mode, 6)
        j = lax.shift_right_logical(mode, 3) & 7
        k = mode & 7
        live = jnp.maximum(jnp.maximum(i, j), k) <= kept
        weight = ((2 * i + 1) * (2 * j + 1) * (2 * k + 1)).astype(F32)
        weights[E * q : E * (q + 1), :] = jnp.where(live, jnp.sqrt(weight), 0.0)


def pack_kernel(coef, pick, weights, tags, out):
    out[pl.ds(40, E, stride=BLOCK), :] = tags[...]

    def send(group_a, group_b, rows):
        high, low = split(rows)
        moved = dot_nt(pick[...], jnp.concatenate([high, low], axis=1))
        for n, group in enumerate((group_a, group_b)):
            out[pl.ds(group, E, stride=BLOCK), :] = moved[:E, E * n : E * n + E]
            out[pl.ds(20 + group, E, stride=BLOCK), :] = moved[E:, E * n : E * n + E]

    for v in range(NV):
        x = (coef[v] * weights[...]).reshape(N, N, N, E)
        sums = [(x[:, p] + x[:, p + 2]) + (x[:, p + 4] + x[:, p + 6]) for p in range(2)]
        sums = [part.reshape(64, E) for part in sums]
        rest = x[:, 2:].reshape(3 * E, E)
        base = NV + 3 * v
        send(v, base, jnp.concatenate(sums + [rest[:E]], axis=0))
        send(base + 1, base + 2, rest[E:])


def write_traces(even, odd, upper, lower, v, i):
    rows = slice((v * N + i) * N, (v * N + i) * N + N)
    upper[rows, :] = even + odd
    lower[rows, :] = even - odd


def placed(got, place, group):
    both = jnp.concatenate(
        [got[pl.ds(group, E, stride=BLOCK), :], got[pl.ds(20 + group, E, stride=BLOCK), :]], axis=0
    )
    high, low = split(both)
    moved = dot(place, jnp.concatenate([high, low], axis=1))
    return (moved[:, :E] + moved[:, E:]).T


def unpack_kernel(got, mortar_up, mortar_low, place_out, degree, upper, lower):
    row = iota((E, E), 0)
    tags = got[pl.ds(40, E, stride=BLOCK), :].T
    place0 = onehot(row.astype(F32) == tags[0:1, :]).astype(BF16)
    place1 = onehot(row.astype(F32) == tags[2:3, :]).astype(BF16)
    place = jnp.concatenate([place0, place1], axis=1)
    place_out[...] = place
    degrees = jnp.concatenate([tags[1:2, :], tags[3:4, :]], axis=1)
    degrees = jnp.broadcast_to(degrees, (16, 2 * E)).astype(BF16)
    degree[...] = dot_nt(degrees, place)[:8, :]
    for v in range(NV):
        sums = placed(got, place, v)
        upper[64 * v : 64 * v + 64, :] = sums[:64] + sums[64:]
        lower[64 * v : 64 * v + 64, :] = sums[:64] - sums[64:]
    for table, face in ((mortar_up, upper), (mortar_low, lower)):
        face[FACE:PAY, :] = jnp.full((PAY - FACE, E), -1.0, F32)
        face[FACE : FACE + 2, :] = table[:, 0:E].astype(F32)
        face[FACE + 2 : FACE + 4, 0:16] = table[:, E : E + 16].astype(F32)


def unpack_rest(got, place, upper, lower, state):
    pick = place[...]
    for v in range(NV):
        for n in range(3):
            rows = placed(got, pick, NV + 3 * v + n)
            for m in range(16):
                i, j = divmod(16 * n + m, 6)
                start = v * MODES + 64 * i + 8 * j + 16
                state[start : start + 8, :] = rows[8 * m : 8 * m + 8]
        for i in range(N):
            base = v * MODES + 64 * i
            face = slice(64 * v + 8 * i, 64 * v + 8 * i + 8)
            line = [state[base + 8 * j : base + 8 * j + 8, :] for j in range(2, N)]
            up, low = 0.5 * upper[face, :], 0.5 * lower[face, :]
            state[base : base + 8, :] = (up + low) - (line[0] + line[2] + line[4])
            state[base + 8 : base + 16, :] = (up - low) - (line[1] + line[3] + line[5])


def couple_one(d, v, first, k):
    half = (0.5 * k) * d[v]
    if v in (0, 4):
        half = half + 0.5 * d[first]
    if v == first:
        half = half + 0.5 * d[4]
    return half


def couple(d, first, k):
    return [couple_one(d, v, first, k) for v in range(NV)]


def halves_of(plus, minus):
    return [p - m for p, m in zip(plus, minus)], [p + m for p, m in zip(plus, minus)]


def degree_masks(degree):
    k_row = iota((8, E), 0)
    return [onehot(jnp.maximum(k_row, n).astype(F32) <= degree[...]) for n in range(N)]


def lift_weights(metric, stage):
    full = jnp.broadcast_to(metric[1:2, :], (8, E))
    return [full * (-0.5 * BETA[stage] * STEP * (2 * a + 1)) for a in range(N)]


def volume_kernel(stage, *refs):
    alpha, beta = ALPHA[stage], BETA[stage]
    if stage:
        first, before, lifts, *refs, state = refs
    else:
        got, place, *refs = refs
        state = refs.pop(8)
    if stage < 2:
        sums_out = refs.pop(7)
    (degree, upper, lower, metric, near, ztab, out, xsum, zsum, xp, xm, zp, zm, xl, zl, cat, live) = refs
    row = iota((E, E), 0)
    masks = degree_masks(degree)
    if stage == 0:
        unpack_rest(got, place, upper, lower, state)
    for n in range(N):
        live[8 * n : 8 * n + 8, :] = masks[n]
    if stage:
        kq = lift_weights(metric, stage - 1)
        for v in range(NV):
            for i in range(N):
                face = 64 * v + 8 * i
                lift = (lifts[face : face + 8, :], lifts[FACE + face : FACE + face + 8, :])
                for j in range(N):
                    start = v * MODES + 64 * i + 8 * j
                    state[start : start + 8, :] = masks[max(i, j)] * (before[start : start + 8, :] + kq[j] * lift[j % 2])
    gather = []
    for d in range(4):
        pick = onehot(row == near[d : d + 1, :]).astype(BF16)
        gather.append(jnp.concatenate([pick, pick], axis=0))
    for v in range(NV):
        for h in range(2):
            base = v * MODES + 256 * h
            high, low = split(state[base : base + 256, :])
            both = jnp.concatenate([high, low], axis=1)
            count = 320 if v >= 3 else 64
            sums = dot(ztab[0:count, :], both)
            sums = sums[:, :E] + sums[:, E:]
            zp[v * 64 + 32 * h : v * 64 + 32 * h + 32, :] = sums[0:32]
            zm[v * 64 + 32 * h : v * 64 + 32 * h + 32, :] = sums[32:64]
            if v >= 3:
                zsum[(v - 3) * MODES + 256 * h : (v - 3) * MODES + 256 * h + 256, :] = sums[64:]
    for v in range(NV):
        for j in range(N):
            line = [state[v * MODES + 64 * i + 8 * j : v * MODES + 64 * i + 8 * j + 8, :] for i in range(N)]
            even = (line[0] + line[2]) + (line[4] + line[6])
            odd = (line[1] + line[3]) + (line[5] + line[7])
            write_traces(even, odd, xp, xm, v, j)

    def outer(face, pick):
        for v in range(NV):
            high, low = split(face[64 * v : 64 * v + 64, :])
            cat[64 * v : 64 * v + 64, 0:E] = high
            cat[64 * v : 64 * v + 64, E : 2 * E] = low
        return dot(cat[...], pick)

    def by_variable(x):
        return [x[64 * v : 64 * v + 64] for v in range(NV)]

    for plus, minus, where, first_v, k_minus, scale, result in (
        (xp, xm, (0, 1), 1, 2.0, 1.0, xl),
        (zp, zm, (2, 3), 3, 1.0, 0.5, zl),
    ):
        d_plus = by_variable(outer(minus, gather[where[0]]) - plus[...])
        d_minus = by_variable(outer(plus, gather[where[1]]) - minus[...])
        even, odd = halves_of(couple(d_plus, first_v, -1.0), couple(d_minus, first_v, k_minus))
        for v in range(NV):
            result[64 * v : 64 * v + 64, :] = scale * even[v] if scale != 1.0 else even[v]
            result[FACE + 64 * v : FACE + 64 * v + 64, :] = scale * odd[v] if scale != 1.0 else odd[v]

    full = [jnp.broadcast_to(metric[d : d + 1, :], (8, E)) for d in range(3)]
    kx = [full[0] * (-0.5 * beta * STEP * (2 * a + 1)) for a in range(N)]
    ky = [full[1] * (-0.05 * beta * STEP * (2 * a + 1)) for a in range(N)]
    kz = full[2] * (-beta * STEP) * (2 * iota((8, E), 0) + 1).astype(F32)
    odd_k = (iota((8, E), 0) & 1) == 1

    def at(ref, start):
        return ref[pl.ds(pl.multiple_of(start, 8), 8), :]

    def x_pass(j, carry):
        s = [
            [at(xl, 64 * v + 8 * j) for v in range(NV)],
            [at(xl, FACE + 64 * v + 8 * j) for v in range(NV)],
        ]
        for i in range(N - 1, -1, -1):
            rows = [v * MODES + 64 * i + 8 * j for v in range(NV)]
            now = s[i % 2]
            for v in range(NV):
                xsum[pl.ds(pl.multiple_of(rows[v], 8), 8), :] = kx[i] * now[v]
            if i:
                r, u, y, w, p = [at(state, rows[v]) for v in range(NV)]
                twice = u + u
                f = [r + twice, u + (p + p), y, w, p + twice]
                s[(i + 1) % 2] = [a + b for a, b in zip(s[(i + 1) % 2], f)]
        return carry

    lax.fori_loop(0, N, x_pass, 0)

    def y_pass(i, carry):
        d_plus = [-at(upper, 64 * v + 8 * i) for v in range(NV)]
        d_minus = [-at(lower, 64 * v + 8 * i) for v in range(NV)]
        even, odd = halves_of(couple(d_plus, 2, -1.0), couple(d_minus, 2, 1.1))
        s = [[10.0 * x for x in even], [10.0 * x for x in odd]]
        z_even = [at(zl, 64 * v + 8 * i) for v in range(NV)]
        z_odd = [at(zl, FACE + 64 * v + 8 * i) for v in range(NV)]
        sums = [[None] * NV, [None] * NV]
        for j in range(N - 1, -1, -1):
            inner = 64 * i + 8 * j
            rows = [v * MODES + inner for v in range(NV)]
            c = [at(state, rows[v]) for v in range(NV)]
            sw, sp = at(zsum, inner), at(zsum, MODES + inner)
            zs = (sw, None, None, sp, sw)
            now = s[j % 2]
            mask = at(live, 8 * jnp.maximum(i, j))
            for v in range(NV):
                lift = jnp.where(
                    odd_k,
                    jnp.broadcast_to(z_odd[v][j : j + 1, :], (8, E)),
                    jnp.broadcast_to(z_even[v][j : j + 1, :], (8, E)),
                )
                if zs[v] is not None:
                    lift = lift + zs[v]
                total = at(xsum, rows[v]) + ky[j] * now[v] + kz * lift
                if alpha:
                    total = total + (alpha * at(first, rows[v]) + beta * c[v])
                else:
                    total = total + c[v]
                total = mask * total
                out[pl.ds(pl.multiple_of(rows[v], 8), 8), :] = total
                held = sums[j % 2]
                held[v] = total if held[v] is None else held[v] + total
            if j:
                r, u, y, w, p = c
                y20 = 20.0 * y
                f = [r + y20, u, y + 20.0 * p, w, p + y20]
                s[(j + 1) % 2] = [a + b for a, b in zip(s[(j + 1) % 2], f)]
        for parity in range(2):
            for v in range(NV if stage < 2 else 0):
                start = FACE * parity + 64 * v + 8 * i
                sums_out[pl.ds(pl.multiple_of(start, 8), 8), :] = sums[parity][v]
        return carry

    lax.fori_loop(0, N, y_pass, 0)


def build_routes(pay, table, inside):
    wide = iota((E, 2 * E), 0).astype(F32)
    pad = jnp.full((1, E - 16), -1.0, F32)

    def own(r):
        return jnp.concatenate([table[r : r + 1, 0:E].astype(F32), table[r : r + 1, E : E + 16].astype(F32), pad], axis=1)

    far_elem = jnp.concatenate([pay[FACE : FACE + 1, :], pay[FACE + 2 : FACE + 3, :]], axis=1)
    far_half = jnp.concatenate([pay[FACE + 1 : FACE + 2, :], pay[FACE + 3 : FACE + 4, :]], axis=1)
    own_elem, own_half = own(0), own(1)
    far_pick = jnp.where(wide == far_elem, inside, 0.0)
    own_pick = onehot(wide == own_elem).astype(BF16)
    far_whole, own_whole = onehot(far_half == 0.0), onehot(own_half == 0.0)
    far_1, far_2 = onehot(far_half == 1.0), onehot(far_half == 2.0)
    own_1, own_2 = onehot(own_half == 1.0), onehot(own_half == 2.0)
    weights = (
        far_whole * own_whole,
        own_whole * (far_1 + far_2),
        own_whole * (far_1 - far_2),
        far_whole * (own_1 + own_2),
        far_whole * (own_1 - own_2),
    )
    return [dot_nt((far_pick * w).astype(BF16), own_pick).astype(BF16) for w in weights]


def far_side(face, cat, routes):
    for v in range(NV):
        high, low = split(face[64 * v : 64 * v + 64, :])
        cat[64 * v : 64 * v + 64, 0:E] = high
        cat[64 * v : 64 * v + 64, E : 2 * E] = low
    return dot(cat[...], routes)


def mixed(picked, v):
    lines = [[picked[64 * v + 8 * a : 64 * v + 8 * a + 8, E * n : E * n + E] for a in range(N)] for n in range(5)]
    totals = []
    for a in range(N):
        total = lines[0][a]
        for b in range(a, N):
            total = total + RESTRICT[a][b] * lines[1 + (a + b) % 2][b]
        for b in range(a + 1):
            total = total + PROJECT[a][b] * lines[3 + (a + b) % 2][b]
        totals.append(total)
    return totals


def far_lifts(above, below, cat_up, cat_low, routes):
    picked_up = far_side(above, cat_up, routes[0 : 2 * E, :])
    picked_low = far_side(below, cat_low, routes[2 * E : 4 * E, :])
    up, low = {}, {}
    for v in (1, 3, 2, 4, 0):
        for n in (2, 4) if v == 2 else (v,):
            if n not in up:
                up[n], low[n] = mixed(picked_up, n), mixed(picked_low, n)
        even, odd = [], []
        for i in range(N):
            plus = couple_one({n: x[i] for n, x in up.items()}, v, 2, -1.0)
            minus = couple_one({n: x[i] for n, x in low.items()}, v, 2, 1.1)
            even.append(plus - minus)
            odd.append(plus + minus)
        yield v, even, odd


def trace_kernel(stage, *refs):
    if stage == 0:
        (sums, above, below, metric, degree, table_up, table_low, upper, lower, lifts, routes, cat_up, cat_low) = refs
        place = lax.axis_index("sub")
        last = lax.axis_size("sub") - 1
        inside = (jnp.where(place < last, 1.0, 0.0), jnp.where(place > 0, 1.0, 0.0))
        for side, (pay, table) in enumerate(((above, table_up), (below, table_low))):
            for n, route in enumerate(build_routes(pay, table, inside[side])):
                for part in range(2):
                    start = (side * 2 + part) * E
                    routes[start : start + E, E * n : E * n + E] = route
    else:
        (sums, above, below, metric, degree, routes, upper, lower, lifts, cat_up, cat_low) = refs
    masks = degree_masks(degree)
    kq = lift_weights(metric, stage)
    weights = [[sum(masks[max(i, j)] * kq[j] for j in range(p, N, 2)) for p in range(2)] for i in range(N)]
    for v, lift_even, lift_odd in far_lifts(above, below, cat_up, cat_low, routes):
        for i in range(N):
            rows = slice(64 * v + 8 * i, 64 * v + 8 * i + 8)
            odd_rows = slice(FACE + 64 * v + 8 * i, FACE + 64 * v + 8 * i + 8)
            lifts[rows, :] = lift_even[i]
            lifts[odd_rows, :] = lift_odd[i]
            even = sums[rows, :] + weights[i][0] * lift_even[i]
            odd = sums[odd_rows, :] + weights[i][1] * lift_odd[i]
            write_traces(even, odd, upper, lower, v, i)


def final_kernel(partial, above, below, metric, degree, routes, final, cat_up, cat_low, out, sems):
    back = 1.0 / jnp.sqrt((2 * iota((8, E), 0) + 1).astype(F32))
    masks = [m * back for m in degree_masks(degree)]
    kq = lift_weights(metric, 2)
    sent = []
    for v, lift_even, lift_odd in far_lifts(above, below, cat_up, cat_low, routes):
        for i in range(N):
            for j in range(N):
                start = 64 * i + 8 * j
                lift = (lift_even, lift_odd)[j % 2][i]
                value = partial[v * MODES + start : v * MODES + start + 8, :] + kq[j] * lift
                value = (masks[max(i, j)] * (1.0 / math.sqrt((2 * i + 1) * (2 * j + 1)))) * value
                out[v, start : start + 8, :] = value
            part = pl.ds(64 * i, 64)
            copy = pltpu.make_async_copy(out.at[v, part, :], final.at[v, part, :], sems.at[v * N + i])
            copy.start()
            sent.append(copy)
    for copy in sent:
        copy.wait()


def call(kernel, outs, scratch, args, result=VMEM, cost=None):
    return pl.pallas_call(
        kernel,
        out_shape=outs,
        in_specs=[VMEM] * len(args),
        out_specs=jax.tree.map(lambda _: result, outs),
        scratch_shapes=scratch,
        compiler_params=PARAMS,
        cost_estimate=cost,
    )(*args)


def f32(*shape):
    return jax.ShapeDtypeStruct(shape, F32)


def swap(upper, lower):
    count = lax.axis_size("sub")
    below = lax.ppermute(upper, "sub", [(i, (i + 1) % count) for i in range(count)])
    above = lax.ppermute(lower, "sub", [((i + 1) % count, i) for i in range(count)])
    return above, below


def shards(coefficients, old_degree, new_degree, destination, metric, near, mortar_up, mortar_low):
    ztab = jnp.asarray(z_table(), BF16)
    chosen = call(
        setup_kernel,
        (jax.ShapeDtypeStruct((2 * E, 2 * E), BF16), f32(MODES, E), f32(E, E)),
        [],
        (jnp.stack([old_degree, new_degree, destination]),),
        cost=pl.CostEstimate(flops=400_000_000, bytes_accessed=1_000_000, transcendentals=0),
    )
    packed = call(pack_kernel, f32(E * BLOCK, E), [], (coefficients, *chosen))
    packed = packed.reshape(E, 1, BLOCK * E)
    got = lax.all_to_all(packed, ("curve", "sub"), split_axis=0, concat_axis=0, tiled=True)
    got = got.reshape(E * BLOCK, E)
    place, degree, upper, lower = call(
        unpack_kernel,
        (jax.ShapeDtypeStruct((E, 2 * E), BF16), f32(8, E), f32(PAY, E), f32(PAY, E)),
        [],
        (got, mortar_up, mortar_low),
    )
    faces = (f32(FACE, E), f32(FACE, E))
    cats = [pltpu.VMEM((FACE, 2 * E), BF16)] * 2
    for stage in range(3):
        above, below = swap(upper, lower)
        given = (got, place) if stage == 0 else (first, partial, lifts)
        partial, *sums = call(
            functools.partial(volume_kernel, stage),
            (f32(ROWS, E), f32(2 * FACE, E), f32(ROWS, E))[: 3 - stage],
            [pltpu.VMEM((ROWS, E), F32), pltpu.VMEM((2 * MODES, E), F32)]
            + [pltpu.VMEM((FACE, E), F32)] * 4
            + [pltpu.VMEM((2 * FACE, E), F32)] * 2
            + [pltpu.VMEM((FACE, 2 * E), BF16), pltpu.VMEM((8 * N, E), F32)]
            + ([pltpu.VMEM((ROWS, E), F32)] if stage else []),
            given + (degree, upper, lower, metric, near, ztab),
        )
        if stage == 0:
            first = sums.pop()
        body = functools.partial(trace_kernel, stage)
        outs = faces + (f32(2 * FACE, E),)
        if stage == 0:
            upper, lower, lifts, routes = call(
                body,
                outs + (jax.ShapeDtypeStruct((4 * E, 5 * E), BF16),),
                cats,
                (*sums, above, below, metric, degree, mortar_up, mortar_low),
            )
        elif stage == 1:
            upper, lower, lifts = call(body, outs, cats, (*sums, above, below, metric, degree, routes))
        else:
            scratch = cats + [pltpu.VMEM((NV, MODES, E), F32), pltpu.SemaphoreType.DMA((NV * N,))]
            args = (partial, above, below, metric, degree, routes)
            return call(final_kernel, f32(NV, MODES, E), scratch, args, result=HBM)


def solution(mesh):
    lanes = P(None, ("curve", "sub"))
    rank = P(("curve", "sub"))
    cube = P(None, None, ("curve", "sub"))
    return jax.shard_map(
        shards,
        mesh=mesh,
        in_specs=(cube, rank, rank, rank, lanes, lanes, lanes, lanes),
        out_specs=cube,
        check_vma=False,
    )
```

```python
import functools
import math

import jax
import jax.numpy as jnp
import numpy as np
from jax import lax
from jax.experimental import pallas as pl
from jax.experimental.pallas import tpu as pltpu
from jax.sharding import PartitionSpec as P

NV = 5
N = 8
MODES = N * N * N
ROWS = NV * MODES
FACE = NV * N * N
E = 128
BLOCK = 41
STEP = 0.006
ALPHA = (0.0, 0.75, 1.0 / 3.0)
BETA = (1.0, 0.25, 2.0 / 3.0)
PAY = FACE + 8
LIMIT = 24 * 1024 * 1024
F32 = jnp.float32
BF16 = jnp.bfloat16

VMEM = pl.BlockSpec(memory_space=pltpu.VMEM)
HBM = pl.BlockSpec(memory_space=pltpu.HBM)
PARAMS = pltpu.CompilerParams(vmem_limit_bytes=LIMIT)


def legendre_pair(degree_n, points):
    points = np.asarray(points) + 0.0
    value_before = points * 0.0
    value_now = points * 0.0 + 1.0
    for order in range(1, degree_n + 1):
        value_next = ((2 * order - 1) * points * value_now - (order - 1) * value_before) / order
        value_before = value_now
        value_now = value_next
    return (value_now, value_before)


def half_table():
    nodes, weights = np.polynomial.legendre.leggauss(2 * N + 2)
    table = np.zeros((N, N))
    for a in range(N):
        for b in range(a, N):
            fa = math.sqrt((2 * a + 1) / 2.0) * legendre_pair(a, nodes)[0]
            fb = math.sqrt((2 * b + 1) / 2.0) * legendre_pair(b, (nodes - 1.0) / 2.0)[0]
            table[a, b] = np.sum(weights * fa * fb)
    return table


HALF = half_table()
RESTRICT = [[float(HALF[a, b] * math.sqrt((2 * a + 1) / (2 * b + 1))) for b in range(N)] for a in range(N)]
PROJECT = [[float(0.5 * HALF[a, b] * math.sqrt((2 * b + 1) / (2 * a + 1))) for a in range(N)] for b in range(N)]


def z_table():
    out = np.zeros((320, 256))
    for col in range(256):
        line, k = divmod(col, N)
        out[line, col] = 1.0
        out[32 + line, col] = (-1.0) ** k
        for a in range(k):
            if (k - a) % 2 == 1:
                out[64 + line * N + a, col] = 1.0
    return out


def iota(shape, axis):
    return lax.broadcasted_iota(jnp.int32, shape, axis)


def split(x):
    high = x.astype(BF16)
    return high, (x - high.astype(F32)).astype(BF16)


def dot(a, b):
    return lax.dot_general(a, b, (((1,), (0,)), ((), ())), preferred_element_type=F32)


def dot_nt(a, b):
    return lax.dot_general(a, b, (((1,), (1,)), ((), ())), preferred_element_type=F32)


def onehot(flag):
    return jnp.where(flag, 1.0, 0.0)


def setup_kernel(index, pick, weights, tags_out):
    row = iota((E, E), 0)
    col = iota((E, E), 1)
    old, new_row, dest = index[0:1, :], index[1:2, :], index[2:3, :]
    kept = jnp.minimum(old, new_row)
    target = lax.shift_right_logical(dest, 7)
    slot = dest & (E - 1)
    target_f = jnp.broadcast_to(target.astype(F32), (E, E))
    same = target_f == target_f.T
    rank = jnp.sum(onehot(same & (row < col)), axis=0, keepdims=True)
    here = jnp.broadcast_to(target, (E, E)) == row
    pick0 = onehot(here & (rank < 0.5)).astype(BF16)
    pick1 = onehot(here & (rank > 0.5)).astype(BF16)
    slot_f = jnp.broadcast_to((slot - E).astype(F32), (E, E))
    new_f = jnp.broadcast_to(new_row.astype(F32), (E, E))
    tags0 = jnp.where(row == 0, slot_f, jnp.where(row == 1, new_f, 0.0)).astype(BF16)
    tags1 = jnp.where(row == 2, slot_f, jnp.where(row == 3, new_f, 0.0)).astype(BF16)
    tags = dot_nt(pick0, tags0) + dot_nt(pick1, tags1)
    tags_out[...] = tags + jnp.where((col == 0) | (col == 2), float(E), 0.0)
    half = jnp.concatenate([pick0, pick1], axis=0)
    pick[...] = jnp.concatenate([half, half], axis=1)
    for q in range(4):
        mode = row + E * q
        i = lax.shift_right_logical(mode, 6)
        j = lax.shift_right_logical(mode, 3) & 7
        k = mode & 7
        live = jnp.maximum(jnp.maximum(i, j), k) <= kept
        weight = ((2 * i + 1) * (2 * j + 1) * (2 * k + 1)).astype(F32)
        weights[E * q : E * (q + 1), :] = jnp.where(live, jnp.sqrt(weight), 0.0)


def pack_kernel(coef, pick, weights, tags, out):
    out[pl.ds(40, E, stride=BLOCK), :] = tags[...]

    def send(group_a, group_b, rows):
        high, low = split(rows)
        moved = dot_nt(pick[...], jnp.concatenate([high, low], axis=1))
        for n, group in enumerate((group_a, group_b)):
            out[pl.ds(group, E, stride=BLOCK), :] = moved[:E, E * n : E * n + E]
            out[pl.ds(20 + group, E, stride=BLOCK), :] = moved[E:, E * n : E * n + E]

    for v in range(NV):
        x = (coef[v] * weights[...]).reshape(N, N, N, E)
        sums = [(x[:, p] + x[:, p + 2]) + (x[:, p + 4] + x[:, p + 6]) for p in range(2)]
        sums = [part.reshape(64, E) for part in sums]
        rest = x[:, 2:].reshape(3 * E, E)
        base = NV + 3 * v
        send(v, base, jnp.concatenate(sums + [rest[:E]], axis=0))
        send(base + 1, base + 2, rest[E:])


def is_even():
    return (lax.axis_index("sub") & 1) == 0


def odd_sign():
    return jnp.where(is_even(), 1.0, -1.0)


def write_traces(even, odd, upper, lower, v, i):
    rows = slice((v * N + i) * N, (v * N + i) * N + N)
    upper[rows, :] = even + odd
    lower[rows, :] = even - odd


def placed(got, place, group):
    both = jnp.concatenate(
        [got[pl.ds(group, E, stride=BLOCK), :], got[pl.ds(20 + group, E, stride=BLOCK), :]], axis=0
    )
    high, low = split(both)
    moved = dot(place, jnp.concatenate([high, low], axis=1))
    return (moved[:, :E] + moved[:, E:]).T


def unpack_kernel(got, mortar_up, mortar_low, place_out, degree, inner, outer):
    row = iota((E, E), 0)
    sign = odd_sign()
    tags = got[pl.ds(40, E, stride=BLOCK), :].T
    place0 = onehot(row.astype(F32) == tags[0:1, :]).astype(BF16)
    place1 = onehot(row.astype(F32) == tags[2:3, :]).astype(BF16)
    place = jnp.concatenate([place0, place1], axis=1)
    place_out[...] = place
    degrees = jnp.concatenate([tags[1:2, :], tags[3:4, :]], axis=1)
    degrees = jnp.broadcast_to(degrees, (16, 2 * E)).astype(BF16)
    degree[...] = dot_nt(degrees, place)[:8, :]
    for v in range(NV):
        sums = placed(got, place, v)
        inner[64 * v : 64 * v + 64, :] = sums[:64] + sign * sums[64:]
        outer[64 * v : 64 * v + 64, :] = sums[:64] - sign * sums[64:]
    up, low = mortar_up[...].astype(F32), mortar_low[...].astype(F32)
    even = is_even()
    for table, face in ((jnp.where(even, up, low), inner), (jnp.where(even, low, up), outer)):
        face[FACE:PAY, :] = jnp.full((PAY - FACE, E), -1.0, F32)
        face[FACE : FACE + 2, :] = table[:, 0:E]
        face[FACE + 2 : FACE + 4, 0:16] = table[:, E : E + 16]


def unpack_rest(got, place, inner, outer, state):
    pick = place[...]
    half_sign = 0.5 * odd_sign()
    for v in range(NV):
        for n in range(3):
            rows = placed(got, pick, NV + 3 * v + n)
            for m in range(16):
                i, j = divmod(16 * n + m, 6)
                start = v * MODES + 64 * i + 8 * j + 16
                state[start : start + 8, :] = rows[8 * m : 8 * m + 8]
        for i in range(N):
            base = v * MODES + 64 * i
            face = slice(64 * v + 8 * i, 64 * v + 8 * i + 8)
            line = [state[base + 8 * j : base + 8 * j + 8, :] for j in range(2, N)]
            near, far = inner[face, :], outer[face, :]
            state[base : base + 8, :] = 0.5 * (near + far) - (line[0] + line[2] + line[4])
            state[base + 8 : base + 16, :] = half_sign * (near - far) - (line[1] + line[3] + line[5])


def couple_one(d, v, first, k):
    half = (0.5 * k) * d[v]
    if v in (0, 4):
        half = half + 0.5 * d[first]
    if v == first:
        half = half + 0.5 * d[4]
    return half


def couple(d, first, k):
    return [couple_one(d, v, first, k) for v in range(NV)]


def halves_of(plus, minus):
    return [p - m for p, m in zip(plus, minus)], [p + m for p, m in zip(plus, minus)]


def degree_masks(degree):
    k_row = iota((8, E), 0)
    return [onehot(jnp.maximum(k_row, n).astype(F32) <= degree[...]) for n in range(N)]


def lift_weights(metric, stage):
    full = jnp.broadcast_to(metric[1:2, :], (8, E))
    return [full * (-0.5 * BETA[stage] * STEP * (2 * a + 1)) for a in range(N)]


def volume_kernel(stage, *refs):
    alpha, beta = ALPHA[stage], BETA[stage]
    if stage:
        first, before, lifts, *refs, state = refs
    else:
        got, place, *refs = refs
        state = refs.pop(8)
    if stage < 2:
        sums_out = refs.pop(7)
    (degree, inner, outer, metric, near, ztab, out, xsum, zsum, xp, xm, zp, zm, xl, zl, cat, live) = refs
    row = iota((E, E), 0)
    masks = degree_masks(degree)
    if stage == 0:
        unpack_rest(got, place, inner, outer, state)
    for n in range(N):
        live[8 * n : 8 * n + 8, :] = masks[n]
    if stage:
        kq = lift_weights(metric, stage - 1)
        for v in range(NV):
            for i in range(N):
                face = 64 * v + 8 * i
                lift = (lifts[face : face + 8, :], lifts[FACE + face : FACE + face + 8, :])
                for j in range(N):
                    start = v * MODES + 64 * i + 8 * j
                    state[start : start + 8, :] = masks[max(i, j)] * (before[start : start + 8, :] + kq[j] * lift[j % 2])
    gather = []
    for d in range(4):
        pick = onehot(row == near[d : d + 1, :]).astype(BF16)
        gather.append(jnp.concatenate([pick, pick], axis=0))
    for v in range(NV):
        for h in range(2):
            base = v * MODES + 256 * h
            high, low = split(state[base : base + 256, :])
            both = jnp.concatenate([high, low], axis=1)
            count = 320 if v >= 3 else 64
            sums = dot(ztab[0:count, :], both)
            sums = sums[:, :E] + sums[:, E:]
            zp[v * 64 + 32 * h : v * 64 + 32 * h + 32, :] = sums[0:32]
            zm[v * 64 + 32 * h : v * 64 + 32 * h + 32, :] = sums[32:64]
            if v >= 3:
                zsum[(v - 3) * MODES + 256 * h : (v - 3) * MODES + 256 * h + 256, :] = sums[64:]
    for v in range(NV):
        for j in range(N):
            line = [state[v * MODES + 64 * i + 8 * j : v * MODES + 64 * i + 8 * j + 8, :] for i in range(N)]
            even = (line[0] + line[2]) + (line[4] + line[6])
            odd = (line[1] + line[3]) + (line[5] + line[7])
            write_traces(even, odd, xp, xm, v, j)

    def across(face, pick):
        for v in range(NV):
            high, low = split(face[64 * v : 64 * v + 64, :])
            cat[64 * v : 64 * v + 64, 0:E] = high
            cat[64 * v : 64 * v + 64, E : 2 * E] = low
        return dot(cat[...], pick)

    def by_variable(x):
        return [x[64 * v : 64 * v + 64] for v in range(NV)]

    for plus, minus, where, first_v, k_minus, scale, result in (
        (xp, xm, (0, 1), 1, 2.0, 1.0, xl),
        (zp, zm, (2, 3), 3, 1.0, 0.5, zl),
    ):
        d_plus = by_variable(across(minus, gather[where[0]]) - plus[...])
        d_minus = by_variable(across(plus, gather[where[1]]) - minus[...])
        even, odd = halves_of(couple(d_plus, first_v, -1.0), couple(d_minus, first_v, k_minus))
        for v in range(NV):
            result[64 * v : 64 * v + 64, :] = scale * even[v] if scale != 1.0 else even[v]
            result[FACE + 64 * v : FACE + 64 * v + 64, :] = scale * odd[v] if scale != 1.0 else odd[v]

    full = [jnp.broadcast_to(metric[d : d + 1, :], (8, E)) for d in range(3)]
    kx = [full[0] * (-0.5 * beta * STEP * (2 * a + 1)) for a in range(N)]
    ky = [full[1] * (-0.05 * beta * STEP * (2 * a + 1)) for a in range(N)]
    kz = full[2] * (-beta * STEP) * (2 * iota((8, E), 0) + 1).astype(F32)
    odd_k = (iota((8, E), 0) & 1) == 1
    even_device = is_even()

    def at(ref, start):
        return ref[pl.ds(pl.multiple_of(start, 8), 8), :]

    def x_pass(j, carry):
        s = [
            [at(xl, 64 * v + 8 * j) for v in range(NV)],
            [at(xl, FACE + 64 * v + 8 * j) for v in range(NV)],
        ]
        for i in range(N - 1, -1, -1):
            rows = [v * MODES + 64 * i + 8 * j for v in range(NV)]
            now = s[i % 2]
            for v in range(NV):
                xsum[pl.ds(pl.multiple_of(rows[v], 8), 8), :] = kx[i] * now[v]
            if i:
                r, u, y, w, p = [at(state, rows[v]) for v in range(NV)]
                twice = u + u
                f = [r + twice, u + (p + p), y, w, p + twice]
                s[(i + 1) % 2] = [a + b for a, b in zip(s[(i + 1) % 2], f)]
        return carry

    lax.fori_loop(0, N, x_pass, 0)

    def y_pass(i, carry):
        near_in = [-at(inner, 64 * v + 8 * i) for v in range(NV)]
        near_out = [-at(outer, 64 * v + 8 * i) for v in range(NV)]
        d_plus = [jnp.where(even_device, a, b) for a, b in zip(near_in, near_out)]
        d_minus = [jnp.where(even_device, b, a) for a, b in zip(near_in, near_out)]
        even, odd = halves_of(couple(d_plus, 2, -1.0), couple(d_minus, 2, 1.1))
        s = [[10.0 * x for x in even], [10.0 * x for x in odd]]
        z_even = [at(zl, 64 * v + 8 * i) for v in range(NV)]
        z_odd = [at(zl, FACE + 64 * v + 8 * i) for v in range(NV)]
        sums = [[None] * NV, [None] * NV]
        for j in range(N - 1, -1, -1):
            offset = 64 * i + 8 * j
            rows = [v * MODES + offset for v in range(NV)]
            c = [at(state, rows[v]) for v in range(NV)]
            sw, sp = at(zsum, offset), at(zsum, MODES + offset)
            zs = (sw, None, None, sp, sw)
            now = s[j % 2]
            mask = at(live, 8 * jnp.maximum(i, j))
            for v in range(NV):
                lift = jnp.where(
                    odd_k,
                    jnp.broadcast_to(z_odd[v][j : j + 1, :], (8, E)),
                    jnp.broadcast_to(z_even[v][j : j + 1, :], (8, E)),
                )
                if zs[v] is not None:
                    lift = lift + zs[v]
                total = at(xsum, rows[v]) + ky[j] * now[v] + kz * lift
                if alpha:
                    total = total + (alpha * at(first, rows[v]) + beta * c[v])
                else:
                    total = total + c[v]
                total = mask * total
                out[pl.ds(pl.multiple_of(rows[v], 8), 8), :] = total
                held = sums[j % 2]
                held[v] = total if held[v] is None else held[v] + total
            if j:
                r, u, y, w, p = c
                y20 = 20.0 * y
                f = [r + y20, u, y + 20.0 * p, w, p + y20]
                s[(j + 1) % 2] = [a + b for a, b in zip(s[(j + 1) % 2], f)]
        for parity in range(2):
            for v in range(NV if stage < 2 else 0):
                start = FACE * parity + 64 * v + 8 * i
                sums_out[pl.ds(pl.multiple_of(start, 8), 8), :] = sums[parity][v]
        return carry

    lax.fori_loop(0, N, y_pass, 0)


def build_routes(pay, table, inside):
    wide = iota((E, 2 * E), 0).astype(F32)
    pad = jnp.full((1, E - 16), -1.0, F32)

    def own(r):
        return jnp.concatenate([table[r : r + 1, 0:E].astype(F32), table[r : r + 1, E : E + 16].astype(F32), pad], axis=1)

    far_elem = jnp.concatenate([pay[0:1, :], pay[2:3, :]], axis=1)
    far_half = jnp.concatenate([pay[1:2, :], pay[3:4, :]], axis=1)
    own_elem, own_half = own(0), own(1)
    far_pick = jnp.where(wide == far_elem, inside, 0.0)
    own_pick = onehot(wide == own_elem).astype(BF16)
    far_whole, own_whole = onehot(far_half == 0.0), onehot(own_half == 0.0)
    far_1, far_2 = onehot(far_half == 1.0), onehot(far_half == 2.0)
    own_1, own_2 = onehot(own_half == 1.0), onehot(own_half == 2.0)
    weights = (
        far_whole * own_whole,
        own_whole * (far_1 + far_2),
        own_whole * (far_1 - far_2),
        far_whole * (own_1 + own_2),
        far_whole * (own_1 - own_2),
    )
    return [dot_nt((far_pick * w).astype(BF16), own_pick).astype(BF16) for w in weights]


def far_side(first, second, cat, routes):
    even = is_even()
    for v in range(NV):
        rows = slice(64 * v, 64 * v + 64)
        high, low = split(jnp.where(even, first[rows, :], second[rows, :]))
        cat[rows, 0:E] = high
        cat[rows, E : 2 * E] = low
    return dot(cat[...], routes)


def mixed(picked, v):
    lines = [[picked[64 * v + 8 * a : 64 * v + 8 * a + 8, E * n : E * n + E] for a in range(N)] for n in range(5)]
    totals = []
    for a in range(N):
        total = lines[0][a]
        for b in range(a, N):
            total = total + RESTRICT[a][b] * lines[1 + (a + b) % 2][b]
        for b in range(a + 1):
            total = total + PROJECT[a][b] * lines[3 + (a + b) % 2][b]
        totals.append(total)
    return totals


def far_lifts(from_in, from_out, cat_up, cat_low, routes):
    picked_up = far_side(from_in, from_out, cat_up, routes[0 : 2 * E, :])
    picked_low = far_side(from_out, from_in, cat_low, routes[2 * E : 4 * E, :])
    up, low = {}, {}
    for v in (1, 3, 2, 4, 0):
        for n in (2, 4) if v == 2 else (v,):
            if n not in up:
                up[n], low[n] = mixed(picked_up, n), mixed(picked_low, n)
        even, odd = [], []
        for i in range(N):
            plus = couple_one({n: x[i] for n, x in up.items()}, v, 2, -1.0)
            minus = couple_one({n: x[i] for n, x in low.items()}, v, 2, 1.1)
            even.append(plus - minus)
            odd.append(plus + minus)
        yield v, even, odd


def trace_kernel(stage, *refs):
    if stage == 0:
        (sums, from_in, from_out, metric, degree, table_up, table_low, inner, outer, lifts, routes, cat_up, cat_low) = refs
        place = lax.axis_index("sub")
        last = lax.axis_size("sub") - 1
        inside = (jnp.where(place < last, 1.0, 0.0), jnp.where(place > 0, 1.0, 0.0))
        tail = slice(FACE, PAY)
        tail_up = jnp.where(is_even(), from_in[tail, :], from_out[tail, :])
        tail_low = jnp.where(is_even(), from_out[tail, :], from_in[tail, :])
        for side, (pay, table) in enumerate(((tail_up, table_up), (tail_low, table_low))):
            for n, route in enumerate(build_routes(pay, table, inside[side])):
                for part in range(2):
                    start = (side * 2 + part) * E
                    routes[start : start + E, E * n : E * n + E] = route
    else:
        (sums, from_in, from_out, metric, degree, routes, inner, outer, lifts, cat_up, cat_low) = refs
    sign = odd_sign()
    masks = degree_masks(degree)
    kq = lift_weights(metric, stage)
    weights = [[sum(masks[max(i, j)] * kq[j] for j in range(p, N, 2)) for p in range(2)] for i in range(N)]
    for v, lift_even, lift_odd in far_lifts(from_in, from_out, cat_up, cat_low, routes):
        for i in range(N):
            rows = slice(64 * v + 8 * i, 64 * v + 8 * i + 8)
            odd_rows = slice(FACE + 64 * v + 8 * i, FACE + 64 * v + 8 * i + 8)
            lifts[rows, :] = lift_even[i]
            lifts[odd_rows, :] = lift_odd[i]
            even = sums[rows, :] + weights[i][0] * lift_even[i]
            odd = sums[odd_rows, :] + weights[i][1] * lift_odd[i]
            write_traces(even, sign * odd, inner, outer, v, i)


def final_kernel(partial, from_in, from_out, metric, degree, routes, final, cat_up, cat_low, out, sems):
    back = 1.0 / jnp.sqrt((2 * iota((8, E), 0) + 1).astype(F32))
    masks = [m * back for m in degree_masks(degree)]
    kq = lift_weights(metric, 2)
    sent = []
    for v, lift_even, lift_odd in far_lifts(from_in, from_out, cat_up, cat_low, routes):
        for i in range(N):
            for j in range(N):
                start = 64 * i + 8 * j
                lift = (lift_even, lift_odd)[j % 2][i]
                value = partial[v * MODES + start : v * MODES + start + 8, :] + kq[j] * lift
                value = (masks[max(i, j)] * (1.0 / math.sqrt((2 * i + 1) * (2 * j + 1)))) * value
                out[v, start : start + 8, :] = value
            part = pl.ds(64 * i, 64)
            copy = pltpu.make_async_copy(out.at[v, part, :], final.at[v, part, :], sems.at[v * N + i])
            copy.start()
            sent.append(copy)
    for copy in sent:
        copy.wait()


def call(kernel, outs, scratch, args, result=VMEM, cost=None):
    return pl.pallas_call(
        kernel,
        out_shape=outs,
        in_specs=[VMEM] * len(args),
        out_specs=jax.tree.map(lambda _: result, outs),
        scratch_shapes=scratch,
        compiler_params=PARAMS,
        cost_estimate=cost,
    )(*args)


def f32(*shape):
    return jax.ShapeDtypeStruct(shape, F32)


def swap(inner, outer):
    count = lax.axis_size("sub")

    def partner(c, s):
        if s in (0, count - 1):
            return (c ^ 1) * count + s
        return c * count + (s + 1 if s % 2 else s - 1)

    pairs = [(c * count + s, partner(c, s)) for c in range(lax.axis_size("curve")) for s in range(count)]
    far = lax.ppermute(outer, ("curve", "sub"), pairs)
    near = lax.ppermute(inner, "sub", [(s, s ^ 1) for s in range(count)])
    return near, far


def shards(coefficients, old_degree, new_degree, destination, metric, near, mortar_up, mortar_low):
    ztab = jnp.asarray(z_table(), BF16)
    chosen = call(
        setup_kernel,
        (jax.ShapeDtypeStruct((2 * E, 2 * E), BF16), f32(MODES, E), f32(E, E)),
        [],
        (jnp.stack([old_degree, new_degree, destination]),),
        cost=pl.CostEstimate(flops=400_000_000, bytes_accessed=1_000_000, transcendentals=0),
    )
    packed = call(pack_kernel, f32(E * BLOCK, E), [], (coefficients, *chosen))
    packed = packed.reshape(E, 1, BLOCK * E)
    got = lax.all_to_all(packed, ("curve", "sub"), split_axis=0, concat_axis=0, tiled=True)
    got = got.reshape(E * BLOCK, E)
    place, degree, inner, outer = call(
        unpack_kernel,
        (jax.ShapeDtypeStruct((E, 2 * E), BF16), f32(8, E), f32(PAY, E), f32(PAY, E)),
        [],
        (got, mortar_up, mortar_low),
    )
    faces = (f32(FACE, E), f32(FACE, E))
    cats = [pltpu.VMEM((FACE, 2 * E), BF16)] * 2
    for stage in range(3):
        from_in, from_out = swap(inner, outer)
        given = (got, place) if stage == 0 else (first, partial, lifts)
        partial, *sums = call(
            functools.partial(volume_kernel, stage),
            (f32(ROWS, E), f32(2 * FACE, E), f32(ROWS, E))[: 3 - stage],
            [pltpu.VMEM((ROWS, E), F32), pltpu.VMEM((2 * MODES, E), F32)]
            + [pltpu.VMEM((FACE, E), F32)] * 4
            + [pltpu.VMEM((2 * FACE, E), F32)] * 2
            + [pltpu.VMEM((FACE, 2 * E), BF16), pltpu.VMEM((8 * N, E), F32)]
            + ([pltpu.VMEM((ROWS, E), F32)] if stage else []),
            given + (degree, inner, outer, metric, near, ztab),
        )
        if stage == 0:
            first = sums.pop()
        body = functools.partial(trace_kernel, stage)
        outs = faces + (f32(2 * FACE, E),)
        if stage == 0:
            inner, outer, lifts, routes = call(
                body,
                outs + (jax.ShapeDtypeStruct((4 * E, 5 * E), BF16),),
                cats,
                (*sums, from_in, from_out, metric, degree, mortar_up, mortar_low),
            )
        elif stage == 1:
            inner, outer, lifts = call(body, outs, cats, (*sums, from_in, from_out, metric, degree, routes))
        else:
            scratch = cats + [pltpu.VMEM((NV, MODES, E), F32), pltpu.SemaphoreType.DMA((NV * N,))]
            args = (partial, from_in, from_out, metric, degree, routes)
            return call(final_kernel, f32(NV, MODES, E), scratch, args, result=HBM)


def solution(mesh):
    lanes = P(None, ("curve", "sub"))
    rank = P(("curve", "sub"))
    cube = P(None, None, ("curve", "sub"))
    return jax.shard_map(
        shards,
        mesh=mesh,
        in_specs=(cube, rank, rank, rank, lanes, lanes, lanes, lanes),
        out_specs=cube,
        check_vma=False,
    )
```

```python
import functools
import math

import jax
import jax.numpy as jnp
import numpy as np
from jax import lax
from jax.experimental import pallas as pl
from jax.experimental.pallas import tpu as pltpu
from jax.sharding import PartitionSpec as P

NV = 5
N = 8
MODES = N * N * N
ROWS = NV * MODES
FACE = NV * N * N
E = 128
BLOCK = 41
STEP = 0.006
ALPHA = (0.0, 0.75, 1.0 / 3.0)
BETA = (1.0, 0.25, 2.0 / 3.0)
PAY = FACE + 8
LIMIT = 24 * 1024 * 1024
F32 = jnp.float32
BF16 = jnp.bfloat16

VMEM = pl.BlockSpec(memory_space=pltpu.VMEM)
HBM = pl.BlockSpec(memory_space=pltpu.HBM)
PARAMS = pltpu.CompilerParams(vmem_limit_bytes=LIMIT)


def legendre_pair(degree_n, points):
    points = np.asarray(points) + 0.0
    value_before = points * 0.0
    value_now = points * 0.0 + 1.0
    for order in range(1, degree_n + 1):
        value_next = ((2 * order - 1) * points * value_now - (order - 1) * value_before) / order
        value_before = value_now
        value_now = value_next
    return (value_now, value_before)


def half_table():
    nodes, weights = np.polynomial.legendre.leggauss(2 * N + 2)
    table = np.zeros((N, N))
    for a in range(N):
        for b in range(a, N):
            fa = math.sqrt((2 * a + 1) / 2.0) * legendre_pair(a, nodes)[0]
            fb = math.sqrt((2 * b + 1) / 2.0) * legendre_pair(b, (nodes - 1.0) / 2.0)[0]
            table[a, b] = np.sum(weights * fa * fb)
    return table


HALF = half_table()
RESTRICT = [[float(HALF[a, b] * math.sqrt((2 * a + 1) / (2 * b + 1))) for b in range(N)] for a in range(N)]
PROJECT = [[float(0.5 * HALF[a, b] * math.sqrt((2 * b + 1) / (2 * a + 1))) for a in range(N)] for b in range(N)]


def z_table():
    out = np.zeros((320, 256))
    for col in range(256):
        line, k = divmod(col, N)
        out[line, col] = 1.0
        out[32 + line, col] = (-1.0) ** k
        for a in range(k):
            if (k - a) % 2 == 1:
                out[64 + line * N + a, col] = 1.0
    return out


def iota(shape, axis):
    return lax.broadcasted_iota(jnp.int32, shape, axis)


def split(x):
    high = x.astype(BF16)
    return high, (x - high.astype(F32)).astype(BF16)


def dot(a, b):
    return lax.dot_general(a, b, (((1,), (0,)), ((), ())), preferred_element_type=F32)


def dot_nt(a, b):
    return lax.dot_general(a, b, (((1,), (1,)), ((), ())), preferred_element_type=F32)


def onehot(flag):
    return jnp.where(flag, 1.0, 0.0)


def setup_kernel(index, pick, weights, tags_out):
    row = iota((E, E), 0)
    col = iota((E, E), 1)
    old, new_row, dest = index[0:1, :], index[1:2, :], index[2:3, :]
    kept = jnp.minimum(old, new_row)
    target = lax.shift_right_logical(dest, 7)
    slot = dest & (E - 1)
    target_f = jnp.broadcast_to(target.astype(F32), (E, E))
    same = target_f == target_f.T
    rank = jnp.sum(onehot(same & (row < col)), axis=0, keepdims=True)
    here = jnp.broadcast_to(target, (E, E)) == row
    pick0 = onehot(here & (rank < 0.5)).astype(BF16)
    pick1 = onehot(here & (rank > 0.5)).astype(BF16)
    slot_f = jnp.broadcast_to((slot - E).astype(F32), (E, E))
    new_f = jnp.broadcast_to(new_row.astype(F32), (E, E))
    tags0 = jnp.where(row == 0, slot_f, jnp.where(row == 1, new_f, 0.0)).astype(BF16)
    tags1 = jnp.where(row == 2, slot_f, jnp.where(row == 3, new_f, 0.0)).astype(BF16)
    tags = dot_nt(pick0, tags0) + dot_nt(pick1, tags1)
    tags_out[...] = tags + jnp.where((col == 0) | (col == 2), float(E), 0.0)
    half = jnp.concatenate([pick0, pick1], axis=0)
    pick[...] = jnp.concatenate([half, half], axis=1)
    for q in range(4):
        mode = row + E * q
        i = lax.shift_right_logical(mode, 6)
        j = lax.shift_right_logical(mode, 3) & 7
        k = mode & 7
        live = jnp.maximum(jnp.maximum(i, j), k) <= kept
        weight = ((2 * i + 1) * (2 * j + 1) * (2 * k + 1)).astype(F32)
        weights[E * q : E * (q + 1), :] = jnp.where(live, jnp.sqrt(weight), 0.0)


def pack_kernel(coef, pick, weights, tags, out):
    out[pl.ds(40, E, stride=BLOCK), :] = tags[...]

    def send(group_a, group_b, rows):
        high, low = split(rows)
        moved = dot_nt(pick[...], jnp.concatenate([high, low], axis=1))
        for n, group in enumerate((group_a, group_b)):
            out[pl.ds(group, E, stride=BLOCK), :] = moved[:E, E * n : E * n + E]
            out[pl.ds(20 + group, E, stride=BLOCK), :] = moved[E:, E * n : E * n + E]

    for v in range(NV):
        x = (coef[v] * weights[...]).reshape(N, N, N, E)
        sums = [(x[:, p] + x[:, p + 2]) + (x[:, p + 4] + x[:, p + 6]) for p in range(2)]
        sums = [part.reshape(64, E) for part in sums]
        rest = x[:, 2:].reshape(3 * E, E)
        base = NV + 3 * v
        send(v, base, jnp.concatenate(sums + [rest[:E]], axis=0))
        send(base + 1, base + 2, rest[E:])


def is_even():
    return (lax.axis_index("sub") & 1) == 0


def odd_sign():
    return jnp.where(is_even(), 1.0, -1.0)


def write_traces(even, odd, upper, lower, v, i):
    rows = slice((v * N + i) * N, (v * N + i) * N + N)
    upper[rows, :] = even + odd
    lower[rows, :] = even - odd


def placed(got, place, group):
    both = jnp.concatenate(
        [got[pl.ds(group, E, stride=BLOCK), :], got[pl.ds(20 + group, E, stride=BLOCK), :]], axis=0
    )
    high, low = split(both)
    moved = dot(place, jnp.concatenate([high, low], axis=1))
    return (moved[:, :E] + moved[:, E:]).T


def unpack_kernel(got, mortar_up, mortar_low, place_out, degree, inner, outer):
    row = iota((E, E), 0)
    sign = odd_sign()
    tags = got[pl.ds(40, E, stride=BLOCK), :].T
    place0 = onehot(row.astype(F32) == tags[0:1, :]).astype(BF16)
    place1 = onehot(row.astype(F32) == tags[2:3, :]).astype(BF16)
    place = jnp.concatenate([place0, place1], axis=1)
    place_out[...] = place
    degrees = jnp.concatenate([tags[1:2, :], tags[3:4, :]], axis=1)
    degrees = jnp.broadcast_to(degrees, (16, 2 * E)).astype(BF16)
    degree[...] = dot_nt(degrees, place)[:8, :]
    for v in range(NV):
        sums = placed(got, place, v)
        inner[64 * v : 64 * v + 64, :] = sums[:64] + sign * sums[64:]
        outer[64 * v : 64 * v + 64, :] = sums[:64] - sign * sums[64:]
    up, low = mortar_up[...].astype(F32), mortar_low[...].astype(F32)
    even = is_even()
    for table, face in ((jnp.where(even, up, low), inner), (jnp.where(even, low, up), outer)):
        face[FACE:PAY, :] = jnp.full((PAY - FACE, E), -1.0, F32)
        face[FACE : FACE + 2, :] = table[:, 0:E]
        face[FACE + 2 : FACE + 4, 0:16] = table[:, E : E + 16]


def unpack_rest(got, place, inner, outer, state):
    pick = place[...]
    half_sign = 0.5 * odd_sign()
    for v in range(NV):
        for n in range(3):
            rows = placed(got, pick, NV + 3 * v + n)
            for m in range(16):
                i, j = divmod(16 * n + m, 6)
                start = v * MODES + 64 * i + 8 * j + 16
                state[start : start + 8, :] = rows[8 * m : 8 * m + 8]
        for i in range(N):
            base = v * MODES + 64 * i
            face = slice(64 * v + 8 * i, 64 * v + 8 * i + 8)
            line = [state[base + 8 * j : base + 8 * j + 8, :] for j in range(2, N)]
            near, far = inner[face, :], outer[face, :]
            state[base : base + 8, :] = 0.5 * (near + far) - (line[0] + line[2] + line[4])
            state[base + 8 : base + 16, :] = half_sign * (near - far) - (line[1] + line[3] + line[5])


def couple_one(d, v, first, k):
    half = (0.5 * k) * d[v]
    if v in (0, 4):
        half = half + 0.5 * d[first]
    if v == first:
        half = half + 0.5 * d[4]
    return half


def couple(d, first, k):
    return [couple_one(d, v, first, k) for v in range(NV)]


def halves_of(plus, minus):
    return [p - m for p, m in zip(plus, minus)], [p + m for p, m in zip(plus, minus)]


def degree_masks(degree):
    k_row = iota((8, E), 0)
    return [onehot(jnp.maximum(k_row, n).astype(F32) <= degree[...]) for n in range(N)]


def lift_weights(metric, stage):
    full = jnp.broadcast_to(metric[1:2, :], (8, E))
    return [full * (-0.5 * BETA[stage] * STEP * (2 * a + 1)) for a in range(N)]


def volume_kernel(stage, *refs):
    alpha, beta = ALPHA[stage], BETA[stage]
    if stage:
        first, before, lifts, *refs, state = refs
    else:
        got, place, *refs = refs
        state = refs.pop(8)
    if stage < 2:
        sums_out = refs.pop(7)
    (degree, inner, outer, metric, near, ztab, out, xsum, zsum, xp, xm, zp, zm, xl, zl, cat, live) = refs
    row = iota((E, E), 0)
    masks = degree_masks(degree)
    if stage == 0:
        unpack_rest(got, place, inner, outer, state)
    for n in range(N):
        live[8 * n : 8 * n + 8, :] = masks[n]
    if stage:
        kq = lift_weights(metric, stage - 1)
        for v in range(NV):
            for i in range(N):
                face = 64 * v + 8 * i
                lift = (lifts[face : face + 8, :], lifts[FACE + face : FACE + face + 8, :])
                for j in range(N):
                    start = v * MODES + 64 * i + 8 * j
                    state[start : start + 8, :] = masks[max(i, j)] * (before[start : start + 8, :] + kq[j] * lift[j % 2])
    gather = []
    for d in range(4):
        pick = onehot(row == near[d : d + 1, :]).astype(BF16)
        gather.append(jnp.concatenate([pick, pick], axis=0))
    for v in range(NV):
        for h in range(2):
            base = v * MODES + 256 * h
            high, low = split(state[base : base + 256, :])
            both = jnp.concatenate([high, low], axis=1)
            count = 320 if v >= 3 else 64
            sums = dot(ztab[0:count, :], both)
            sums = sums[:, :E] + sums[:, E:]
            zp[v * 64 + 32 * h : v * 64 + 32 * h + 32, :] = sums[0:32]
            zm[v * 64 + 32 * h : v * 64 + 32 * h + 32, :] = sums[32:64]
            if v >= 3:
                zsum[(v - 3) * MODES + 256 * h : (v - 3) * MODES + 256 * h + 256, :] = sums[64:]
    for v in range(NV):
        for j in range(N):
            line = [state[v * MODES + 64 * i + 8 * j : v * MODES + 64 * i + 8 * j + 8, :] for i in range(N)]
            even = (line[0] + line[2]) + (line[4] + line[6])
            odd = (line[1] + line[3]) + (line[5] + line[7])
            write_traces(even, odd, xp, xm, v, j)

    def across(face, pick):
        for v in range(NV):
            high, low = split(face[64 * v : 64 * v + 64, :])
            cat[64 * v : 64 * v + 64, 0:E] = high
            cat[64 * v : 64 * v + 64, E : 2 * E] = low
        return dot(cat[...], pick)

    def by_variable(x):
        return [x[64 * v : 64 * v + 64] for v in range(NV)]

    for plus, minus, where, first_v, k_minus, scale, result in (
        (xp, xm, (0, 1), 1, 2.0, 1.0, xl),
        (zp, zm, (2, 3), 3, 1.0, 0.5, zl),
    ):
        d_plus = by_variable(across(minus, gather[where[0]]) - plus[...])
        d_minus = by_variable(across(plus, gather[where[1]]) - minus[...])
        even, odd = halves_of(couple(d_plus, first_v, -1.0), couple(d_minus, first_v, k_minus))
        for v in range(NV):
            result[64 * v : 64 * v + 64, :] = scale * even[v] if scale != 1.0 else even[v]
            result[FACE + 64 * v : FACE + 64 * v + 64, :] = scale * odd[v] if scale != 1.0 else odd[v]

    full = [jnp.broadcast_to(metric[d : d + 1, :], (8, E)) for d in range(3)]
    kx = [full[0] * (-0.5 * beta * STEP * (2 * a + 1)) for a in range(N)]
    ky = [full[1] * (-0.05 * beta * STEP * (2 * a + 1)) for a in range(N)]
    kz = full[2] * (-beta * STEP) * (2 * iota((8, E), 0) + 1).astype(F32)
    odd_k = (iota((8, E), 0) & 1) == 1
    even_device = is_even()

    def at(ref, start):
        return ref[pl.ds(pl.multiple_of(start, 8), 8), :]

    def x_pass(j, carry):
        s = [
            [at(xl, 64 * v + 8 * j) for v in range(NV)],
            [at(xl, FACE + 64 * v + 8 * j) for v in range(NV)],
        ]
        for i in range(N - 1, -1, -1):
            rows = [v * MODES + 64 * i + 8 * j for v in range(NV)]
            now = s[i % 2]
            for v in range(NV):
                xsum[pl.ds(pl.multiple_of(rows[v], 8), 8), :] = kx[i] * now[v]
            if i:
                r, u, y, w, p = [at(state, rows[v]) for v in range(NV)]
                twice = u + u
                f = [r + twice, u + (p + p), y, w, p + twice]
                s[(i + 1) % 2] = [a + b for a, b in zip(s[(i + 1) % 2], f)]
        return carry

    lax.fori_loop(0, N, x_pass, 0)

    def y_pass(i, carry):
        near_in = [-at(inner, 64 * v + 8 * i) for v in range(NV)]
        near_out = [-at(outer, 64 * v + 8 * i) for v in range(NV)]
        d_plus = [jnp.where(even_device, a, b) for a, b in zip(near_in, near_out)]
        d_minus = [jnp.where(even_device, b, a) for a, b in zip(near_in, near_out)]
        even, odd = halves_of(couple(d_plus, 2, -1.0), couple(d_minus, 2, 1.1))
        s = [[10.0 * x for x in even], [10.0 * x for x in odd]]
        z_even = [at(zl, 64 * v + 8 * i) for v in range(NV)]
        z_odd = [at(zl, FACE + 64 * v + 8 * i) for v in range(NV)]
        sums = [[None] * NV, [None] * NV]
        for j in range(N - 1, -1, -1):
            offset = 64 * i + 8 * j
            rows = [v * MODES + offset for v in range(NV)]
            c = [at(state, rows[v]) for v in range(NV)]
            sw, sp = at(zsum, offset), at(zsum, MODES + offset)
            zs = (sw, None, None, sp, sw)
            now = s[j % 2]
            mask = at(live, 8 * jnp.maximum(i, j))
            for v in range(NV):
                lift = jnp.where(
                    odd_k,
                    jnp.broadcast_to(z_odd[v][j : j + 1, :], (8, E)),
                    jnp.broadcast_to(z_even[v][j : j + 1, :], (8, E)),
                )
                if zs[v] is not None:
                    lift = lift + zs[v]
                total = at(xsum, rows[v]) + ky[j] * now[v] + kz * lift
                if alpha:
                    total = total + (alpha * at(first, rows[v]) + beta * c[v])
                else:
                    total = total + c[v]
                total = mask * total
                out[pl.ds(pl.multiple_of(rows[v], 8), 8), :] = total
                held = sums[j % 2]
                held[v] = total if held[v] is None else held[v] + total
            if j:
                r, u, y, w, p = c
                y20 = 20.0 * y
                f = [r + y20, u, y + 20.0 * p, w, p + y20]
                s[(j + 1) % 2] = [a + b for a, b in zip(s[(j + 1) % 2], f)]
        for parity in range(2):
            for v in range(NV if stage < 2 else 0):
                start = FACE * parity + 64 * v + 8 * i
                sums_out[pl.ds(pl.multiple_of(start, 8), 8), :] = sums[parity][v]
        return carry

    lax.fori_loop(0, N, y_pass, 0)


def build_routes(pay, table, inside):
    wide = iota((E, 2 * E), 0).astype(F32)
    pad = jnp.full((1, E - 16), -1.0, F32)

    def own(r):
        return jnp.concatenate([table[r : r + 1, 0:E].astype(F32), table[r : r + 1, E : E + 16].astype(F32), pad], axis=1)

    far_elem = jnp.concatenate([pay[0:1, :], pay[2:3, :]], axis=1)
    far_half = jnp.concatenate([pay[1:2, :], pay[3:4, :]], axis=1)
    own_elem, own_half = own(0), own(1)
    far_pick = jnp.where(wide == far_elem, inside, 0.0)
    own_pick = onehot(wide == own_elem)
    far_1, far_2 = onehot(far_half == 1.0), onehot(far_half == 2.0)
    own_1, own_2 = onehot(own_half == 1.0), onehot(own_half == 2.0)
    far_kinds = [(far_pick * w).astype(BF16) for w in (onehot(far_half == 0.0), far_1 + far_2, far_1 - far_2)]
    own_kinds = [(own_pick * w).astype(BF16) for w in (onehot(own_half == 0.0), own_1 + own_2, own_1 - own_2)]
    whole = dot_nt(jnp.concatenate(far_kinds, axis=0), own_kinds[0]).astype(BF16)
    halves = dot_nt(far_kinds[0], jnp.concatenate(own_kinds[1:], axis=0)).astype(BF16)
    return [whole[E * n : E * n + E] for n in range(3)] + [halves[:, E * n : E * n + E] for n in range(2)]


def far_side(first, second, cat, routes):
    even = is_even()
    for v in range(NV):
        rows = slice(64 * v, 64 * v + 64)
        high, low = split(jnp.where(even, first[rows, :], second[rows, :]))
        cat[rows, 0:E] = high
        cat[rows, E : 2 * E] = low
    return dot(cat[...], routes)


def mixed(picked, v):
    lines = [[picked[64 * v + 8 * a : 64 * v + 8 * a + 8, E * n : E * n + E] for a in range(N)] for n in range(5)]
    totals = []
    for a in range(N):
        total = lines[0][a]
        for b in range(a, N):
            total = total + RESTRICT[a][b] * lines[1 + (a + b) % 2][b]
        for b in range(a + 1):
            total = total + PROJECT[a][b] * lines[3 + (a + b) % 2][b]
        totals.append(total)
    return totals


def far_lifts(from_in, from_out, cat_up, cat_low, routes):
    picked_up = far_side(from_in, from_out, cat_up, routes[0 : 2 * E, :])
    picked_low = far_side(from_out, from_in, cat_low, routes[2 * E : 4 * E, :])
    up, low = {}, {}
    for v in (1, 3, 2, 4, 0):
        for n in (2, 4) if v == 2 else (v,):
            if n not in up:
                up[n], low[n] = mixed(picked_up, n), mixed(picked_low, n)
        even, odd = [], []
        for i in range(N):
            plus = couple_one({n: x[i] for n, x in up.items()}, v, 2, -1.0)
            minus = couple_one({n: x[i] for n, x in low.items()}, v, 2, 1.1)
            even.append(plus - minus)
            odd.append(plus + minus)
        yield v, even, odd


def trace_kernel(stage, *refs):
    if stage == 0:
        (sums, from_in, from_out, metric, degree, table_up, table_low, inner, outer, lifts, routes, cat_up, cat_low) = refs
        place = lax.axis_index("sub")
        last = lax.axis_size("sub") - 1
        inside = (jnp.where(place < last, 1.0, 0.0), jnp.where(place > 0, 1.0, 0.0))
        tail = slice(FACE, PAY)
        tail_up = jnp.where(is_even(), from_in[tail, :], from_out[tail, :])
        tail_low = jnp.where(is_even(), from_out[tail, :], from_in[tail, :])
        for side, (pay, table) in enumerate(((tail_up, table_up), (tail_low, table_low))):
            for n, route in enumerate(build_routes(pay, table, inside[side])):
                for part in range(2):
                    start = (side * 2 + part) * E
                    routes[start : start + E, E * n : E * n + E] = route
    else:
        (sums, from_in, from_out, metric, degree, routes, inner, outer, lifts, cat_up, cat_low) = refs
    sign = odd_sign()
    masks = degree_masks(degree)
    kq = lift_weights(metric, stage)
    weights = [[sum(masks[max(i, j)] * kq[j] for j in range(p, N, 2)) for p in range(2)] for i in range(N)]
    for v, lift_even, lift_odd in far_lifts(from_in, from_out, cat_up, cat_low, routes):
        for i in range(N):
            rows = slice(64 * v + 8 * i, 64 * v + 8 * i + 8)
            odd_rows = slice(FACE + 64 * v + 8 * i, FACE + 64 * v + 8 * i + 8)
            lifts[rows, :] = lift_even[i]
            lifts[odd_rows, :] = lift_odd[i]
            even = sums[rows, :] + weights[i][0] * lift_even[i]
            odd = sums[odd_rows, :] + weights[i][1] * lift_odd[i]
            write_traces(even, sign * odd, inner, outer, v, i)


def final_kernel(partial, from_in, from_out, metric, degree, routes, final, cat_up, cat_low, out, sems):
    back = 1.0 / jnp.sqrt((2 * iota((8, E), 0) + 1).astype(F32))
    masks = [m * back for m in degree_masks(degree)]
    kq = lift_weights(metric, 2)
    scales = [[masks[max(i, j)] * (1.0 / math.sqrt((2 * i + 1) * (2 * j + 1))) for j in range(N)] for i in range(N)]
    sent = []
    for v, lift_even, lift_odd in far_lifts(from_in, from_out, cat_up, cat_low, routes):
        for i in range(N):
            for j in range(N):
                start = 64 * i + 8 * j
                lift = (lift_even, lift_odd)[j % 2][i]
                value = partial[v * MODES + start : v * MODES + start + 8, :] + kq[j] * lift
                value = scales[i][j] * value
                out[v, start : start + 8, :] = value
            part = pl.ds(64 * i, 64)
            copy = pltpu.make_async_copy(out.at[v, part, :], final.at[v, part, :], sems.at[v * N + i])
            copy.start()
            sent.append(copy)
    for copy in sent:
        copy.wait()


def call(kernel, outs, scratch, args, result=VMEM, cost=None):
    return pl.pallas_call(
        kernel,
        out_shape=outs,
        in_specs=[VMEM] * len(args),
        out_specs=jax.tree.map(lambda _: result, outs),
        scratch_shapes=scratch,
        compiler_params=PARAMS,
        cost_estimate=cost,
    )(*args)


def f32(*shape):
    return jax.ShapeDtypeStruct(shape, F32)


def swap(inner, outer):
    count = lax.axis_size("sub")

    def partner(c, s):
        if s in (0, count - 1):
            return (c ^ 1) * count + s
        return c * count + (s + 1 if s % 2 else s - 1)

    pairs = [(c * count + s, partner(c, s)) for c in range(lax.axis_size("curve")) for s in range(count)]
    near = lax.ppermute(inner, "sub", [(s, s ^ 1) for s in range(count)])
    far = lax.ppermute(outer, ("curve", "sub"), pairs)
    return near, far


def shards(coefficients, old_degree, new_degree, destination, metric, near, mortar_up, mortar_low):
    ztab = jnp.asarray(z_table(), BF16)
    chosen = call(
        setup_kernel,
        (jax.ShapeDtypeStruct((2 * E, 2 * E), BF16), f32(MODES, E), f32(E, E)),
        [],
        (jnp.stack([old_degree, new_degree, destination]),),
        cost=pl.CostEstimate(flops=400_000_000, bytes_accessed=1_000_000, transcendentals=0),
    )
    packed = call(pack_kernel, f32(E * BLOCK, E), [], (coefficients, *chosen))
    packed = packed.reshape(E, 1, BLOCK * E)
    got = lax.all_to_all(packed, ("curve", "sub"), split_axis=0, concat_axis=0, tiled=True)
    got = got.reshape(E * BLOCK, E)
    place, degree, inner, outer = call(
        unpack_kernel,
        (jax.ShapeDtypeStruct((E, 2 * E), BF16), f32(8, E), f32(PAY, E), f32(PAY, E)),
        [],
        (got, mortar_up, mortar_low),
    )
    faces = (f32(FACE, E), f32(FACE, E))
    cats = [pltpu.VMEM((FACE, 2 * E), BF16)] * 2
    for stage in range(3):
        from_in, from_out = swap(inner, outer)
        given = (got, place) if stage == 0 else (first, partial, lifts)
        partial, *sums = call(
            functools.partial(volume_kernel, stage),
            (f32(ROWS, E), f32(2 * FACE, E), f32(ROWS, E))[: 3 - stage],
            [pltpu.VMEM((ROWS, E), F32), pltpu.VMEM((2 * MODES, E), F32)]
            + [pltpu.VMEM((FACE, E), F32)] * 4
            + [pltpu.VMEM((2 * FACE, E), F32)] * 2
            + [pltpu.VMEM((FACE, 2 * E), BF16), pltpu.VMEM((8 * N, E), F32)]
            + ([pltpu.VMEM((ROWS, E), F32)] if stage else []),
            given + (degree, inner, outer, metric, near, ztab),
        )
        if stage == 0:
            first = sums.pop()
        body = functools.partial(trace_kernel, stage)
        outs = faces + (f32(2 * FACE, E),)
        if stage == 0:
            inner, outer, lifts, routes = call(
                body,
                outs + (jax.ShapeDtypeStruct((4 * E, 5 * E), BF16),),
                cats,
                (*sums, from_in, from_out, metric, degree, mortar_up, mortar_low),
            )
        elif stage == 1:
            inner, outer, lifts = call(body, outs, cats, (*sums, from_in, from_out, metric, degree, routes))
        else:
            scratch = cats + [pltpu.VMEM((NV, MODES, E), F32), pltpu.SemaphoreType.DMA((NV * N,))]
            args = (partial, from_in, from_out, metric, degree, routes)
            return call(final_kernel, f32(NV, MODES, E), scratch, args, result=HBM)


def solution(mesh):
    lanes = P(None, ("curve", "sub"))
    rank = P(("curve", "sub"))
    cube = P(None, None, ("curve", "sub"))
    return jax.shard_map(
        shards,
        mesh=mesh,
        in_specs=(cube, rank, rank, rank, lanes, lanes, lanes, lanes),
        out_specs=cube,
        check_vma=False,
    )
```

```python
import functools
import math

import jax
import jax.numpy as jnp
import numpy as np
from jax import lax
from jax.experimental import pallas as pl
from jax.experimental.pallas import tpu as pltpu
from jax.sharding import PartitionSpec as P

NV = 5
N = 8
MODES = N * N * N
ROWS = NV * MODES
FACE = NV * N * N
E = 128
BLOCK = 41
STEP = 0.006
ALPHA = (0.0, 0.75, 1.0 / 3.0)
BETA = (1.0, 0.25, 2.0 / 3.0)
PAY = FACE + 8
LIMIT = 24 * 1024 * 1024
F32 = jnp.float32
BF16 = jnp.bfloat16

VMEM = pl.BlockSpec(memory_space=pltpu.VMEM)
HBM = pl.BlockSpec(memory_space=pltpu.HBM)
PARAMS = pltpu.CompilerParams(vmem_limit_bytes=LIMIT)


def legendre_pair(degree_n, points):
    points = np.asarray(points) + 0.0
    value_before = points * 0.0
    value_now = points * 0.0 + 1.0
    for order in range(1, degree_n + 1):
        value_next = ((2 * order - 1) * points * value_now - (order - 1) * value_before) / order
        value_before = value_now
        value_now = value_next
    return (value_now, value_before)


def half_table():
    nodes, weights = np.polynomial.legendre.leggauss(2 * N + 2)
    table = np.zeros((N, N))
    for a in range(N):
        for b in range(a, N):
            fa = math.sqrt((2 * a + 1) / 2.0) * legendre_pair(a, nodes)[0]
            fb = math.sqrt((2 * b + 1) / 2.0) * legendre_pair(b, (nodes - 1.0) / 2.0)[0]
            table[a, b] = np.sum(weights * fa * fb)
    return table


HALF = half_table()
RESTRICT = [[float(HALF[a, b] * math.sqrt((2 * a + 1) / (2 * b + 1))) for b in range(N)] for a in range(N)]
PROJECT = [[float(0.5 * HALF[a, b] * math.sqrt((2 * b + 1) / (2 * a + 1))) for a in range(N)] for b in range(N)]


def z_table():
    out = np.zeros((320, 256))
    for col in range(256):
        line, k = divmod(col, N)
        out[line, col] = 1.0
        out[32 + line, col] = (-1.0) ** k
        for a in range(k):
            if (k - a) % 2 == 1:
                out[64 + line * N + a, col] = 1.0
    return out


def iota(shape, axis):
    return lax.broadcasted_iota(jnp.int32, shape, axis)


def split(x):
    high = x.astype(BF16)
    return high, (x - high.astype(F32)).astype(BF16)


def dot(a, b):
    return lax.dot_general(a, b, (((1,), (0,)), ((), ())), preferred_element_type=F32)


def dot_nt(a, b):
    return lax.dot_general(a, b, (((1,), (1,)), ((), ())), preferred_element_type=F32)


def onehot(flag):
    return jnp.where(flag, 1.0, 0.0)


def setup_kernel(index, pick, weights, tags_out):
    row = iota((E, E), 0)
    col = iota((E, E), 1)
    old, new_row, dest = index[0:1, :], index[1:2, :], index[2:3, :]
    kept = jnp.minimum(old, new_row)
    target = lax.shift_right_logical(dest, 7)
    slot = dest & (E - 1)
    target_f = jnp.broadcast_to(target.astype(F32), (E, E))
    same = target_f == target_f.T
    rank = jnp.sum(onehot(same & (row < col)), axis=0, keepdims=True)
    here = jnp.broadcast_to(target, (E, E)) == row
    pick0 = onehot(here & (rank < 0.5)).astype(BF16)
    pick1 = onehot(here & (rank > 0.5)).astype(BF16)
    slot_f = jnp.broadcast_to((slot - E).astype(F32), (E, E))
    new_f = jnp.broadcast_to(new_row.astype(F32), (E, E))
    tags0 = jnp.where(row == 0, slot_f, jnp.where(row == 1, new_f, 0.0)).astype(BF16)
    tags1 = jnp.where(row == 2, slot_f, jnp.where(row == 3, new_f, 0.0)).astype(BF16)
    tags = dot_nt(pick0, tags0) + dot_nt(pick1, tags1)
    tags_out[...] = tags + jnp.where((col == 0) | (col == 2), float(E), 0.0)
    half = jnp.concatenate([pick0, pick1], axis=0)
    pick[...] = jnp.concatenate([half, half], axis=1)
    for q in range(4):
        mode = row + E * q
        i = lax.shift_right_logical(mode, 6)
        j = lax.shift_right_logical(mode, 3) & 7
        k = mode & 7
        live = jnp.maximum(jnp.maximum(i, j), k) <= kept
        weight = ((2 * i + 1) * (2 * j + 1) * (2 * k + 1)).astype(F32)
        weights[E * q : E * (q + 1), :] = jnp.where(live, jnp.sqrt(weight), 0.0)


def pack_kernel(coef, pick, weights, tags, out):
    out[pl.ds(40, E, stride=BLOCK), :] = tags[...]

    def send(group_a, group_b, rows):
        high, low = split(rows)
        moved = dot_nt(pick[...], jnp.concatenate([high, low], axis=1))
        for n, group in enumerate((group_a, group_b)):
            out[pl.ds(group, E, stride=BLOCK), :] = moved[:E, E * n : E * n + E]
            out[pl.ds(20 + group, E, stride=BLOCK), :] = moved[E:, E * n : E * n + E]

    for v in range(NV):
        x = (coef[v] * weights[...]).reshape(N, N, N, E)
        sums = [(x[:, p] + x[:, p + 2]) + (x[:, p + 4] + x[:, p + 6]) for p in range(2)]
        sums = [part.reshape(64, E) for part in sums]
        rest = x[:, 2:].reshape(3 * E, E)
        base = NV + 3 * v
        send(v, base, jnp.concatenate(sums + [rest[:E]], axis=0))
        send(base + 1, base + 2, rest[E:])


def is_even():
    return (lax.axis_index("sub") & 1) == 0


def odd_sign():
    return jnp.where(is_even(), 1.0, -1.0)


def write_traces(even, odd, upper, lower, v, i):
    rows = slice((v * N + i) * N, (v * N + i) * N + N)
    upper[rows, :] = even + odd
    lower[rows, :] = even - odd


def placed(got, place, group):
    both = jnp.concatenate(
        [got[pl.ds(group, E, stride=BLOCK), :], got[pl.ds(20 + group, E, stride=BLOCK), :]], axis=0
    )
    high, low = split(both)
    moved = dot(place, jnp.concatenate([high, low], axis=1))
    return (moved[:, :E] + moved[:, E:]).T


def unpack_kernel(got, mortar_up, mortar_low, place_out, degree, inner, outer):
    row = iota((E, E), 0)
    sign = odd_sign()
    tags = got[pl.ds(40, E, stride=BLOCK), :].T
    place0 = onehot(row.astype(F32) == tags[0:1, :]).astype(BF16)
    place1 = onehot(row.astype(F32) == tags[2:3, :]).astype(BF16)
    place = jnp.concatenate([place0, place1], axis=1)
    place_out[...] = place
    degrees = jnp.concatenate([tags[1:2, :], tags[3:4, :]], axis=1)
    degrees = jnp.broadcast_to(degrees, (16, 2 * E)).astype(BF16)
    degree[...] = dot_nt(degrees, place)[:8, :]
    for v in range(NV):
        sums = placed(got, place, v)
        inner[64 * v : 64 * v + 64, :] = sums[:64] + sign * sums[64:]
        outer[64 * v : 64 * v + 64, :] = sums[:64] - sign * sums[64:]
    up, low = mortar_up[...].astype(F32), mortar_low[...].astype(F32)
    even = is_even()
    for table, face in ((jnp.where(even, up, low), inner), (jnp.where(even, low, up), outer)):
        face[FACE:PAY, :] = jnp.full((PAY - FACE, E), -1.0, F32)
        face[FACE : FACE + 2, :] = table[:, 0:E]
        face[FACE + 2 : FACE + 4, 0:16] = table[:, E : E + 16]


def unpack_rest(got, place, inner, outer, state):
    pick = place[...]
    half_sign = 0.5 * odd_sign()
    for v in range(NV):
        for n in range(3):
            rows = placed(got, pick, NV + 3 * v + n)
            for m in range(16):
                i, j = divmod(16 * n + m, 6)
                start = v * MODES + 64 * i + 8 * j + 16
                state[start : start + 8, :] = rows[8 * m : 8 * m + 8]
        for i in range(N):
            base = v * MODES + 64 * i
            face = slice(64 * v + 8 * i, 64 * v + 8 * i + 8)
            line = [state[base + 8 * j : base + 8 * j + 8, :] for j in range(2, N)]
            near, far = inner[face, :], outer[face, :]
            state[base : base + 8, :] = 0.5 * (near + far) - (line[0] + line[2] + line[4])
            state[base + 8 : base + 16, :] = half_sign * (near - far) - (line[1] + line[3] + line[5])


def couple_one(d, v, first, k):
    half = (0.5 * k) * d[v]
    if v in (0, 4):
        half = half + 0.5 * d[first]
    if v == first:
        half = half + 0.5 * d[4]
    return half


def couple(d, first, k):
    return [couple_one(d, v, first, k) for v in range(NV)]


def halves_of(plus, minus):
    return [p - m for p, m in zip(plus, minus)], [p + m for p, m in zip(plus, minus)]


def degree_masks(degree):
    k_row = iota((8, E), 0)
    return [onehot(jnp.maximum(k_row, n).astype(F32) <= degree[...]) for n in range(N)]


def lift_weights(metric, stage):
    full = jnp.broadcast_to(metric[1:2, :], (8, E))
    return [full * (-0.5 * BETA[stage] * STEP * (2 * a + 1)) for a in range(N)]


def volume_kernel(stage, *refs):
    alpha, beta = ALPHA[stage], BETA[stage]
    if stage:
        first, before, lifts, *refs, state = refs
    else:
        got, place, *refs = refs
        state = refs.pop(8)
    if stage < 2:
        sums_out = refs.pop(7)
    (degree, inner, outer, metric, near, ztab, out, xsum, zsum, xp, xm, zp, zm, xl, zl, cat, live) = refs
    row = iota((E, E), 0)
    masks = degree_masks(degree)
    if stage == 0:
        unpack_rest(got, place, inner, outer, state)
    for n in range(N):
        live[8 * n : 8 * n + 8, :] = masks[n]
    if stage:
        kq = lift_weights(metric, stage - 1)
        for v in range(NV):
            for i in range(N):
                face = 64 * v + 8 * i
                lift = (lifts[face : face + 8, :], lifts[FACE + face : FACE + face + 8, :])
                for j in range(N):
                    start = v * MODES + 64 * i + 8 * j
                    state[start : start + 8, :] = masks[max(i, j)] * (before[start : start + 8, :] + kq[j] * lift[j % 2])
    gather = []
    for d in range(4):
        pick = onehot(row == near[d : d + 1, :]).astype(BF16)
        gather.append(jnp.concatenate([pick, pick], axis=0))
    for v in range(NV):
        for h in range(2):
            base = v * MODES + 256 * h
            high, low = split(state[base : base + 256, :])
            both = jnp.concatenate([high, low], axis=1)
            count = 320 if v >= 3 else 64
            sums = dot(ztab[0:count, :], both)
            sums = sums[:, :E] + sums[:, E:]
            zp[v * 64 + 32 * h : v * 64 + 32 * h + 32, :] = sums[0:32]
            zm[v * 64 + 32 * h : v * 64 + 32 * h + 32, :] = sums[32:64]
            if v >= 3:
                zsum[(v - 3) * MODES + 256 * h : (v - 3) * MODES + 256 * h + 256, :] = sums[64:]
    for v in range(NV):
        for j in range(N):
            line = [state[v * MODES + 64 * i + 8 * j : v * MODES + 64 * i + 8 * j + 8, :] for i in range(N)]
            even = (line[0] + line[2]) + (line[4] + line[6])
            odd = (line[1] + line[3]) + (line[5] + line[7])
            write_traces(even, odd, xp, xm, v, j)

    def across(face, pick):
        for v in range(NV):
            high, low = split(face[64 * v : 64 * v + 64, :])
            cat[64 * v : 64 * v + 64, 0:E] = high
            cat[64 * v : 64 * v + 64, E : 2 * E] = low
        return dot(cat[...], pick)

    def by_variable(x):
        return [x[64 * v : 64 * v + 64] for v in range(NV)]

    for plus, minus, where, first_v, k_minus, scale, result in (
        (xp, xm, (0, 1), 1, 2.0, 1.0, xl),
        (zp, zm, (2, 3), 3, 1.0, 0.5, zl),
    ):
        d_plus = by_variable(across(minus, gather[where[0]]) - plus[...])
        d_minus = by_variable(across(plus, gather[where[1]]) - minus[...])
        even, odd = halves_of(couple(d_plus, first_v, -1.0), couple(d_minus, first_v, k_minus))
        for v in range(NV):
            result[64 * v : 64 * v + 64, :] = scale * even[v] if scale != 1.0 else even[v]
            result[FACE + 64 * v : FACE + 64 * v + 64, :] = scale * odd[v] if scale != 1.0 else odd[v]

    full = [jnp.broadcast_to(metric[d : d + 1, :], (8, E)) for d in range(3)]
    kx = [full[0] * (-0.5 * beta * STEP * (2 * a + 1)) for a in range(N)]
    ky = [full[1] * (-0.05 * beta * STEP * (2 * a + 1)) for a in range(N)]
    kz = full[2] * (-beta * STEP) * (2 * iota((8, E), 0) + 1).astype(F32)
    odd_k = (iota((8, E), 0) & 1) == 1
    even_device = is_even()

    def at(ref, start):
        return ref[pl.ds(pl.multiple_of(start, 8), 8), :]

    def x_pass(j, carry):
        s = [
            [at(xl, 64 * v + 8 * j) for v in range(NV)],
            [at(xl, FACE + 64 * v + 8 * j) for v in range(NV)],
        ]
        for i in range(N - 1, -1, -1):
            rows = [v * MODES + 64 * i + 8 * j for v in range(NV)]
            now = s[i % 2]
            for v in range(NV):
                xsum[pl.ds(pl.multiple_of(rows[v], 8), 8), :] = kx[i] * now[v]
            if i:
                r, u, y, w, p = [at(state, rows[v]) for v in range(NV)]
                twice = u + u
                f = [r + twice, u + (p + p), y, w, p + twice]
                s[(i + 1) % 2] = [a + b for a, b in zip(s[(i + 1) % 2], f)]
        return carry

    lax.fori_loop(0, N, x_pass, 0)

    def y_pass(i, carry):
        near_in = [-at(inner, 64 * v + 8 * i) for v in range(NV)]
        near_out = [-at(outer, 64 * v + 8 * i) for v in range(NV)]
        d_plus = [jnp.where(even_device, a, b) for a, b in zip(near_in, near_out)]
        d_minus = [jnp.where(even_device, b, a) for a, b in zip(near_in, near_out)]
        even, odd = halves_of(couple(d_plus, 2, -1.0), couple(d_minus, 2, 1.1))
        s = [[10.0 * x for x in even], [10.0 * x for x in odd]]
        z_even = [at(zl, 64 * v + 8 * i) for v in range(NV)]
        z_odd = [at(zl, FACE + 64 * v + 8 * i) for v in range(NV)]
        sums = [[None] * NV, [None] * NV]
        for j in range(N - 1, -1, -1):
            offset = 64 * i + 8 * j
            rows = [v * MODES + offset for v in range(NV)]
            c = [at(state, rows[v]) for v in range(NV)]
            sw, sp = at(zsum, offset), at(zsum, MODES + offset)
            zs = (sw, None, None, sp, sw)
            now = s[j % 2]
            mask = at(live, 8 * jnp.maximum(i, j))
            for v in range(NV):
                lift = jnp.where(
                    odd_k,
                    jnp.broadcast_to(z_odd[v][j : j + 1, :], (8, E)),
                    jnp.broadcast_to(z_even[v][j : j + 1, :], (8, E)),
                )
                if zs[v] is not None:
                    lift = lift + zs[v]
                total = at(xsum, rows[v]) + ky[j] * now[v] + kz * lift
                if alpha:
                    total = total + (alpha * at(first, rows[v]) + beta * c[v])
                else:
                    total = total + c[v]
                total = mask * total
                out[pl.ds(pl.multiple_of(rows[v], 8), 8), :] = total
                held = sums[j % 2]
                held[v] = total if held[v] is None else held[v] + total
            if j:
                r, u, y, w, p = c
                y20 = 20.0 * y
                f = [r + y20, u, y + 20.0 * p, w, p + y20]
                s[(j + 1) % 2] = [a + b for a, b in zip(s[(j + 1) % 2], f)]
        for parity in range(2):
            for v in range(NV if stage < 2 else 0):
                start = FACE * parity + 64 * v + 8 * i
                sums_out[pl.ds(pl.multiple_of(start, 8), 8), :] = sums[parity][v]
        return carry

    lax.fori_loop(0, N, y_pass, 0)


def build_routes(pay, table, inside):
    wide = iota((E, 2 * E), 0).astype(F32)
    pad = jnp.full((1, E - 16), -1.0, F32)

    def own(r):
        return jnp.concatenate([table[r : r + 1, 0:E].astype(F32), table[r : r + 1, E : E + 16].astype(F32), pad], axis=1)

    far_elem = jnp.concatenate([pay[0:1, :], pay[2:3, :]], axis=1)
    far_half = jnp.concatenate([pay[1:2, :], pay[3:4, :]], axis=1)
    own_elem, own_half = own(0), own(1)
    far_pick = jnp.where(wide == far_elem, inside, 0.0)
    own_pick = onehot(wide == own_elem).astype(BF16)
    far_whole, own_whole = onehot(far_half == 0.0), onehot(own_half == 0.0)
    far_1, far_2 = onehot(far_half == 1.0), onehot(far_half == 2.0)
    own_1, own_2 = onehot(own_half == 1.0), onehot(own_half == 2.0)
    weights = (
        far_whole * own_whole,
        own_whole * (far_1 + far_2),
        own_whole * (far_1 - far_2),
        far_whole * (own_1 + own_2),
        far_whole * (own_1 - own_2),
    )
    return [dot_nt((far_pick * w).astype(BF16), own_pick).astype(BF16) for w in weights]


def far_side(first, second, cat, routes):
    even = is_even()
    for v in range(NV):
        rows = slice(64 * v, 64 * v + 64)
        high, low = split(jnp.where(even, first[rows, :], second[rows, :]))
        cat[rows, 0:E] = high
        cat[rows, E : 2 * E] = low
    return dot(cat[...], routes)


def mixed(picked, v):
    lines = [[picked[64 * v + 8 * a : 64 * v + 8 * a + 8, E * n : E * n + E] for a in range(N)] for n in range(5)]
    totals = []
    for a in range(N):
        total = lines[0][a]
        for b in range(a, N):
            total = total + RESTRICT[a][b] * lines[1 + (a + b) % 2][b]
        for b in range(a + 1):
            total = total + PROJECT[a][b] * lines[3 + (a + b) % 2][b]
        totals.append(total)
    return totals


def far_lifts(from_in, from_out, cat_up, cat_low, routes):
    picked_up = far_side(from_in, from_out, cat_up, routes[0 : 2 * E, :])
    picked_low = far_side(from_out, from_in, cat_low, routes[2 * E : 4 * E, :])
    up, low = {}, {}
    for v in (1, 3, 2, 4, 0):
        for n in (2, 4) if v == 2 else (v,):
            if n not in up:
                up[n], low[n] = mixed(picked_up, n), mixed(picked_low, n)
        even, odd = [], []
        for i in range(N):
            plus = couple_one({n: x[i] for n, x in up.items()}, v, 2, -1.0)
            minus = couple_one({n: x[i] for n, x in low.items()}, v, 2, 1.1)
            even.append(plus - minus)
            odd.append(plus + minus)
        yield v, even, odd


def trace_kernel(stage, *refs):
    if stage == 0:
        (sums, from_in, from_out, metric, degree, table_up, table_low, inner, outer, lifts, routes, cat_up, cat_low) = refs
        place = lax.axis_index("sub")
        last = lax.axis_size("sub") - 1
        inside = (jnp.where(place < last, 1.0, 0.0), jnp.where(place > 0, 1.0, 0.0))
        tail = slice(FACE, PAY)
        tail_up = jnp.where(is_even(), from_in[tail, :], from_out[tail, :])
        tail_low = jnp.where(is_even(), from_out[tail, :], from_in[tail, :])
        for side, (pay, table) in enumerate(((tail_up, table_up), (tail_low, table_low))):
            for n, route in enumerate(build_routes(pay, table, inside[side])):
                for part in range(2):
                    start = (side * 2 + part) * E
                    routes[start : start + E, E * n : E * n + E] = route
    else:
        (sums, from_in, from_out, metric, degree, routes, inner, outer, lifts, cat_up, cat_low) = refs
    sign = odd_sign()
    masks = degree_masks(degree)
    kq = lift_weights(metric, stage)
    weights = [[sum(masks[max(i, j)] * kq[j] for j in range(p, N, 2)) for p in range(2)] for i in range(N)]
    for v, lift_even, lift_odd in far_lifts(from_in, from_out, cat_up, cat_low, routes):
        for i in range(N):
            rows = slice(64 * v + 8 * i, 64 * v + 8 * i + 8)
            odd_rows = slice(FACE + 64 * v + 8 * i, FACE + 64 * v + 8 * i + 8)
            lifts[rows, :] = lift_even[i]
            lifts[odd_rows, :] = lift_odd[i]
            even = sums[rows, :] + weights[i][0] * lift_even[i]
            odd = sums[odd_rows, :] + weights[i][1] * lift_odd[i]
            write_traces(even, sign * odd, inner, outer, v, i)


def final_kernel(partial, from_in, from_out, metric, degree, routes, final, cat_up, cat_low, out, sems):
    back = 1.0 / jnp.sqrt((2 * iota((8, E), 0) + 1).astype(F32))
    masks = [m * back for m in degree_masks(degree)]
    kq = lift_weights(metric, 2)
    sent = []
    for v, lift_even, lift_odd in far_lifts(from_in, from_out, cat_up, cat_low, routes):
        for i in range(N):
            for j in range(N):
                start = 64 * i + 8 * j
                lift = (lift_even, lift_odd)[j % 2][i]
                value = partial[v * MODES + start : v * MODES + start + 8, :] + kq[j] * lift
                value = (masks[max(i, j)] * (1.0 / math.sqrt((2 * i + 1) * (2 * j + 1)))) * value
                out[v, start : start + 8, :] = value
            part = pl.ds(64 * i, 64)
            copy = pltpu.make_async_copy(out.at[v, part, :], final.at[v, part, :], sems.at[v * N + i])
            copy.start()
            sent.append(copy)
    for copy in sent:
        copy.wait()


def call(kernel, outs, scratch, args, result=VMEM, cost=None):
    return pl.pallas_call(
        kernel,
        out_shape=outs,
        in_specs=[VMEM] * len(args),
        out_specs=jax.tree.map(lambda _: result, outs),
        scratch_shapes=scratch,
        compiler_params=PARAMS,
        cost_estimate=cost,
    )(*args)


def f32(*shape):
    return jax.ShapeDtypeStruct(shape, F32)


def swap(inner, outer):
    count = lax.axis_size("sub")

    def partner(c, s):
        if s in (0, count - 1):
            return (c ^ 4) * count + s
        return c * count + (s + 1 if s % 2 else s - 1)

    pairs = [(c * count + s, partner(c, s)) for c in range(lax.axis_size("curve")) for s in range(count)]
    far = lax.ppermute(outer, ("curve", "sub"), pairs)
    near = lax.ppermute(inner, "sub", [(s, s ^ 1) for s in range(count)])
    return near, far


def shards(coefficients, old_degree, new_degree, destination, metric, near, mortar_up, mortar_low):
    ztab = jnp.asarray(z_table(), BF16)
    chosen = call(
        setup_kernel,
        (jax.ShapeDtypeStruct((2 * E, 2 * E), BF16), f32(MODES, E), f32(E, E)),
        [],
        (jnp.stack([old_degree, new_degree, destination]),),
        cost=pl.CostEstimate(flops=400_000_000, bytes_accessed=1_000_000, transcendentals=0),
    )
    packed = call(pack_kernel, f32(E * BLOCK, E), [], (coefficients, *chosen))
    packed = packed.reshape(E, 1, BLOCK * E)
    got = lax.all_to_all(packed, ("curve", "sub"), split_axis=0, concat_axis=0, tiled=True)
    got = got.reshape(E * BLOCK, E)
    place, degree, inner, outer = call(
        unpack_kernel,
        (jax.ShapeDtypeStruct((E, 2 * E), BF16), f32(8, E), f32(PAY, E), f32(PAY, E)),
        [],
        (got, mortar_up, mortar_low),
    )
    faces = (f32(FACE, E), f32(FACE, E))
    cats = [pltpu.VMEM((FACE, 2 * E), BF16)] * 2
    for stage in range(3):
        from_in, from_out = swap(inner, outer)
        given = (got, place) if stage == 0 else (first, partial, lifts)
        partial, *sums = call(
            functools.partial(volume_kernel, stage),
            (f32(ROWS, E), f32(2 * FACE, E), f32(ROWS, E))[: 3 - stage],
            [pltpu.VMEM((ROWS, E), F32), pltpu.VMEM((2 * MODES, E), F32)]
            + [pltpu.VMEM((FACE, E), F32)] * 4
            + [pltpu.VMEM((2 * FACE, E), F32)] * 2
            + [pltpu.VMEM((FACE, 2 * E), BF16), pltpu.VMEM((8 * N, E), F32)]
            + ([pltpu.VMEM((ROWS, E), F32)] if stage else []),
            given + (degree, inner, outer, metric, near, ztab),
        )
        if stage == 0:
            first = sums.pop()
        body = functools.partial(trace_kernel, stage)
        outs = faces + (f32(2 * FACE, E),)
        if stage == 0:
            inner, outer, lifts, routes = call(
                body,
                outs + (jax.ShapeDtypeStruct((4 * E, 5 * E), BF16),),
                cats,
                (*sums, from_in, from_out, metric, degree, mortar_up, mortar_low),
            )
        elif stage == 1:
            inner, outer, lifts = call(body, outs, cats, (*sums, from_in, from_out, metric, degree, routes))
        else:
            scratch = cats + [pltpu.VMEM((NV, MODES, E), F32), pltpu.SemaphoreType.DMA((NV * N,))]
            args = (partial, from_in, from_out, metric, degree, routes)
            return call(final_kernel, f32(NV, MODES, E), scratch, args, result=HBM)


def solution(mesh):
    lanes = P(None, ("curve", "sub"))
    rank = P(("curve", "sub"))
    cube = P(None, None, ("curve", "sub"))
    return jax.shard_map(
        shards,
        mesh=mesh,
        in_specs=(cube, rank, rank, rank, lanes, lanes, lanes, lanes),
        out_specs=cube,
        check_vma=False,
    )
```
